32 devices in a mesh: dp: 4 (over z), expert: 8 (over y, x, core).
Axes of the slice: x: 2, y: 2, z: 4, core: 2. Of those that a mesh axis runs over, the one named last changes fastest.
Arguments:
- tokens: bfloat16 [6144, 2048], P(('dp', 'expert')), may hold values from -6 to 6
- cotangent: bfloat16 [6144, 2048], P(('dp', 'expert')), may hold values from -6 to 6
- lengths: int32 [32, 4], P(('dp', 'expert')), may hold values from 1 to 144, 192 in all within a row
- routes: int32 [6144, 8], P(('dp', 'expert')), may hold values from 0 to 15, all different within a row; in each aligned block of 192 rows (0 to 191, 192 to 383, ...) at most 120 rows name the same one
- w_query: bfloat16 [2048, 2048], P(('dp', 'expert')), may hold values from -0.125 to 0.125
- w_key: bfloat16 [2048, 2048], P(('dp', 'expert')), may hold values from -0.125 to 0.125
- w_value: bfloat16 [2048, 2048], P(('dp', 'expert')), may hold values from -0.125 to 0.125
- w_out: bfloat16 [2048, 2048], P(('dp', 'expert')), may hold values from -0.75 to 0.75
- w_router: bfloat16 [2048, 16], P(('dp', 'expert')), may hold values from -0.06591797 to 0.06591797
- w_gate: bfloat16 [16, 2048, 1024], P('expert', 'dp'), may hold values from -0.125 to 0.125
- w_up: bfloat16 [16, 2048, 1024], P('expert', 'dp'), may hold values from -0.125 to 0.125
- w_down: bfloat16 [16, 1024, 2048], P('expert', 'dp'), may hold values from -0.75 to 0.75
- g_attn: bfloat16 [2048], P(('dp', 'expert')), may hold values from 0.099609375 to 1.8984375
- g_query: bfloat16 [2048], P(('dp', 'expert')), may hold values from 0.099609375 to 1.8984375
- g_key: bfloat16 [2048], P(('dp', 'expert')), may hold values from 0.099609375 to 1.8984375
- g_ffn: bfloat16 [2048], P(('dp', 'expert')), may hold values from 0.099609375 to 1.8984375
Outputs:
- block_out: bfloat16 [6144, 2048], P(('dp', 'expert'))
- grad_tokens: bfloat16 [6144, 2048], P(('dp', 'expert'))
- grad_query: float32 [2048, 2048], P(('dp', 'expert'))
- grad_key: float32 [2048, 2048], P(('dp', 'expert'))
- grad_value: float32 [2048, 2048], P(('dp', 'expert'))
- grad_outproj: float32 [2048, 2048], P(('dp', 'expert'))
- grad_router: float32 [2048, 16], P(('dp', 'expert'))
- grad_gate: float32 [16, 2048, 1024], P('expert', 'dp')
- grad_up: float32 [16, 2048, 1024], P('expert', 'dp')
- grad_down: float32 [16, 1024, 2048], P('expert', 'dp')
- grad_gattn: float32 [2048], P(('dp', 'expert'))
- grad_gquery: float32 [2048], P(('dp', 'expert'))
- grad_gkey: float32 [2048], P(('dp', 'expert'))
- grad_gffn: float32 [2048], P(('dp', 'expert'))
The draws below stay inside these ranges and needn't reach their ends.
Inputs may be any that keep to these rules, and one draw needn't show every extreme that they name: Each device's row of lengths sums to 192, and its largest entry is 144. `routes`: A token's 8 experts differ. Among the rows of one device, no expert is named more than 120 times, a bound that some block reaches.
All inputs are finite; a program needn't handle non-finite values.
Results may differ from the reference program's by a relative error of at most 0.018.
Values may be sent and summed in bfloat16 or wider, within the bound.
No kernel may reach another device: no remote copies, remote signals or barrier semaphores. Data moves between devices by JAX's collectives and lax.ppermute only.
A program may use at most 448 MiB of HBM per device.

```python
import math
import jax
import jax.numpy as jnp
import numpy as np
from jax import lax

D = 2048
HEADS = 16
HD = 128
FF = 1024
TOP = 8
SEGS = 4
TOK_DEV = 192
LONGEST = 144
TOKENS = 6144
EXPERTS = 16
CAP = 120
N_DP = 4
N_EXPERT = 8


def strengthened(values, key, source, target, blocks, factor):
    def block_of(axis_at):
        return (jnp.arange(values.shape[axis_at]) // (values.shape[axis_at] // blocks)).reshape((-1,) + (1,) * (values.ndim - 1 - axis_at))

    near = jax.random.permutation(key, blocks)[block_of(target)]
    far = (block_of(target) + blocks // 2) % blocks
    return jnp.where((block_of(source) == near) | (block_of(source) == far), factor * values, values)


def levels(rng, extent, split, smallest, largest):
    factor_of = 1.0
    for dim, parts in split:
        draws = jax.random.uniform(jax.random.fold_in(jax.random.fold_in(rng, 6), dim), (parts,), jnp.float32, smallest / len(split), largest / len(split))
        factor_of = factor_of * jnp.repeat(jnp.exp(draws), extent[dim] // parts).reshape((-1,) + (1,) * (len(extent) - 1 - dim))
    return factor_of


def profile(count, total, reach, skew):
    loads = [(1 << 20) // math.isqrt(grade ** skew) + 1 for grade in range(2, count + 1)]
    surplus, counts = total - reach - (count - 1), [1] * (count - 1)
    while surplus > 0:
        candidates = [i for i in range(count - 1) if counts[i] < reach]
        pool, remaining = sum([loads[i] for i in candidates]), surplus
        for i in candidates:
            addition = min(reach - counts[i], max(1, remaining * loads[i] // pool), surplus)
            counts[i] = counts[i] + addition
            surplus = surplus - addition
    return np.array([reach] + counts)


def uneven(key, amount, total, bound, skew):
    if amount == 2:
        one = jax.random.randint(key, (), max(1, total - bound), min(bound, total - 1) + 1)
        return jnp.stack([one, total - one])
    sizes = jnp.asarray(profile(amount, total, bound, skew), jnp.int32)
    pairs = (amount - 1) // 2
    giver, taker = sizes[1:1 + 2 * pairs:2], sizes[2:2 + 2 * pairs:2]
    slack = jnp.minimum(giver - 1, bound - taker)
    moved = jax.random.randint(jax.random.fold_in(key, 1), (pairs,), 0, 1 << 20) % (slack + 1)
    sizes = sizes.at[1:1 + 2 * pairs:2].set(giver - moved).at[2:2 + 2 * pairs:2].set(taker + moved)
    return sizes[jax.random.permutation(jax.random.fold_in(key, 2), amount)]


def deal_out(key, own, number, rows, number_of, top, bound, skew):
    ranking = jax.random.permutation(key, number_of)
    crowded, ordinary = load_shares(number_of, rows * top, bound, skew, True), load_shares(number_of, rows * top, bound, skew, False)
    places = jnp.arange(number_of)

    def named(sizes, offset_by):
        used = int((sizes > 0).sum())
        fixed = max(1, used // 4)
        moved = fixed + (places - fixed + offset_by * (used - fixed)) % max(1, number_of - fixed)
        return jnp.zeros((number_of,), jnp.int32).at[ranking[jnp.where(places < fixed, places, moved)]].set(jnp.asarray(sizes, jnp.int32))

    sizes = jnp.where(number % 4 == 0, named(crowded, number // 4), named(ordinary, number - number // 4 - 1))
    mixed = jax.random.permutation(jax.random.fold_in(own, 3), number_of)
    giver, receiver = mixed[0:number_of // 2 * 2:2], mixed[1:number_of // 2 * 2:2]
    margin = jnp.minimum(sizes[giver] - 1, bound - sizes[receiver]) // 2
    margin = jnp.where((giver == ranking[0]) | (receiver == ranking[0]) | (sizes[receiver] == 0), 0, jnp.maximum(margin, 0))
    moved = jax.random.randint(jax.random.fold_in(own, 4), (number_of // 2,), 0, 1 << 20) % (margin + 1)
    sizes = sizes.at[giver].add(-moved).at[receiver].add(moved)
    items = jnp.searchsorted(jnp.cumsum(sizes), jnp.arange(rows * top), side="right").astype(jnp.int32)
    listing = items.reshape(top, rows).T
    listing = listing[jax.random.permutation(jax.random.fold_in(own, 1), rows)]
    offset_by = jax.random.randint(jax.random.fold_in(own, 2), (rows, 1), 0, top)
    return jnp.take_along_axis(listing, (jnp.arange(top)[None, :] + offset_by) % top, axis=1)


def load_shares(count, total, limit, slope, full):
    portions = [(1 << 20) // math.isqrt(standing ** slope) + 1 for standing in range(1, count + 1)]
    largest = limit if full else min(limit, max(-(-total // count), total * portions[0] // sum(portions)))
    least = 1 if total - largest >= count - 1 else 0
    counts, rest = [largest] + [least] * (count - 1), total - largest - least * (count - 1)
    while rest > 0:
        candidates = [i for i in range(1, count) if counts[i] < largest] or [i for i in range(1, count) if counts[i] < limit]
        whole, left = sum([portions[i] for i in candidates]), rest
        for i in candidates:
            more = min(limit - counts[i], max(1, left * portions[i] // whole), rest)
            counts[i] = counts[i] + more
            rest = rest - more
    return np.array(counts)


def bell_draw(key, extent, deviation, limit, cuts=(), held_as=jnp.bfloat16):
    values = deviation * jax.random.normal(key, extent, jnp.float32)
    if cuts:
        values = values * levels(key, extent, cuts, -0.22, 0.18)
    return jnp.clip(values, -limit, limit).astype(held_as)


def bell_draw_with(stream_key, dims, width, most, shards, heavy, held_as=jnp.bfloat16):
    values = width * jax.random.normal(stream_key, dims, jnp.float32)
    if shards:
        values = values * levels(stream_key, dims, shards, -0.22, 0.18)
    return jnp.clip(strengthened(values, jax.random.fold_in(stream_key, 3), *heavy), -most, most).astype(held_as)


def setup_inputs(seed: int = 0) -> dict:
    arg_keys = jax.random.split(jax.random.key(seed), 17)
    tokens = bell_draw(arg_keys[0], (TOKENS, D), 1.0, 6.0, ((0, 32),))
    cotangent = bell_draw_with(arg_keys[1], (TOKENS, D), 1.0, 6.0, ((0, 32),), (0, 1, 32, 2.75))
    lengths = jax.vmap(lambda own: uneven(own, SEGS, TOK_DEV, LONGEST, 2))(jax.random.split(arg_keys[2], (N_DP * N_EXPERT))).reshape((N_DP * N_EXPERT, SEGS)).astype(jnp.int32)
    routes_keys = jax.random.split(jax.random.fold_in(arg_keys[3], 1), TOKENS // TOK_DEV)
    routes_turns = jax.random.permutation(jax.random.fold_in(arg_keys[3], 3), TOKENS // TOK_DEV)
    routes = jax.vmap(lambda own, number: deal_out(jax.random.fold_in(arg_keys[3], 2), own, number, TOK_DEV, EXPERTS, TOP, CAP, 1))(routes_keys, routes_turns).reshape((TOKENS, TOP))
    w_query = bell_draw(arg_keys[4], (D, D), D ** -0.5, 0.125, ((0, 32),))
    w_key = bell_draw(arg_keys[5], (D, D), D ** -0.5, 0.125, ((0, 32),))
    w_value = bell_draw(arg_keys[6], (D, D), D ** -0.5, 0.125, ((0, 32),))
    w_out = bell_draw(arg_keys[7], (D, D), (D // 32) ** -0.5, 0.75, ((0, 32),))
    w_router = bell_draw(arg_keys[8], (D, EXPERTS), (0.5 * D ** -0.5), 0.06591797, ((0, 32),))
    w_gate = bell_draw(arg_keys[9], (EXPERTS, D, FF), D ** -0.5, 0.125, ((0, 8), (1, 4)))
    w_up = bell_draw(arg_keys[10], (EXPERTS, D, FF), D ** -0.5, 0.125, ((0, 8), (1, 4)))
    w_down = bell_draw(arg_keys[11], (EXPERTS, FF, D), (FF // 16) ** -0.5, 0.75, ((0, 8), (1, 4)))
    g_attn = jnp.clip(1.0 + 0.18 * jax.random.normal(arg_keys[12], (D,), jnp.float32), 0.099609375, 1.8984375).astype(jnp.bfloat16)
    g_query = jnp.clip(1.0 + 0.18 * jax.random.normal(arg_keys[13], (D,), jnp.float32), 0.099609375, 1.8984375).astype(jnp.bfloat16)
    g_key = jnp.clip(1.0 + 0.18 * jax.random.normal(arg_keys[14], (D,), jnp.float32), 0.099609375, 1.8984375).astype(jnp.bfloat16)
    g_ffn = jnp.clip(1.0 + 0.18 * jax.random.normal(arg_keys[15], (D,), jnp.float32), 0.099609375, 1.8984375).astype(jnp.bfloat16)
    return {"tokens": tokens, "cotangent": cotangent, "lengths": lengths, "routes": routes, "w_query": w_query, "w_key": w_key, "w_value": w_value, "w_out": w_out, "w_router": w_router, "w_gate": w_gate, "w_up": w_up, "w_down": w_down, "g_attn": g_attn, "g_query": g_query, "g_key": g_key, "g_ffn": g_ffn}


EPS = 1e-05
THETA = 50000.0
HIGHEST_PRECISION = lax.Precision.HIGHEST

@jax.custom_vjp
def low(v):
    return lax.optimization_barrier(v.astype(jnp.bfloat16)).astype(jnp.float32)

@jax.custom_vjp
def low_back(v):
    return v

def low_keep(v):
    return (low(v), None)

def low_pass(kept, grad):
    return (grad,)

def back_keep(v):
    return (v, None)

def back_low(kept, grad):
    return (low(grad),)
low.defvjp(low_keep, low_pass)
low_back.defvjp(back_keep, back_low)

def matmul(left, right):
    return jnp.dot(left, right, precision=HIGHEST_PRECISION, preferred_element_type=jnp.float32)

def normalize(v, gain):
    return v * lax.rsqrt(lax.optimization_barrier(jnp.mean(v * v, axis=-1, keepdims=True)) + EPS) * gain

def layout(lengths_row, row_count):
    seq_ends = jnp.cumsum(lengths_row).astype(jnp.int32)
    position = jnp.arange(row_count, dtype=jnp.int32)
    segment = lax.optimization_barrier(jnp.sum((position[:, None] >= seq_ends[None, :]).astype(jnp.int32), axis=1))
    seq_starts = seq_ends - lengths_row
    labels = jnp.arange(lengths_row.shape[0], dtype=jnp.int32)
    seq_start = lax.optimization_barrier(jnp.sum(jnp.where(segment[:, None] == labels[None, :], seq_starts[None, :], 0), axis=1))
    return (segment, position - seq_start)

def rotate(v, offset):
    half_dim = v.shape[-1] // 2
    frequency = THETA ** (-jnp.arange(half_dim).astype(v.dtype) / half_dim)
    angles = offset.astype(v.dtype)[:, None] * frequency[None, :]
    cosine = jnp.cos(angles)[:, None, :]
    sine_part = jnp.sin(angles)[:, None, :]
    first_half = v[..., :half_dim]
    second_half = v[..., half_dim:]
    return jnp.concatenate([first_half * cosine - second_half * sine_part, second_half * cosine + first_half * sine_part], axis=-1)

def head_prep(raw_q, raw_k, gain_q, gain_k, offset):
    row_count = raw_q.shape[0]
    queries = rotate(normalize(raw_q.reshape(row_count, HEADS, HD), gain_q.reshape(HEADS, HD)), offset)
    keys_rot = rotate(normalize(raw_k.reshape(row_count, HEADS, HD), gain_k.reshape(HEADS, HD)), offset)
    return (queries, keys_rot)

def route_softmax(chosen):
    peak = lax.optimization_barrier(jnp.max(chosen, axis=-1, keepdims=True))
    exp_scores = jnp.exp(chosen - peak)
    return exp_scores / lax.optimization_barrier(jnp.sum(exp_scores, axis=-1, keepdims=True))

def swiglu(gate_act, up_act):
    return jax.nn.silu(gate_act) * up_act

def slots(flat_routes, expert_count, capacity):
    one_hot = (flat_routes[:, None] == jnp.arange(expert_count, dtype=jnp.int32)[None, :]).astype(jnp.int32)
    slot_rank = lax.optimization_barrier(jnp.sum((jnp.cumsum(one_hot, axis=0) - one_hot) * one_hot, axis=1))
    return (flat_routes * capacity + slot_rank).astype(jnp.int32)

def layer_block(params, inputs, lengths_row, routes_block):
    query_w, key_w, value_w, out_w, router_w, gate_w, up_w, down_w, attn_gain, query_gain, key_gain, ffn_gain = params
    row_count = inputs.shape[0]
    segment, offset = layout(lengths_row, row_count)
    normed_attn = low(normalize(inputs, attn_gain))
    raw_q = low_back(matmul(normed_attn, query_w))
    raw_k = low_back(matmul(normed_attn, key_w))
    values = low(low_back(matmul(normed_attn, value_w))).reshape(row_count, HEADS, HD)
    queries, keys_rot = head_prep(raw_q, raw_k, query_gain, key_gain, offset)
    queries = low(queries)
    keys_rot = low(keys_rot)
    scores = low_back(jnp.einsum('qhd,khd->hqk', queries, keys_rot, precision=HIGHEST_PRECISION) * HD ** (-0.5))
    seq_mask = (segment[:, None] == segment[None, :])[None]
    scores = jnp.where(seq_mask, scores, -1e+30)
    peak = lax.optimization_barrier(jnp.max(scores, axis=-1, keepdims=True))
    exp_scores = jnp.exp(scores - peak)
    probs = low(exp_scores / lax.optimization_barrier(jnp.sum(exp_scores, axis=-1, keepdims=True)))
    context = low(low_back(jnp.einsum('hqk,khd->qhd', probs, values, precision=HIGHEST_PRECISION))).reshape(row_count, D)
    midway = inputs + low_back(matmul(context, out_w))
    normed_ffn = low(normalize(midway, ffn_gain))
    logits = low_back(matmul(normed_ffn, router_w))
    chosen = jnp.take_along_axis(logits, routes_block, axis=1)
    gates = route_softmax(chosen)
    slot_index = slots(routes_block.reshape(-1), EXPERTS, CAP)
    sent_rows = low_back(jnp.repeat(normed_ffn, TOP, axis=0))
    buffer_in = jnp.zeros((EXPERTS * CAP, D), inputs.dtype).at[slot_index].add(sent_rows).reshape(EXPERTS, CAP, D)
    gate_act = low_back(jnp.einsum('erd,edf->erf', buffer_in, gate_w, precision=HIGHEST_PRECISION))
    up_act = low_back(jnp.einsum('erd,edf->erf', buffer_in, up_w, precision=HIGHEST_PRECISION))
    hidden = low(swiglu(gate_act, up_act))
    expert_out = low(low_back(jnp.einsum('erf,efd->erd', hidden, down_w, precision=HIGHEST_PRECISION))).reshape(EXPERTS * CAP, D)
    picked = expert_out[slot_index].reshape(row_count, TOP, D)
    return midway + lax.optimization_barrier(jnp.sum(gates[:, :, None] * picked, axis=1))

def forward(params, inputs, lengths, routes):
    blocks = inputs.reshape(-1, TOK_DEV, D)
    route_blocks = routes.reshape(-1, TOK_DEV, TOP)
    checked = jax.checkpoint(layer_block)

    def scan_step(scan_carry, pieces):
        return (scan_carry, checked(params, pieces[0], pieces[1], pieces[2]))
    start_carry = jnp.zeros((), jnp.float32)
    finish, results = lax.scan(scan_step, start_carry, (blocks, lengths, route_blocks))
    return results.reshape(-1, D)

def reference(tokens, cotangent, lengths, routes, w_query, w_key, w_value, w_out, w_router, w_gate, w_up, w_down, g_attn, g_query, g_key, g_ffn):
    params = tuple((weight.astype(jnp.float32) for weight in (w_query, w_key, w_value, w_out, w_router, w_gate, w_up, w_down, g_attn, g_query, g_key, g_ffn)))
    inputs_f = tokens.astype(jnp.float32)

    def whole(weights, inputs):
        return forward(weights, inputs, lengths, routes)
    result, pullback = jax.vjp(whole, params, inputs_f)
    gradients, grad_inputs = pullback(cotangent.astype(jnp.float32))
    return (result.astype(jnp.bfloat16), grad_inputs.astype(jnp.bfloat16), gradients[0], gradients[1], gradients[2], gradients[3], gradients[4], gradients[5], gradients[6], gradients[7], gradients[8], gradients[9], gradients[10], gradients[11])
```

```python
import functools

import jax
import jax.numpy as jnp
from jax import lax
from jax.experimental import pallas as pl
from jax.experimental.pallas import tpu as pltpu
from jax.sharding import PartitionSpec as P

D = 2048
HEADS = 16
HD = 128


EPS = 1e-05
THETA = 50000.0


def normalize(v, gain):
    return v * lax.rsqrt(jnp.mean(v * v, axis=-1, keepdims=True) + EPS) * gain


def layout(lengths_row, row_count):
    seq_ends = jnp.cumsum(lengths_row)
    position = jnp.arange(row_count, dtype=jnp.int32)
    segment = jnp.sum((position[:, None] >= seq_ends[None, :]).astype(jnp.int32), axis=1)
    seq_starts = seq_ends - lengths_row
    labels = jnp.arange(lengths_row.shape[0], dtype=jnp.int32)
    seq_start = jnp.sum(
        jnp.where(segment[:, None] == labels[None, :], seq_starts[None, :], 0), axis=1
    )
    return (segment, position - seq_start)


def rotate(v, offset):
    half_dim = v.shape[-1] // 2
    frequency = THETA ** (-jnp.arange(half_dim).astype(v.dtype) / half_dim)
    angles = offset.astype(v.dtype)[:, None] * frequency[None, :]
    cosine = jnp.cos(angles)[:, None, :]
    sine_part = jnp.sin(angles)[:, None, :]
    first_half = v[..., :half_dim]
    second_half = v[..., half_dim:]
    return jnp.concatenate(
        [
            first_half * cosine - second_half * sine_part,
            second_half * cosine + first_half * sine_part,
        ],
        axis=-1,
    )


def head_prep(raw_q, raw_k, gain_q, gain_k, offset):
    row_count = raw_q.shape[0]
    queries = rotate(
        normalize(raw_q.reshape(row_count, HEADS, HD), gain_q.reshape(HEADS, HD)), offset
    )
    keys_rot = rotate(
        normalize(raw_k.reshape(row_count, HEADS, HD), gain_k.reshape(HEADS, HD)), offset
    )
    return (queries, keys_rot)


def route_softmax(chosen):
    peak = jnp.max(chosen, axis=-1, keepdims=True)
    exp_scores = jnp.exp(chosen - peak)
    return exp_scores / jnp.sum(exp_scores, axis=-1, keepdims=True)


def swiglu(gate_act, up_act):
    return jax.nn.silu(gate_act) * up_act


def slots(flat_routes, expert_count, capacity):
    one_hot = (flat_routes[:, None] == jnp.arange(expert_count, dtype=jnp.int32)[None, :]).astype(
        jnp.int32
    )
    slot_rank = jnp.sum((jnp.cumsum(one_hot, axis=0) - one_hot) * one_hot, axis=1)
    return flat_routes * capacity + slot_rank


def contract_rows(left, right):
    return lax.dot_general(
        left, right, (((0,), (0,)), ((), ())), preferred_element_type=jnp.float32
    )


def times_transposed(left, right):
    return lax.dot_general(
        left, right, (((1,), (1,)), ((), ())), preferred_element_type=jnp.float32
    )


def by_axes(
    tokens,
    cotangent,
    lengths,
    routes,
    w_query,
    w_key,
    w_value,
    w_out,
    w_router,
    w_gate,
    w_up,
    w_down,
    g_attn,
    g_query,
    g_key,
    g_ffn,
):
    row_count = tokens.shape[0]
    top_count = routes.shape[1]
    local_experts = w_gate.shape[0]
    owners = lax.axis_size("expert")
    experts = local_experts * owners
    capacity = row_count * top_count * 5 // (4 * experts)
    score_scale = HD ** (-0.5)
    segment, offset = layout(lengths[0], row_count)
    seq_mask = (segment[:, None] == segment[None, :])[None]
    dense = (
        lax.all_gather(w_query, ("dp", "expert"), axis=0, tiled=True),
        lax.all_gather(w_key, ("dp", "expert"), axis=0, tiled=True),
        lax.all_gather(w_value, ("dp", "expert"), axis=0, tiled=True),
        lax.all_gather(w_out, ("dp", "expert"), axis=0, tiled=True),
        lax.all_gather(w_router, ("dp", "expert"), axis=0, tiled=True),
        lax.all_gather(g_attn, ("dp", "expert"), axis=0, tiled=True),
        lax.all_gather(g_query, ("dp", "expert"), axis=0, tiled=True),
        lax.all_gather(g_key, ("dp", "expert"), axis=0, tiled=True),
        lax.all_gather(g_ffn, ("dp", "expert"), axis=0, tiled=True),
    )
    query_w, key_w, value_w, out_w, router_w, attn_gain, query_gain, key_gain, ffn_gain = dense
    expert_full = (
        lax.all_gather(w_gate, "dp", axis=1, tiled=True),
        lax.all_gather(w_up, "dp", axis=1, tiled=True),
        lax.all_gather(w_down, "dp", axis=1, tiled=True),
    )
    gate_full, up_full, down_full = expert_full
    inputs = tokens.astype(jnp.float32)
    normed_f, norm_attn_pull = jax.vjp(normalize, inputs, attn_gain.astype(jnp.float32))
    normed_attn = normed_f.astype(jnp.bfloat16)
    raw_q = jnp.dot(normed_attn, query_w, preferred_element_type=jnp.float32)
    raw_k = jnp.dot(normed_attn, key_w, preferred_element_type=jnp.float32)
    values = jnp.dot(normed_attn, value_w, preferred_element_type=jnp.float32).astype(jnp.bfloat16)
    value_heads = values.reshape(row_count, HEADS, HD)

    def prep_local(first, second, first_gain, second_gain):
        return head_prep(first, second, first_gain, second_gain, offset)

    rotated, heads_pull = jax.vjp(
        prep_local, raw_q, raw_k, query_gain.astype(jnp.float32), key_gain.astype(jnp.float32)
    )
    queries = rotated[0].astype(jnp.bfloat16)
    keys_rot = rotated[1].astype(jnp.bfloat16)
    scores = (
        jnp.einsum("qhd,khd->hqk", queries, keys_rot, preferred_element_type=jnp.float32)
        * score_scale
    )
    scores = jnp.where(seq_mask, scores, -1e30)
    peak = jnp.max(scores, axis=-1, keepdims=True)
    exp_scores = jnp.exp(scores - peak)
    exp_total = jnp.sum(exp_scores, axis=-1, keepdims=True)
    log_total = peak + jnp.log(exp_total)
    probs_low = (exp_scores / exp_total).astype(jnp.bfloat16)
    context = (
        jnp.einsum("hqk,khd->qhd", probs_low, value_heads, preferred_element_type=jnp.float32)
        .astype(jnp.bfloat16)
        .reshape(row_count, D)
    )
    midway = inputs + jnp.dot(context, out_w, preferred_element_type=jnp.float32)
    normed2_f, norm_ffn_pull = jax.vjp(normalize, midway, ffn_gain.astype(jnp.float32))
    normed_ffn = normed2_f.astype(jnp.bfloat16)
    logits = jnp.dot(normed_ffn, router_w, preferred_element_type=jnp.float32)
    chosen = jnp.take_along_axis(logits, routes, axis=1)
    gates, gates_pull = jax.vjp(route_softmax, chosen)
    slot_index = slots(routes.reshape(-1), experts, capacity)
    sent_rows = (
        jnp.zeros((experts * capacity, D), jnp.bfloat16)
        .at[slot_index]
        .set(jnp.repeat(normed_ffn, top_count, axis=0))
    )
    sent_rows = sent_rows.reshape(owners, local_experts, capacity, D)
    arrived = lax.all_to_all(sent_rows, "expert", split_axis=0, concat_axis=2, tiled=True).reshape(
        local_experts, owners * capacity, D
    )
    gate_act = jnp.einsum("erd,edf->erf", arrived, gate_full, preferred_element_type=jnp.float32)
    up_act = jnp.einsum("erd,edf->erf", arrived, up_full, preferred_element_type=jnp.float32)
    hidden = swiglu(gate_act, up_act).astype(jnp.bfloat16)
    produced = jnp.einsum(
        "erf,efd->erd", hidden, down_full, preferred_element_type=jnp.float32
    ).astype(jnp.bfloat16)
    returned = lax.all_to_all(
        produced.reshape(1, local_experts, owners * capacity, D),
        "expert",
        split_axis=2,
        concat_axis=0,
        tiled=True,
    ).reshape(experts * capacity, D)
    picked = returned[slot_index].reshape(row_count, top_count, D).astype(jnp.float32)
    block_out = (midway + jnp.sum(gates[:, :, None] * picked, axis=1)).astype(jnp.bfloat16)
    grad_out = cotangent.astype(jnp.float32)
    grad_gates = jnp.sum(grad_out[:, None, :] * picked, axis=2)
    grad_picked = (
        (gates[:, :, None] * grad_out[:, None, :])
        .astype(jnp.bfloat16)
        .reshape(row_count * top_count, D)
    )
    grad_sent = jnp.zeros((experts * capacity, D), jnp.bfloat16).at[slot_index].set(grad_picked)
    grad_sent = grad_sent.reshape(owners, local_experts, capacity, D)
    grad_arrived = lax.all_to_all(
        grad_sent, "expert", split_axis=0, concat_axis=2, tiled=True
    ).reshape(local_experts, owners * capacity, D)
    gate_back, up_back, down_back = (
        lax.all_gather(w_gate, "dp", axis=1, tiled=True),
        lax.all_gather(w_up, "dp", axis=1, tiled=True),
        lax.all_gather(w_down, "dp", axis=1, tiled=True),
    )
    grad_hidden = jnp.einsum(
        "erd,efd->erf", grad_arrived, down_back, preferred_element_type=jnp.float32
    )
    grad_down_local = jnp.einsum(
        "erf,erd->efd", hidden, grad_arrived, preferred_element_type=jnp.float32
    )
    act_unused, act_pull = jax.vjp(swiglu, gate_act, up_act)
    grad_gate_act, grad_up_act = act_pull(grad_hidden)
    grad_gate_low = grad_gate_act.astype(jnp.bfloat16)
    grad_up_low = grad_up_act.astype(jnp.bfloat16)
    grad_gate_local = jnp.einsum(
        "erd,erf->edf", arrived, grad_gate_low, preferred_element_type=jnp.float32
    )
    grad_up_local = jnp.einsum(
        "erd,erf->edf", arrived, grad_up_low, preferred_element_type=jnp.float32
    )
    grad_arrival = jnp.einsum(
        "erf,edf->erd", grad_gate_low, gate_back, preferred_element_type=jnp.float32
    )
    grad_arrival = grad_arrival + jnp.einsum(
        "erf,edf->erd", grad_up_low, up_back, preferred_element_type=jnp.float32
    )
    grad_arrival = grad_arrival.astype(jnp.bfloat16).reshape(1, local_experts, owners * capacity, D)
    grad_back = lax.all_to_all(
        grad_arrival, "expert", split_axis=2, concat_axis=0, tiled=True
    ).reshape(experts * capacity, D)
    grad_normed_ffn = jnp.sum(
        grad_back[slot_index].reshape(row_count, top_count, D).astype(jnp.float32), axis=1
    )
    expert_grads = (
        lax.psum_scatter(grad_gate_local, "dp", scatter_dimension=1, tiled=True),
        lax.psum_scatter(grad_up_local, "dp", scatter_dimension=1, tiled=True),
        lax.psum_scatter(grad_down_local, "dp", scatter_dimension=1, tiled=True),
    )
    grad_chosen = gates_pull(grad_gates)[0]
    expert_ids = jnp.arange(experts, dtype=jnp.int32)
    grad_logits = jnp.sum(
        jnp.where(routes[:, :, None] == expert_ids[None, None, :], grad_chosen[:, :, None], 0.0),
        axis=1,
    ).astype(jnp.bfloat16)
    grad_router_local = contract_rows(normed_ffn, grad_logits)
    dense_back = (
        lax.all_gather(w_query, ("dp", "expert"), axis=0, tiled=True),
        lax.all_gather(w_key, ("dp", "expert"), axis=0, tiled=True),
        lax.all_gather(w_value, ("dp", "expert"), axis=0, tiled=True),
        lax.all_gather(w_out, ("dp", "expert"), axis=0, tiled=True),
        lax.all_gather(w_router, ("dp", "expert"), axis=0, tiled=True),
    )
    query_back, key_back, value_back, out_back, router_back = dense_back
    grad_normed_ffn = grad_normed_ffn + times_transposed(grad_logits, router_back)
    grad_midway_norm, grad_ffn_gain = norm_ffn_pull(grad_normed_ffn)
    grad_midway = grad_out + grad_midway_norm
    grad_attn = grad_midway.astype(jnp.bfloat16)
    grad_out_local = contract_rows(context, grad_attn)
    grad_context = (
        times_transposed(grad_attn, out_back).astype(jnp.bfloat16).reshape(row_count, HEADS, HD)
    )
    probs = jnp.where(seq_mask, jnp.exp(scores - log_total), 0.0)
    grad_probs = jnp.einsum(
        "qhd,khd->hqk", grad_context, value_heads, preferred_element_type=jnp.float32
    )
    grad_scores = (
        probs * (grad_probs - jnp.sum(grad_probs * probs, axis=-1, keepdims=True))
    ).astype(jnp.bfloat16)
    grad_values = (
        jnp.einsum("hqk,qhd->khd", probs_low, grad_context, preferred_element_type=jnp.float32)
        .astype(jnp.bfloat16)
        .reshape(row_count, D)
    )
    grad_queries = (
        jnp.einsum("hqk,khd->qhd", grad_scores, keys_rot, preferred_element_type=jnp.float32)
        * score_scale
    )
    grad_keys = (
        jnp.einsum("hqk,qhd->khd", grad_scores, queries, preferred_element_type=jnp.float32)
        * score_scale
    )
    grad_raw_q, grad_raw_k, grad_query_gain, grad_key_gain = heads_pull((grad_queries, grad_keys))
    grad_raw_q = grad_raw_q.astype(jnp.bfloat16)
    grad_raw_k = grad_raw_k.astype(jnp.bfloat16)
    grad_query_local = contract_rows(normed_attn, grad_raw_q)
    grad_key_local = contract_rows(normed_attn, grad_raw_k)
    grad_value_local = contract_rows(normed_attn, grad_values)
    grad_normed_attn = (
        times_transposed(grad_raw_q, query_back)
        + times_transposed(grad_raw_k, key_back)
        + times_transposed(grad_values, value_back)
    )
    grad_inputs_norm, grad_attn_gain = norm_attn_pull(grad_normed_attn)
    grad_tokens = (grad_midway + grad_inputs_norm).astype(jnp.bfloat16)
    dense_grads = (
        lax.psum_scatter(grad_query_local, ("dp", "expert"), scatter_dimension=0, tiled=True),
        lax.psum_scatter(grad_key_local, ("dp", "expert"), scatter_dimension=0, tiled=True),
        lax.psum_scatter(grad_value_local, ("dp", "expert"), scatter_dimension=0, tiled=True),
        lax.psum_scatter(grad_out_local, ("dp", "expert"), scatter_dimension=0, tiled=True),
        lax.psum_scatter(grad_router_local, ("dp", "expert"), scatter_dimension=0, tiled=True),
        lax.psum_scatter(grad_attn_gain, ("dp", "expert"), scatter_dimension=0, tiled=True),
        lax.psum_scatter(grad_query_gain, ("dp", "expert"), scatter_dimension=0, tiled=True),
        lax.psum_scatter(grad_key_gain, ("dp", "expert"), scatter_dimension=0, tiled=True),
        lax.psum_scatter(grad_ffn_gain, ("dp", "expert"), scatter_dimension=0, tiled=True),
    )
    return (
        block_out,
        grad_tokens,
        dense_grads[0],
        dense_grads[1],
        dense_grads[2],
        dense_grads[3],
        dense_grads[4],
        expert_grads[0],
        expert_grads[1],
        expert_grads[2],
        dense_grads[5],
        dense_grads[6],
        dense_grads[7],
        dense_grads[8],
    )


SLOTS = 128


def flip(value, bit):
    count = lax.axis_size("expert")
    return lax.ppermute(value, "expert", [(i, i ^ bit) for i in range(count)])


def turn(value, step):
    count = lax.axis_size("dp")
    return lax.ppermute(value, "dp", [(i, (i + step) % count) for i in range(count)])


def order_kernel(to_own, order_ref, v_ref, o_ref):
    half = 64
    lanes = v_ref.shape[1] // 2
    groups = v_ref.shape[1] // 128
    odd = order_ref[groups] == 1
    for pair in range(groups // 2):
        first = pl.ds(pl.multiple_of(order_ref[2 * pair] * 128, 128), 128)
        second = pl.ds(pl.multiple_of(order_ref[2 * pair + 1] * 128, 128), 128)
        if to_own:
            a = v_ref[:, first].astype(jnp.float32)
            b = v_ref[:, second].astype(jnp.float32)
            low = jnp.concatenate([a[:, :half], b[:, :half]], axis=1)
            high = jnp.concatenate([a[:, half:], b[:, half:]], axis=1)
            o_ref[:, pair * 128 : pair * 128 + 128] = jnp.where(odd, high, low).astype(o_ref.dtype)
            o_ref[:, lanes + pair * 128 : lanes + pair * 128 + 128] = jnp.where(
                odd, low, high
            ).astype(o_ref.dtype)
        else:
            low = v_ref[:, pair * 128 : pair * 128 + 128].astype(jnp.float32)
            high = v_ref[:, lanes + pair * 128 : lanes + pair * 128 + 128].astype(jnp.float32)
            low, high = jnp.where(odd, high, low), jnp.where(odd, low, high)
            o_ref[:, first] = jnp.concatenate([low[:, :half], high[:, :half]], axis=1).astype(
                o_ref.dtype
            )
            o_ref[:, second] = jnp.concatenate([low[:, half:], high[:, half:]], axis=1).astype(
                o_ref.dtype
            )


def reorder(value, order, to_own):
    return pl.pallas_call(
        functools.partial(order_kernel, to_own),
        out_shape=jax.ShapeDtypeStruct(value.shape, value.dtype),
        in_specs=[
            pl.BlockSpec(memory_space=pltpu.SMEM),
            pl.BlockSpec(memory_space=pltpu.VMEM),
        ],
        out_specs=pl.BlockSpec(memory_space=pltpu.VMEM),
        compiler_params=pltpu.CompilerParams(vmem_limit_bytes=16 * 1024 * 1024),
        cost_estimate=pl.CostEstimate(flops=0, bytes_accessed=4 * value.size, transcendentals=0),
    )(order, value)


def ring_gather(value):
    pieces = [value]
    for _ in range(lax.axis_size("dp") - 1):
        pieces.append(turn(pieces[-1], 1))
    return pieces


def ring_scatter(pieces):
    total = pieces[-1]
    for piece in pieces[-2::-1]:
        total = turn(total, -1).astype(jnp.float32) + piece.astype(jnp.float32)
        if piece is not pieces[0]:
            total = total.astype(piece.dtype)
    return total


def gather_weight(shard):
    half = shard.shape[1] // 2
    pieces = ring_gather(shard)
    left = jnp.concatenate([p[:, :half] for p in pieces], axis=0)
    right = jnp.concatenate([p[:, half:] for p in pieces], axis=0)
    left_x, right_y = flip(left, 2), flip(right, 4)
    left = jnp.concatenate([left, left_x], axis=0)
    right = jnp.concatenate([right, right_y], axis=0)
    left_y, right_x = flip(left, 4), flip(right, 2)
    n = left.shape[0] // 2
    own = jnp.concatenate(
        [
            jnp.concatenate([left, left_y], axis=0),
            jnp.concatenate([right[:n], right_x[:n], right[n:], right_x[n:]], axis=0),
        ],
        axis=1,
    )
    return own, flip(own, 1)


def scatter_weight(own, other, rows):
    width = own.shape[1]
    half = width // 2
    n = own.shape[0] // 4
    low = jnp.bfloat16
    total = (own + flip(other.astype(low), 1).astype(jnp.float32)).astype(low)
    left, right = total[:, :half], total[:, half:]
    left_y = flip(left[2 * n :], 4).astype(jnp.float32)
    right_x = flip(jnp.concatenate([right[n : 2 * n], right[3 * n :]], axis=0), 2).astype(
        jnp.float32
    )
    left = (left[: 2 * n].astype(jnp.float32) + left_y).astype(low)
    right = (
        jnp.concatenate([right[:n], right[2 * n : 3 * n]], axis=0).astype(jnp.float32) + right_x
    ).astype(low)
    left_x, right_y = flip(left[n:], 2).astype(jnp.float32), flip(right[n:], 4).astype(jnp.float32)
    total = jnp.concatenate(
        [
            left[:n].astype(jnp.float32) + left_x,
            right[:n].astype(jnp.float32) + right_y,
        ],
        axis=1,
    ).astype(low)
    return ring_scatter([total[i * rows : (i + 1) * rows] for i in range(n // rows)])


def gather_small(shard, shard_order):
    pieces = jnp.stack(ring_gather(shard))
    for bit in (2, 4, 1):
        pieces = jnp.concatenate([pieces, flip(pieces, bit)], axis=0)
    return jnp.take(pieces, shard_order, axis=0).reshape(-1, shard.shape[1])


def scatter_small(value, shard_order, rows):
    pieces = jnp.take(value.reshape(-1, rows, value.shape[1]), shard_order, axis=0)
    for bit in (1, 4, 2):
        n = pieces.shape[0] // 2
        pieces = pieces[:n] + flip(pieces[n:], bit)
    return ring_scatter([pieces[i] for i in range(pieces.shape[0])])


def gather_tokens(value):
    pieces = ring_gather(value)
    mine = pieces + [flip(p, 2) for p in pieces]
    mine = jnp.stack(mine)
    return jnp.concatenate([mine, flip(mine, 1)], axis=0)


def scatter_tokens(blocks):
    n = blocks.shape[0] // 4
    low = blocks.dtype
    wide = jnp.float32
    across = blocks[2 * n :]
    total = (blocks[: 2 * n].astype(wide) + flip(across, 1).astype(wide)).astype(low)
    total = (total[:n].astype(wide) + flip(total[n:], 2).astype(wide)).astype(low)
    return ring_scatter([total[i] for i in range(n)])


def expert_rounds(count_dp, count_expert):
    rounds = []
    for k in range(count_dp):
        pairs = []
        for d in range(count_dp):
            part = (d + k) % count_dp
            for e in range(count_expert):
                goal = 2 * (e & 1) + part // 2
                pairs.append((d * count_expert + e, goal * count_expert + (e & ~1) + part % 2))
        rounds.append(pairs)
    return rounds


def gather_expert(weight, place):
    d, c, x, y = place
    count_dp, count_expert = lax.axis_size("dp"), lax.axis_size("expert")
    _, depth, width = weight.shape
    half = width // 2
    held = jnp.zeros((count_dp, depth, half), weight.dtype)
    for k, pairs in enumerate(expert_rounds(count_dp, count_expert)):
        part = (d + k) % count_dp
        piece = lax.dynamic_slice(weight, (part // 2, 0, half * (part % 2)), (1, depth, half))
        piece = lax.ppermute(piece, ("dp", "expert"), pairs)
        source = (2 * (d % 2) + c - k) % count_dp
        held = lax.dynamic_update_slice(held, piece, (source, 0, 0))
    held = held.reshape(count_dp * depth, half)
    far = flip(held, 4)
    keep = jnp.where(y == c, held, far)
    give = jnp.where(y == c, far, held)
    got = flip(give, 1)
    return jnp.concatenate(
        [jnp.where(c == 0, keep, got), jnp.where(c == 0, got, keep)], axis=1
    )


def scatter_expert(grad, place):
    d, c, x, y = place
    count_dp, count_expert = lax.axis_size("dp"), lax.axis_size("expert")
    half = grad.shape[1] // 2
    depth = grad.shape[0] // count_dp
    left, right = grad[:, :half], grad[:, half:]
    keep = jnp.where(c == 0, left, right)
    give = jnp.where(c == 0, right, left)
    got = flip(give, 1)
    far = flip(jnp.where(y == c, got, keep), 4)
    total = jnp.where(y == c, keep, got).astype(jnp.float32) + far.astype(jnp.float32)
    total = total.astype(grad.dtype).reshape(count_dp, depth, half)
    out = jnp.zeros((2, depth, 2 * half), jnp.float32)
    for k, pairs in enumerate(expert_rounds(count_dp, count_expert)):
        source = (2 * (d % 2) + c - k) % count_dp
        piece = lax.dynamic_slice(total, (source, 0, 0), (1, depth, half))
        piece = lax.ppermute(piece, ("dp", "expert"), [(b, a) for a, b in pairs])
        part = (d + k) % count_dp
        out = lax.dynamic_update_slice(
            out, piece.astype(jnp.float32), (part // 2, 0, half * (part % 2))
        )
    return out


def by_links(
    tokens,
    cotangent,
    lengths,
    routes,
    w_query,
    w_key,
    w_value,
    w_out,
    w_router,
    w_gate,
    w_up,
    w_down,
    g_attn,
    g_query,
    g_key,
    g_ffn,
):
    low, wide = jnp.bfloat16, jnp.float32
    row_count = tokens.shape[0]
    rows = w_query.shape[0]
    experts = w_router.shape[1]
    count_dp = lax.axis_size("dp")
    score_scale = HD ** (-0.5)
    d = lax.axis_index("dp")
    e = lax.axis_index("expert")
    c, x, y = e & 1, (e >> 1) & 1, e >> 2
    place = (d, c, x, y)
    own_expert = 8 * c + 4 * x + d
    group = jnp.arange(16, dtype=jnp.int32)
    group_order = (
        ((d - (group & 3)) % count_dp) * 4 + ((((group >> 3) & 1) ^ y) * 2 + (((group >> 2) & 1) ^ x))
    )
    order = jnp.concatenate([group_order, c[None]]).astype(jnp.int32)
    shard = jnp.arange(32, dtype=jnp.int32)
    to_own = group_order[shard & 15] * 2 + ((shard >> 4) ^ c)
    to_whole = (
        (((shard & 1) ^ c) * 16)
        + (((shard >> 2) & 1) ^ y) * 8
        + (((shard >> 1) & 1) ^ x) * 4
        + (d - (shard >> 3)) % count_dp
    )

    slab = jnp.concatenate(
        [w_router]
        + [g[:, None] for g in (g_attn, g_query, g_key, g_ffn)]
        + [jnp.zeros((rows, 128 - experts - 4), low)],
        axis=1,
    )
    slab = gather_small(slab, to_whole)
    router_w = slab[:, :experts]
    attn_gain, query_gain, key_gain, ffn_gain = (
        slab[:, experts + i].astype(wide) for i in range(4)
    )
    query_w = gather_weight(w_query)
    key_w = gather_weight(w_key)
    value_w = gather_weight(w_value)
    out_w = gather_weight(w_out)
    routes_all = gather_tokens(routes)
    gate_w = gather_expert(w_gate, place)
    up_w = gather_expert(w_up, place)
    down_w = gather_expert(w_down, place)
    grad_out_all = gather_tokens(cotangent)

    segment, offset = layout(lengths[0], row_count)
    seq_mask = (segment[:, None] == segment[None, :])[None]
    inputs = tokens.astype(wide)
    normed_f, norm_attn_pull = jax.vjp(normalize, inputs, attn_gain)
    normed_attn = reorder(normed_f.astype(low), order, True)
    half = D // 2

    def times(left, pair):
        return jnp.dot(left[:, :half], pair[0], preferred_element_type=wide) + jnp.dot(
            left[:, half:], pair[1], preferred_element_type=wide
        )

    raw_q = times(normed_attn, query_w)
    raw_k = times(normed_attn, key_w)
    values = times(normed_attn, value_w).astype(low)
    value_heads = values.reshape(row_count, HEADS, HD)

    def prep_local(first, second, first_gain, second_gain):
        return head_prep(first, second, first_gain, second_gain, offset)

    rotated, heads_pull = jax.vjp(prep_local, raw_q, raw_k, query_gain, key_gain)
    queries = rotated[0].astype(low)
    keys_rot = rotated[1].astype(low)
    scores = (
        jnp.einsum("qhd,khd->hqk", queries, keys_rot, preferred_element_type=wide) * score_scale
    )
    scores = jnp.where(seq_mask, scores, -1e30)
    peak = jnp.max(scores, axis=-1, keepdims=True)
    exp_scores = jnp.exp(scores - peak)
    exp_total = jnp.sum(exp_scores, axis=-1, keepdims=True)
    log_total = peak + jnp.log(exp_total)
    probs_low = (exp_scores / exp_total).astype(low)
    context = (
        jnp.einsum("hqk,khd->qhd", probs_low, value_heads, preferred_element_type=wide)
        .astype(low)
        .reshape(row_count, D)
    )
    context = reorder(context, order, True)
    midway = inputs + times(context, out_w)
    normed2_f, norm_ffn_pull = jax.vjp(normalize, midway, ffn_gain)
    normed_ffn = normed2_f.astype(low)

    normed_all = gather_tokens(normed_ffn)
    blocks = normed_all.shape[0]

    def dense_gates(logits, named):
        logits = jnp.where(named, logits, -jnp.inf)
        exp_logits = jnp.exp(logits - jnp.max(logits, axis=-1, keepdims=True))
        return exp_logits / jnp.sum(exp_logits, axis=-1, keepdims=True)

    expert_ids = jnp.arange(experts, dtype=jnp.int32)

    def named_of(table):
        return jnp.any(table[..., :, None] == expert_ids, axis=-2)

    logits_all = jnp.einsum("btd,de->bte", normed_all, router_w, preferred_element_type=wide)
    named_all = named_of(routes_all)
    gates_all = dense_gates(logits_all, named_all)
    mine = (expert_ids == own_expert)[None, None, :]
    own_gate = jnp.sum(jnp.where(mine, gates_all, 0.0), axis=2)
    own_named = jnp.any(named_all & mine, axis=2)
    rank = jnp.cumsum(own_named.astype(jnp.int32), axis=1) - 1
    slot_ids = jnp.arange(SLOTS, dtype=jnp.int32)
    chosen = (rank[:, None, :] == slot_ids[None, :, None]) & own_named[:, None, :]
    picks = chosen.astype(low)
    slot_gate = jnp.sum(jnp.where(chosen, own_gate[:, None, :], 0.0), axis=2)

    def to_slots(value):
        return jnp.einsum("bst,btd->bsd", picks, value, preferred_element_type=wide).astype(low)

    def to_tokens(value):
        return jnp.einsum("bst,bsd->btd", picks, value, preferred_element_type=wide).astype(low)

    arrived = to_slots(normed_all).reshape(blocks * SLOTS, D)
    grad_rows = to_slots(grad_out_all)
    gate_act = jnp.dot(arrived, gate_w, preferred_element_type=wide)
    up_act = jnp.dot(arrived, up_w, preferred_element_type=wide)
    hidden = swiglu(gate_act, up_act).astype(low)
    produced = (
        jnp.dot(hidden, down_w, preferred_element_type=wide).astype(low).reshape(blocks, SLOTS, D)
    )
    slot_grad_gate = jnp.sum(grad_rows.astype(wide) * produced.astype(wide), axis=2)
    grad_gates_own = jnp.sum(jnp.where(chosen, slot_grad_gate[:, :, None], 0.0), axis=1)
    grad_gates_all = jnp.where(
        (expert_ids == own_expert)[None, :, None], grad_gates_own[:, None, :], 0.0
    )
    grad_gates = scatter_tokens(grad_gates_all).T
    moe_part = to_tokens((slot_gate[:, :, None] * produced.astype(wide)).astype(low))
    grad_produced = (
        (slot_gate[:, :, None] * grad_rows.astype(wide)).astype(low).reshape(blocks * SLOTS, D)
    )
    grad_hidden = times_transposed(grad_produced, down_w)
    act_unused, act_pull = jax.vjp(swiglu, gate_act, up_act)
    grad_gate_act, grad_up_act = act_pull(grad_hidden)
    grad_gate_low = grad_gate_act.astype(low)
    grad_up_low = grad_up_act.astype(low)
    grad_arrival = (
        times_transposed(grad_gate_low, gate_w) + times_transposed(grad_up_low, up_w)
    ).astype(low)
    grad_normed_ffn = scatter_tokens(to_tokens(grad_arrival.reshape(blocks, SLOTS, D)))
    block_out = (midway + scatter_tokens(moe_part)).astype(low)
    grad_down = scatter_expert(contract_rows(hidden, grad_produced).astype(low), place)
    grad_gate = scatter_expert(contract_rows(arrived, grad_gate_low).astype(low), place)
    grad_up = scatter_expert(contract_rows(arrived, grad_up_low).astype(low), place)

    grad_out = cotangent.astype(wide)
    gates = gates_all[0]
    grad_chosen = gates * (grad_gates - jnp.sum(gates * grad_gates, axis=1, keepdims=True))
    grad_logits = grad_chosen.astype(low)
    grad_router_local = contract_rows(normed_ffn, grad_logits)
    grad_normed_ffn = grad_normed_ffn + times_transposed(grad_logits, router_w)
    grad_midway_norm, grad_ffn_gain = norm_ffn_pull(grad_normed_ffn)
    grad_midway = grad_out + grad_midway_norm
    grad_attn = grad_midway.astype(low)

    def weight_grad(left, right):
        own = contract_rows(left[:, :half], right)
        other = contract_rows(left[:, half:], right)
        return scatter_weight(own, other, rows)

    def times_back(left, pair):
        return jnp.concatenate(
            [times_transposed(left, pair[0]), times_transposed(left, pair[1])], axis=1
        )

    grad_outproj = weight_grad(context, grad_attn)
    grad_context = reorder(times_back(grad_attn, out_w).astype(low), order, False).reshape(
        row_count, HEADS, HD
    )
    probs = jnp.where(seq_mask, jnp.exp(scores - log_total), 0.0)
    grad_probs = jnp.einsum("qhd,khd->hqk", grad_context, value_heads, preferred_element_type=wide)
    grad_scores = (
        probs * (grad_probs - jnp.sum(grad_probs * probs, axis=-1, keepdims=True))
    ).astype(low)
    grad_values = (
        jnp.einsum("hqk,qhd->khd", probs_low, grad_context, preferred_element_type=wide)
        .astype(low)
        .reshape(row_count, D)
    )
    grad_queries = (
        jnp.einsum("hqk,khd->qhd", grad_scores, keys_rot, preferred_element_type=wide)
        * score_scale
    )
    grad_keys = (
        jnp.einsum("hqk,qhd->khd", grad_scores, queries, preferred_element_type=wide) * score_scale
    )
    grad_raw_q, grad_raw_k, grad_query_gain, grad_key_gain = heads_pull((grad_queries, grad_keys))
    grad_raw_q = grad_raw_q.astype(low)
    grad_raw_k = grad_raw_k.astype(low)
    grad_value = weight_grad(normed_attn, grad_values)
    grad_query = weight_grad(normed_attn, grad_raw_q)
    grad_key = weight_grad(normed_attn, grad_raw_k)
    grad_normed_attn = (
        times_back(grad_raw_q, query_w)
        + times_back(grad_raw_k, key_w)
        + times_back(grad_values, value_w)
    )
    grad_normed_attn = reorder(grad_normed_attn, order, False)
    grad_inputs_norm, grad_attn_gain = norm_attn_pull(grad_normed_attn)
    grad_tokens = (grad_midway + grad_inputs_norm).astype(low)
    small = jnp.concatenate(
        [grad_router_local]
        + [g[:, None] for g in (grad_attn_gain, grad_query_gain, grad_key_gain, grad_ffn_gain)]
        + [jnp.zeros((D, 128 - experts - 4), wide)],
        axis=1,
    )
    small = scatter_small(small, to_own, rows)
    return (
        block_out,
        grad_tokens,
        grad_query,
        grad_key,
        grad_value,
        grad_outproj,
        small[:, :experts],
        grad_gate,
        grad_up,
        grad_down,
        small[:, experts],
        small[:, experts + 1],
        small[:, experts + 2],
        small[:, experts + 3],
    )


def solution(mesh):
    in_specs = (
        P(("dp", "expert"), None),
        P(("dp", "expert"), None),
        P(("dp", "expert"), None),
        P(("dp", "expert"), None),
        P(("dp", "expert"), None),
        P(("dp", "expert"), None),
        P(("dp", "expert"), None),
        P(("dp", "expert"), None),
        P(("dp", "expert"), None),
        P("expert", "dp", None),
        P("expert", "dp", None),
        P("expert", "dp", None),
        P(("dp", "expert")),
        P(("dp", "expert")),
        P(("dp", "expert")),
        P(("dp", "expert")),
    )
    out_specs = (
        P(("dp", "expert"), None),
        P(("dp", "expert"), None),
        P(("dp", "expert"), None),
        P(("dp", "expert"), None),
        P(("dp", "expert"), None),
        P(("dp", "expert"), None),
        P(("dp", "expert"), None),
        P("expert", "dp", None),
        P("expert", "dp", None),
        P("expert", "dp", None),
        P(("dp", "expert")),
        P(("dp", "expert")),
        P(("dp", "expert")),
        P(("dp", "expert")),
    )
    local = by_links if (mesh.shape["dp"], mesh.shape["expert"]) == (4, 8) else by_axes
    return jax.shard_map(local, mesh=mesh, in_specs=in_specs, out_specs=out_specs, check_vma=False)
```

```python
import functools

import jax
import jax.numpy as jnp
from jax import lax
from jax.experimental import pallas as pl
from jax.experimental.pallas import tpu as pltpu
from jax.sharding import PartitionSpec as P

D = 2048
HEADS = 16
HD = 128


EPS = 1e-05
THETA = 50000.0


def normalize(v, gain):
    return v * lax.rsqrt(jnp.mean(v * v, axis=-1, keepdims=True) + EPS) * gain


def layout(lengths_row, row_count):
    seq_ends = jnp.cumsum(lengths_row)
    position = jnp.arange(row_count, dtype=jnp.int32)
    segment = jnp.sum((position[:, None] >= seq_ends[None, :]).astype(jnp.int32), axis=1)
    seq_starts = seq_ends - lengths_row
    labels = jnp.arange(lengths_row.shape[0], dtype=jnp.int32)
    seq_start = jnp.sum(
        jnp.where(segment[:, None] == labels[None, :], seq_starts[None, :], 0), axis=1
    )
    return (segment, position - seq_start)


def rotate(v, offset):
    half_dim = v.shape[-1] // 2
    frequency = THETA ** (-jnp.arange(half_dim).astype(v.dtype) / half_dim)
    angles = offset.astype(v.dtype)[:, None] * frequency[None, :]
    cosine = jnp.cos(angles)[:, None, :]
    sine_part = jnp.sin(angles)[:, None, :]
    first_half = v[..., :half_dim]
    second_half = v[..., half_dim:]
    return jnp.concatenate(
        [
            first_half * cosine - second_half * sine_part,
            second_half * cosine + first_half * sine_part,
        ],
        axis=-1,
    )


def head_prep(raw_q, raw_k, gain_q, gain_k, offset):
    row_count = raw_q.shape[0]
    queries = rotate(
        normalize(raw_q.reshape(row_count, HEADS, HD), gain_q.reshape(HEADS, HD)), offset
    )
    keys_rot = rotate(
        normalize(raw_k.reshape(row_count, HEADS, HD), gain_k.reshape(HEADS, HD)), offset
    )
    return (queries, keys_rot)


def route_softmax(chosen):
    peak = jnp.max(chosen, axis=-1, keepdims=True)
    exp_scores = jnp.exp(chosen - peak)
    return exp_scores / jnp.sum(exp_scores, axis=-1, keepdims=True)


def swiglu(gate_act, up_act):
    return jax.nn.silu(gate_act) * up_act


def slots(flat_routes, expert_count, capacity):
    one_hot = (flat_routes[:, None] == jnp.arange(expert_count, dtype=jnp.int32)[None, :]).astype(
        jnp.int32
    )
    slot_rank = jnp.sum((jnp.cumsum(one_hot, axis=0) - one_hot) * one_hot, axis=1)
    return flat_routes * capacity + slot_rank


def contract_rows(left, right):
    return lax.dot_general(
        left, right, (((0,), (0,)), ((), ())), preferred_element_type=jnp.float32
    )


def times_transposed(left, right):
    return lax.dot_general(
        left, right, (((1,), (1,)), ((), ())), preferred_element_type=jnp.float32
    )


def by_axes(
    tokens,
    cotangent,
    lengths,
    routes,
    w_query,
    w_key,
    w_value,
    w_out,
    w_router,
    w_gate,
    w_up,
    w_down,
    g_attn,
    g_query,
    g_key,
    g_ffn,
):
    row_count = tokens.shape[0]
    top_count = routes.shape[1]
    local_experts = w_gate.shape[0]
    owners = lax.axis_size("expert")
    experts = local_experts * owners
    capacity = row_count * top_count * 5 // (4 * experts)
    score_scale = HD ** (-0.5)
    segment, offset = layout(lengths[0], row_count)
    seq_mask = (segment[:, None] == segment[None, :])[None]
    dense = (
        lax.all_gather(w_query, ("dp", "expert"), axis=0, tiled=True),
        lax.all_gather(w_key, ("dp", "expert"), axis=0, tiled=True),
        lax.all_gather(w_value, ("dp", "expert"), axis=0, tiled=True),
        lax.all_gather(w_out, ("dp", "expert"), axis=0, tiled=True),
        lax.all_gather(w_router, ("dp", "expert"), axis=0, tiled=True),
        lax.all_gather(g_attn, ("dp", "expert"), axis=0, tiled=True),
        lax.all_gather(g_query, ("dp", "expert"), axis=0, tiled=True),
        lax.all_gather(g_key, ("dp", "expert"), axis=0, tiled=True),
        lax.all_gather(g_ffn, ("dp", "expert"), axis=0, tiled=True),
    )
    query_w, key_w, value_w, out_w, router_w, attn_gain, query_gain, key_gain, ffn_gain = dense
    expert_full = (
        lax.all_gather(w_gate, "dp", axis=1, tiled=True),
        lax.all_gather(w_up, "dp", axis=1, tiled=True),
        lax.all_gather(w_down, "dp", axis=1, tiled=True),
    )
    gate_full, up_full, down_full = expert_full
    inputs = tokens.astype(jnp.float32)
    normed_f, norm_attn_pull = jax.vjp(normalize, inputs, attn_gain.astype(jnp.float32))
    normed_attn = normed_f.astype(jnp.bfloat16)
    raw_q = jnp.dot(normed_attn, query_w, preferred_element_type=jnp.float32)
    raw_k = jnp.dot(normed_attn, key_w, preferred_element_type=jnp.float32)
    values = jnp.dot(normed_attn, value_w, preferred_element_type=jnp.float32).astype(jnp.bfloat16)
    value_heads = values.reshape(row_count, HEADS, HD)

    def prep_local(first, second, first_gain, second_gain):
        return head_prep(first, second, first_gain, second_gain, offset)

    rotated, heads_pull = jax.vjp(
        prep_local, raw_q, raw_k, query_gain.astype(jnp.float32), key_gain.astype(jnp.float32)
    )
    queries = rotated[0].astype(jnp.bfloat16)
    keys_rot = rotated[1].astype(jnp.bfloat16)
    scores = (
        jnp.einsum("qhd,khd->hqk", queries, keys_rot, preferred_element_type=jnp.float32)
        * score_scale
    )
    scores = jnp.where(seq_mask, scores, -1e30)
    peak = jnp.max(scores, axis=-1, keepdims=True)
    exp_scores = jnp.exp(scores - peak)
    exp_total = jnp.sum(exp_scores, axis=-1, keepdims=True)
    log_total = peak + jnp.log(exp_total)
    probs_low = (exp_scores / exp_total).astype(jnp.bfloat16)
    context = (
        jnp.einsum("hqk,khd->qhd", probs_low, value_heads, preferred_element_type=jnp.float32)
        .astype(jnp.bfloat16)
        .reshape(row_count, D)
    )
    midway = inputs + jnp.dot(context, out_w, preferred_element_type=jnp.float32)
    normed2_f, norm_ffn_pull = jax.vjp(normalize, midway, ffn_gain.astype(jnp.float32))
    normed_ffn = normed2_f.astype(jnp.bfloat16)
    logits = jnp.dot(normed_ffn, router_w, preferred_element_type=jnp.float32)
    chosen = jnp.take_along_axis(logits, routes, axis=1)
    gates, gates_pull = jax.vjp(route_softmax, chosen)
    slot_index = slots(routes.reshape(-1), experts, capacity)
    sent_rows = (
        jnp.zeros((experts * capacity, D), jnp.bfloat16)
        .at[slot_index]
        .set(jnp.repeat(normed_ffn, top_count, axis=0))
    )
    sent_rows = sent_rows.reshape(owners, local_experts, capacity, D)
    arrived = lax.all_to_all(sent_rows, "expert", split_axis=0, concat_axis=2, tiled=True).reshape(
        local_experts, owners * capacity, D
    )
    gate_act = jnp.einsum("erd,edf->erf", arrived, gate_full, preferred_element_type=jnp.float32)
    up_act = jnp.einsum("erd,edf->erf", arrived, up_full, preferred_element_type=jnp.float32)
    hidden = swiglu(gate_act, up_act).astype(jnp.bfloat16)
    produced = jnp.einsum(
        "erf,efd->erd", hidden, down_full, preferred_element_type=jnp.float32
    ).astype(jnp.bfloat16)
    returned = lax.all_to_all(
        produced.reshape(1, local_experts, owners * capacity, D),
        "expert",
        split_axis=2,
        concat_axis=0,
        tiled=True,
    ).reshape(experts * capacity, D)
    picked = returned[slot_index].reshape(row_count, top_count, D).astype(jnp.float32)
    block_out = (midway + jnp.sum(gates[:, :, None] * picked, axis=1)).astype(jnp.bfloat16)
    grad_out = cotangent.astype(jnp.float32)
    grad_gates = jnp.sum(grad_out[:, None, :] * picked, axis=2)
    grad_picked = (
        (gates[:, :, None] * grad_out[:, None, :])
        .astype(jnp.bfloat16)
        .reshape(row_count * top_count, D)
    )
    grad_sent = jnp.zeros((experts * capacity, D), jnp.bfloat16).at[slot_index].set(grad_picked)
    grad_sent = grad_sent.reshape(owners, local_experts, capacity, D)
    grad_arrived = lax.all_to_all(
        grad_sent, "expert", split_axis=0, concat_axis=2, tiled=True
    ).reshape(local_experts, owners * capacity, D)
    gate_back, up_back, down_back = (
        lax.all_gather(w_gate, "dp", axis=1, tiled=True),
        lax.all_gather(w_up, "dp", axis=1, tiled=True),
        lax.all_gather(w_down, "dp", axis=1, tiled=True),
    )
    grad_hidden = jnp.einsum(
        "erd,efd->erf", grad_arrived, down_back, preferred_element_type=jnp.float32
    )
    grad_down_local = jnp.einsum(
        "erf,erd->efd", hidden, grad_arrived, preferred_element_type=jnp.float32
    )
    act_unused, act_pull = jax.vjp(swiglu, gate_act, up_act)
    grad_gate_act, grad_up_act = act_pull(grad_hidden)
    grad_gate_low = grad_gate_act.astype(jnp.bfloat16)
    grad_up_low = grad_up_act.astype(jnp.bfloat16)
    grad_gate_local = jnp.einsum(
        "erd,erf->edf", arrived, grad_gate_low, preferred_element_type=jnp.float32
    )
    grad_up_local = jnp.einsum(
        "erd,erf->edf", arrived, grad_up_low, preferred_element_type=jnp.float32
    )
    grad_arrival = jnp.einsum(
        "erf,edf->erd", grad_gate_low, gate_back, preferred_element_type=jnp.float32
    )
    grad_arrival = grad_arrival + jnp.einsum(
        "erf,edf->erd", grad_up_low, up_back, preferred_element_type=jnp.float32
    )
    grad_arrival = grad_arrival.astype(jnp.bfloat16).reshape(1, local_experts, owners * capacity, D)
    grad_back = lax.all_to_all(
        grad_arrival, "expert", split_axis=2, concat_axis=0, tiled=True
    ).reshape(experts * capacity, D)
    grad_normed_ffn = jnp.sum(
        grad_back[slot_index].reshape(row_count, top_count, D).astype(jnp.float32), axis=1
    )
    expert_grads = (
        lax.psum_scatter(grad_gate_local, "dp", scatter_dimension=1, tiled=True),
        lax.psum_scatter(grad_up_local, "dp", scatter_dimension=1, tiled=True),
        lax.psum_scatter(grad_down_local, "dp", scatter_dimension=1, tiled=True),
    )
    grad_chosen = gates_pull(grad_gates)[0]
    expert_ids = jnp.arange(experts, dtype=jnp.int32)
    grad_logits = jnp.sum(
        jnp.where(routes[:, :, None] == expert_ids[None, None, :], grad_chosen[:, :, None], 0.0),
        axis=1,
    ).astype(jnp.bfloat16)
    grad_router_local = contract_rows(normed_ffn, grad_logits)
    dense_back = (
        lax.all_gather(w_query, ("dp", "expert"), axis=0, tiled=True),
        lax.all_gather(w_key, ("dp", "expert"), axis=0, tiled=True),
        lax.all_gather(w_value, ("dp", "expert"), axis=0, tiled=True),
        lax.all_gather(w_out, ("dp", "expert"), axis=0, tiled=True),
        lax.all_gather(w_router, ("dp", "expert"), axis=0, tiled=True),
    )
    query_back, key_back, value_back, out_back, router_back = dense_back
    grad_normed_ffn = grad_normed_ffn + times_transposed(grad_logits, router_back)
    grad_midway_norm, grad_ffn_gain = norm_ffn_pull(grad_normed_ffn)
    grad_midway = grad_out + grad_midway_norm
    grad_attn = grad_midway.astype(jnp.bfloat16)
    grad_out_local = contract_rows(context, grad_attn)
    grad_context = (
        times_transposed(grad_attn, out_back).astype(jnp.bfloat16).reshape(row_count, HEADS, HD)
    )
    probs = jnp.where(seq_mask, jnp.exp(scores - log_total), 0.0)
    grad_probs = jnp.einsum(
        "qhd,khd->hqk", grad_context, value_heads, preferred_element_type=jnp.float32
    )
    grad_scores = (
        probs * (grad_probs - jnp.sum(grad_probs * probs, axis=-1, keepdims=True))
    ).astype(jnp.bfloat16)
    grad_values = (
        jnp.einsum("hqk,qhd->khd", probs_low, grad_context, preferred_element_type=jnp.float32)
        .astype(jnp.bfloat16)
        .reshape(row_count, D)
    )
    grad_queries = (
        jnp.einsum("hqk,khd->qhd", grad_scores, keys_rot, preferred_element_type=jnp.float32)
        * score_scale
    )
    grad_keys = (
        jnp.einsum("hqk,qhd->khd", grad_scores, queries, preferred_element_type=jnp.float32)
        * score_scale
    )
    grad_raw_q, grad_raw_k, grad_query_gain, grad_key_gain = heads_pull((grad_queries, grad_keys))
    grad_raw_q = grad_raw_q.astype(jnp.bfloat16)
    grad_raw_k = grad_raw_k.astype(jnp.bfloat16)
    grad_query_local = contract_rows(normed_attn, grad_raw_q)
    grad_key_local = contract_rows(normed_attn, grad_raw_k)
    grad_value_local = contract_rows(normed_attn, grad_values)
    grad_normed_attn = (
        times_transposed(grad_raw_q, query_back)
        + times_transposed(grad_raw_k, key_back)
        + times_transposed(grad_values, value_back)
    )
    grad_inputs_norm, grad_attn_gain = norm_attn_pull(grad_normed_attn)
    grad_tokens = (grad_midway + grad_inputs_norm).astype(jnp.bfloat16)
    dense_grads = (
        lax.psum_scatter(grad_query_local, ("dp", "expert"), scatter_dimension=0, tiled=True),
        lax.psum_scatter(grad_key_local, ("dp", "expert"), scatter_dimension=0, tiled=True),
        lax.psum_scatter(grad_value_local, ("dp", "expert"), scatter_dimension=0, tiled=True),
        lax.psum_scatter(grad_out_local, ("dp", "expert"), scatter_dimension=0, tiled=True),
        lax.psum_scatter(grad_router_local, ("dp", "expert"), scatter_dimension=0, tiled=True),
        lax.psum_scatter(grad_attn_gain, ("dp", "expert"), scatter_dimension=0, tiled=True),
        lax.psum_scatter(grad_query_gain, ("dp", "expert"), scatter_dimension=0, tiled=True),
        lax.psum_scatter(grad_key_gain, ("dp", "expert"), scatter_dimension=0, tiled=True),
        lax.psum_scatter(grad_ffn_gain, ("dp", "expert"), scatter_dimension=0, tiled=True),
    )
    return (
        block_out,
        grad_tokens,
        dense_grads[0],
        dense_grads[1],
        dense_grads[2],
        dense_grads[3],
        dense_grads[4],
        expert_grads[0],
        expert_grads[1],
        expert_grads[2],
        dense_grads[5],
        dense_grads[6],
        dense_grads[7],
        dense_grads[8],
    )


SLOTS = 128
SMALL = pl.CostEstimate(flops=1, bytes_accessed=1, transcendentals=0)


def flip(value, bit):
    count = lax.axis_size("expert")
    return lax.ppermute(value, "expert", [(i, i ^ bit) for i in range(count)])


def turn(value, step):
    count = lax.axis_size("dp")
    return lax.ppermute(value, "dp", [(i, (i + step) % count) for i in range(count)])


def order_kernel(to_own, order_ref, v_ref, o_ref):
    half = 64
    lanes = v_ref.shape[1] // 2
    groups = v_ref.shape[1] // 128
    odd = order_ref[groups] == 1
    for pair in range(groups // 2):
        first = pl.ds(pl.multiple_of(order_ref[2 * pair] * 128, 128), 128)
        second = pl.ds(pl.multiple_of(order_ref[2 * pair + 1] * 128, 128), 128)
        if to_own:
            a = v_ref[:, first].astype(jnp.float32)
            b = v_ref[:, second].astype(jnp.float32)
            low = jnp.concatenate([a[:, :half], b[:, :half]], axis=1)
            high = jnp.concatenate([a[:, half:], b[:, half:]], axis=1)
            o_ref[:, pair * 128 : pair * 128 + 128] = jnp.where(odd, high, low).astype(o_ref.dtype)
            o_ref[:, lanes + pair * 128 : lanes + pair * 128 + 128] = jnp.where(
                odd, low, high
            ).astype(o_ref.dtype)
        else:
            low = v_ref[:, pair * 128 : pair * 128 + 128].astype(jnp.float32)
            high = v_ref[:, lanes + pair * 128 : lanes + pair * 128 + 128].astype(jnp.float32)
            low, high = jnp.where(odd, high, low), jnp.where(odd, low, high)
            o_ref[:, first] = jnp.concatenate([low[:, :half], high[:, :half]], axis=1).astype(
                o_ref.dtype
            )
            o_ref[:, second] = jnp.concatenate([low[:, half:], high[:, half:]], axis=1).astype(
                o_ref.dtype
            )


def reorder(value, order, to_own):
    return pl.pallas_call(
        functools.partial(order_kernel, to_own),
        out_shape=jax.ShapeDtypeStruct(value.shape, value.dtype),
        in_specs=[
            pl.BlockSpec(memory_space=pltpu.SMEM),
            pl.BlockSpec(memory_space=pltpu.VMEM),
        ],
        out_specs=pl.BlockSpec(memory_space=pltpu.VMEM),
        compiler_params=pltpu.CompilerParams(vmem_limit_bytes=16 * 1024 * 1024),
        cost_estimate=pl.CostEstimate(flops=0, bytes_accessed=4 * value.size, transcendentals=0),
    )(order, value)


def ring_gather(value):
    pieces = [value]
    for _ in range(lax.axis_size("dp") - 1):
        pieces.append(turn(pieces[-1], 1))
    return pieces


def ring_scatter(pieces):
    total = pieces[-1]
    for piece in pieces[-2::-1]:
        total = turn(total, -1).astype(jnp.float32) + piece.astype(jnp.float32)
        if piece is not pieces[0]:
            total = total.astype(piece.dtype)
    return total


def side_by_side(pieces, width):
    return (
        jnp.concatenate([p[:, :width] for p in pieces], axis=0),
        jnp.concatenate([p[:, width:] for p in pieces], axis=0),
    )


def by_x(own, far):
    n = own.shape[0] // 2
    return jnp.concatenate([own[:n], far[:n], own[n:], far[n:]], axis=0)


def ring_scatter_up(pieces):
    low, wide = pieces[0].dtype, jnp.float32
    total = pieces[1]
    for piece in pieces[2:]:
        total = (turn(total, 1).astype(wide) + piece.astype(wide)).astype(low)
    return turn(total, 1).astype(wide) + pieces[0].astype(wide)


def expert_rounds(count_dp, count_expert):
    rounds = []
    for r in range(2):
        pairs = []
        for d in range(count_dp):
            for e in range(count_expert):
                goal = 2 * (e & 1) + (d // 2 + r) % 2
                pairs.append((d * count_expert + e, goal * count_expert + (e & ~1) + d % 2))
        rounds.append(pairs)
    return rounds


def to_owner(weight, place):
    d, c, x, y = place
    rounds = expert_rounds(lax.axis_size("dp"), lax.axis_size("expert"))
    pieces = []
    for r, pairs in enumerate(rounds):
        piece = lax.dynamic_index_in_dim(weight, (d // 2 + r) % 2, 0, keepdims=False)
        pieces.append(lax.ppermute(piece, ("dp", "expert"), pairs))
    return pieces


def to_both(held, far, place):
    d, c, x, y = place
    return jnp.where(y == c, held, far), jnp.where(y == c, far, held)


def from_owner(keep, got, place):
    d, c, x, y = place
    return jnp.where(y == c, keep, got), jnp.where(y == c, got, keep)


def to_shards(total, place):
    d, c, x, y = place
    rounds = expert_rounds(lax.axis_size("dp"), lax.axis_size("expert"))
    n = total.shape[0] // 2
    return [
        lax.ppermute(total[r * n : (r + 1) * n], ("dp", "expert"), [(b, a) for a, b in pairs])
        for r, pairs in enumerate(rounds)
    ]


def two_experts(pieces, place):
    d, c, x, y = place
    first, second = (p.astype(jnp.float32) for p in pieces)
    own = d // 2 == 0
    return jnp.stack([jnp.where(own, first, second), jnp.where(own, second, first)])


def contract_kernel(count, *refs):
    out_ref = refs[-1]
    out_ref[...] = sum(
        lax.dot_general(
            left_ref[...],
            right_ref[...],
            (((0,), (0,)), ((), ())),
            preferred_element_type=jnp.float32,
        )
        for left_ref, right_ref in zip(refs[:count], refs[count : 2 * count])
    ).astype(out_ref.dtype)


def contract(lefts, rights, low=jnp.bfloat16):
    depth, width = lefts[0].shape
    across = rights[0].shape[1]
    block = 512
    return pl.pallas_call(
        functools.partial(contract_kernel, len(lefts)),
        grid=(width // block,),
        in_specs=[pl.BlockSpec((depth, block), lambda i: (0, i))] * len(lefts)
        + [pl.BlockSpec((depth, across), lambda i: (0, 0))] * len(rights),
        out_specs=pl.BlockSpec((block, across), lambda i: (i, 0)),
        out_shape=jax.ShapeDtypeStruct((width, across), low),
        compiler_params=pltpu.CompilerParams(vmem_limit_bytes=48 * 1024 * 1024),
        cost_estimate=SMALL,
    )(*lefts, *rights)


def head_norm(v):
    return lax.rsqrt(jnp.mean(v * v, axis=-1, keepdims=True) + EPS)


def dot32(left, right, dims):
    return lax.dot_general(
        left, right, ((dims[:1], dims[1:]), ((), ())), preferred_element_type=jnp.float32
    )


def masked_softmax(q, k, same):
    scores = jnp.where(same, dot32(q, k, (1, 1)) * HD ** (-0.5), -1e30)
    weights = jnp.exp(scores - jnp.max(scores, axis=-1, keepdims=True))
    return weights / jnp.sum(weights, axis=-1, keepdims=True)


def attend_kernel(
    order_ref, raw_q, raw_k, v_ref, gain_q, gain_k, cos_ref, sin_ref, seg_c, seg_r, q_ref, k_ref, o_ref
):
    low = jnp.bfloat16
    same = seg_c[...] == seg_r[...]
    lanes = o_ref.shape[1] // 2
    groups = lanes // 64
    odd = order_ref[groups] == 1

    def head(h):
        cols = pl.ds(pl.multiple_of(h * HD, HD), HD)

        def prepared(raw, gain):
            v = raw[:, cols]
            v = v * head_norm(v) * gain[:, cols]
            return (v * cos_ref[...] + pltpu.roll(v, HD // 2, 1) * sin_ref[...]).astype(low)

        q, k = prepared(raw_q, gain_q), prepared(raw_k, gain_k)
        q_ref[:, cols], k_ref[:, cols] = q, k
        probs = masked_softmax(q, k, same).astype(low)
        return dot32(probs, v_ref[:, cols], (1, 0))

    @pl.loop(0, groups // 2)
    def _(pair):
        a, b = head(order_ref[2 * pair]), head(order_ref[2 * pair + 1])
        first = jnp.concatenate([a[:, :64], b[:, :64]], axis=1)
        second = jnp.concatenate([a[:, 64:], b[:, 64:]], axis=1)
        cols = pl.ds(pl.multiple_of(pair * 128, 128), 128)
        o_ref[:, cols] = jnp.where(odd, second, first).astype(low)
        cols = pl.ds(pl.multiple_of(lanes + pair * 128, 128), 128)
        o_ref[:, cols] = jnp.where(odd, first, second).astype(low)


def attend_back_kernel(
    order_ref,
    grad_ref,
    q_ref,
    k_ref,
    v_ref,
    raw_q,
    raw_k,
    gain_q,
    gain_k,
    cos_ref,
    sin_ref,
    seg_c,
    seg_r,
    d_ref,
    gq_ref,
    gk_ref,
):
    low, wide = jnp.bfloat16, jnp.float32
    same = seg_c[...] == seg_r[...]
    lanes = grad_ref.shape[1] // 2
    groups = lanes // 64
    odd = order_ref[groups] == 1
    scale = HD ** (-0.5)

    def back(grad, raw, gain, at, g_ref, cols):
        grad = grad * cos_ref[...] + pltpu.roll(grad * sin_ref[...], HD // 2, 1)
        v = raw[:, cols]
        r = head_norm(v)
        g_ref[:, cols] = jnp.sum(grad * v * r, axis=0, keepdims=True)
        grad = grad * gain[:, cols]
        d_ref[:, at] = (
            r * grad - v * (r * r * r) * jnp.mean(grad * v, axis=-1, keepdims=True)
        ).astype(low)

    def head(h, grad):
        cols, at_k, at_v = (
            pl.ds(pl.multiple_of(h * HD + n * 2 * lanes, HD), HD) for n in range(3)
        )
        q, k = q_ref[:, cols], k_ref[:, cols]
        probs = jnp.where(same, masked_softmax(q, k, same), 0.0)
        grad_probs = dot32(grad, v_ref[:, cols], (1, 1))
        grad_scores = probs * (grad_probs - jnp.sum(grad_probs * probs, axis=-1, keepdims=True))
        grad_scores = grad_scores.astype(low)
        d_ref[:, at_v] = dot32(probs.astype(low), grad, (0, 0)).astype(low)
        back(dot32(grad_scores, k, (1, 0)) * scale, raw_q, gain_q, cols, gq_ref, cols)
        back(dot32(grad_scores, q, (0, 0)) * scale, raw_k, gain_k, at_k, gk_ref, cols)

    @pl.loop(0, groups // 2)
    def _(pair):
        cols = pl.ds(pl.multiple_of(pair * 128, 128), 128)
        first = grad_ref[:, cols].astype(wide)
        cols = pl.ds(pl.multiple_of(lanes + pair * 128, 128), 128)
        second = grad_ref[:, cols].astype(wide)
        first, second = jnp.where(odd, second, first), jnp.where(odd, first, second)
        for n in range(2):
            part = slice(64 * n, 64 * n + 64)
            grad = jnp.concatenate([first[:, part], second[:, part]], axis=1).astype(low)
            head(order_ref[2 * pair + n], grad)


def on_chip(kernel, outs, *args):
    vmem = pl.BlockSpec(memory_space=pltpu.VMEM)
    return pl.pallas_call(
        kernel,
        out_shape=outs,
        in_specs=[pl.BlockSpec(memory_space=pltpu.SMEM)] + [vmem] * (len(args) - 1),
        out_specs=[vmem] * len(outs),
        compiler_params=pltpu.CompilerParams(vmem_limit_bytes=32 * 1024 * 1024),
        cost_estimate=SMALL,
    )(*args)


def expert_kernel(experts, count, tokens, *refs):
    low, wide = jnp.bfloat16, jnp.float32
    place_ref, refs = refs[0], refs[1:]
    in_refs, refs = refs[:count], refs[count:]
    gate_refs, up_refs, down_refs, router_ref, refs = refs[:2], refs[2:4], refs[4:6], refs[6], refs[7:]
    x_ref, hid_ref, dy_ref, da_ref, du_ref, refs = *refs[:5], refs[5:]
    dh_refs, out_refs, refs = refs[:2], refs[2:4], refs[4:]
    pair = count // 2
    pick_ref, turned_ref, c_ref, a_ref, u_ref, y_ref, dx_ref = refs
    expert = place_ref[0]
    width = in_refs[0].shape[1]
    inner = hid_ref.shape[1]
    name_rows = in_refs[0].shape[0] - 2 * tokens
    tile = 256
    deep, flat = width // 4, inner // 4

    def dot(left, right, dims):
        return lax.dot_general(left, right, ((dims[:1], dims[1:]), ((), ())), preferred_element_type=wide)

    def slice_at(pos, size):
        return pl.ds(pl.multiple_of(place_ref[1 + pos] * size, size), size)

    before = lax.broadcasted_iota(jnp.int32, (tokens, tokens), 0)
    upto = lax.broadcasted_iota(jnp.int32, (tokens, tokens), 1)
    upto = jnp.where(before <= upto, 1.0, 0.0).astype(low)
    name_row = lax.broadcasted_iota(jnp.int32, (name_rows, tokens), 0)
    slot = lax.broadcasted_iota(jnp.int32, (SLOTS, tokens), 0)
    lane = lax.broadcasted_iota(jnp.int32, (SLOTS, 128), 1)
    gates = []
    for b in range(count):
        named = in_refs[b][2 * tokens :, :tokens]
        own = jnp.sum(jnp.where(name_row == expert, named.astype(wide), 0.0), axis=0, keepdims=True)
        rank = dot(jnp.broadcast_to(own, (16, tokens)).astype(low), upto, (1, 0))[:1]
        chosen = (rank.astype(jnp.int32) - 1 == slot) & (own > 0.5)
        picks = jnp.where(chosen, 1.0, 0.0)
        turned_ref[b] = picks.T.astype(low)
        picks = picks.astype(low)
        rows = pl.ds(b * SLOTS, SLOTS)
        pick_ref[b] = picks
        logits = jnp.zeros((SLOTS, 128), wide)
        for pos in range(4):
            x = dot(picks, in_refs[b][:tokens, slice_at(pos, deep)], (1, 0)).astype(low)
            x_ref[rows, pos * deep : (pos + 1) * deep] = x
            logits += dot(x, router_ref[slice_at(pos, deep), :], (1, 0))
        c_ref[rows] = dot(picks, in_refs[b][tokens : 2 * tokens], (1, 0)).astype(low)
        named = jnp.concatenate([named, jnp.zeros((128 - name_rows, tokens), low)], axis=0)
        named = dot(picks, named, (1, 1)) > 0.5
        logits = jnp.where(named, logits, -1e30)
        weights = jnp.exp(logits - jnp.max(logits, axis=1, keepdims=True))
        total = jnp.sum(weights, axis=1, keepdims=True)
        gates.append(jnp.sum(jnp.where(lane == expert, weights, 0.0), axis=1, keepdims=True) / total)
    gate = jnp.concatenate(gates, axis=0)

    @pl.loop(0, 4)
    def _(pos):
        cols = slice_at(pos, flat)
        a, u = (
            sum(
                dot(x_ref[:, h * (width // 2) : (h + 1) * (width // 2)], w_refs[h][:, cols], (1, 0))
                for h in range(2)
            )
            for w_refs in (gate_refs, up_refs)
        )
        cols = pl.ds(pl.multiple_of(pos * flat, flat), flat)
        a_ref[:, cols] = a
        u_ref[:, cols] = u
        hid_ref[:, cols] = (a / (1.0 + jnp.exp(-a)) * u).astype(low)

    def forward(j, dgate):
        cols = pl.ds(pl.multiple_of(j * tile, tile), tile)
        y = sum(
            dot(hid_ref[:, h * (inner // 2) : (h + 1) * (inner // 2)], down_refs[h][:, cols], (1, 0))
            for h in range(2)
        )
        y = y.astype(low).astype(wide)
        c = c_ref[:, cols].astype(wide)
        y_ref[...] = (gate * y).astype(low)
        dy_ref[:, cols] = (gate * c).astype(low)
        for b in range(count):
            out_refs[b // pair][b % pair, :, cols] = dot(
                turned_ref[b], y_ref[pl.ds(b * SLOTS, SLOTS)], (1, 0)
            ).astype(low)
        return dgate + jnp.sum(c * y, axis=1, keepdims=True)

    dgate = lax.fori_loop(0, width // tile, forward, jnp.zeros((count * SLOTS, 1), wide))
    for b in range(count):
        rows = dgate[b * SLOTS : (b + 1) * SLOTS]
        rows = jnp.sum(jnp.where(pick_ref[b].astype(wide) > 0.5, rows, 0.0), axis=0, keepdims=True)
        rows = jnp.where(name_row == expert, rows, 0.0)
        high = rows.astype(low)
        names = pl.ds(tokens, name_rows)
        dh_ref = dh_refs[b // pair]
        dh_ref[b % pair, names, :] = jnp.zeros((name_rows, width), low)
        dh_ref[b % pair, names, :tokens] = high
        dh_ref[b % pair, names, 2 * tokens : 3 * tokens] = (rows - high.astype(wide)).astype(low)

    for h in range(2):

        @pl.loop(0, 2)
        def _(r, h=h):
            dhid = dot(
                dy_ref[...], down_refs[h][pl.ds(pl.multiple_of(r * flat, flat), flat), :], (1, 1)
            )
            pos = 2 * h + r
            cols = pl.ds(pl.multiple_of(pos * flat, flat), flat)
            a, u = a_ref[:, cols], u_ref[:, cols]
            s = 1.0 / (1.0 + jnp.exp(-a))
            cols = slice_at(pos, flat)
            da_ref[:, cols] = (dhid * u * (s * (1.0 + a * (1.0 - s)))).astype(low)
            du_ref[:, cols] = (dhid * (a * s)).astype(low)

    for h in range(2):

        @pl.loop(0, width // (2 * tile))
        def _(i, h=h):
            rows = pl.ds(pl.multiple_of(i * tile, tile), tile)
            dx = dot(da_ref[...], gate_refs[h][rows, :], (1, 1)) + dot(
                du_ref[...], up_refs[h][rows, :], (1, 1)
            )
            dx_ref[...] = dx.astype(low)
            per = deep // tile
            start = place_ref[1 + 2 * h + i // per] * deep + (i % per) * tile
            cols = pl.ds(pl.multiple_of(start, tile), tile)
            for b in range(count):
                dh_refs[b // pair][b % pair, :tokens, cols] = dot(
                    turned_ref[b], dx_ref[pl.ds(b * SLOTS, SLOTS)], (1, 0)
                ).astype(low)


def expert_chunk(place, blocks, tokens, gate_w, up_w, down_w, router_w, experts):
    low, wide = jnp.bfloat16, jnp.float32
    count = len(blocks)
    width = blocks[0].shape[1]
    inner = gate_w[0].shape[1]
    rows = count * SLOTS
    vmem = pl.BlockSpec(memory_space=pltpu.VMEM)
    outs = [
        jax.ShapeDtypeStruct((rows, width), low),
        jax.ShapeDtypeStruct((rows, inner), low),
        jax.ShapeDtypeStruct((rows, width), low),
        jax.ShapeDtypeStruct((rows, inner), low),
        jax.ShapeDtypeStruct((rows, inner), low),
        *[jax.ShapeDtypeStruct((count // 2, blocks[0].shape[0] - tokens, width), low)] * 2,
        *[jax.ShapeDtypeStruct((count // 2, tokens, width), low)] * 2,
    ]
    return pl.pallas_call(
        functools.partial(expert_kernel, experts, count, tokens),
        out_shape=outs,
        in_specs=[pl.BlockSpec(memory_space=pltpu.SMEM)] + [vmem] * (count + 7),
        out_specs=[vmem] * len(outs),
        scratch_shapes=[
            pltpu.VMEM((count, SLOTS, tokens), low),
            pltpu.VMEM((count, tokens, SLOTS), low),
            pltpu.VMEM((rows, width), low),
            pltpu.VMEM((rows, inner), wide),
            pltpu.VMEM((rows, inner), wide),
            pltpu.VMEM((rows, 256), low),
            pltpu.VMEM((rows, 256), low),
        ],
        compiler_params=pltpu.CompilerParams(vmem_limit_bytes=58 * 1024 * 1024),
        cost_estimate=SMALL,
    )(place, *blocks, *gate_w, *up_w, *down_w, router_w)


def by_links(
    tokens,
    cotangent,
    lengths,
    routes,
    w_query,
    w_key,
    w_value,
    w_out,
    w_router,
    w_gate,
    w_up,
    w_down,
    g_attn,
    g_query,
    g_key,
    g_ffn,
):
    low, wide = jnp.bfloat16, jnp.float32
    row_count = tokens.shape[0]
    rows = w_query.shape[0]
    experts = w_router.shape[1]
    count_dp = lax.axis_size("dp")
    score_scale = HD ** (-0.5)
    d = lax.axis_index("dp")
    e = lax.axis_index("expert")
    c, x, y = e & 1, (e >> 1) & 1, e >> 2
    place = (d, c, x, y)
    own_expert = 8 * c + 4 * x + d
    at_owner = jnp.stack(
        [own_expert] + [2 * ((d + r) % 2) + (c ^ h) for h in range(2) for r in range(2)]
    ).astype(jnp.int32)
    group = jnp.arange(16, dtype=jnp.int32)
    group_order = (
        ((d - (group & 3)) % count_dp) * 4 + ((((group >> 3) & 1) ^ y) * 2 + (((group >> 2) & 1) ^ x))
    )
    order = jnp.concatenate([group_order, c[None]]).astype(jnp.int32)
    shard = jnp.arange(32, dtype=jnp.int32)
    to_whole = (
        (((shard & 1) ^ c) * 16)
        + (((shard >> 2) & 1) ^ y) * 8
        + (((shard >> 1) & 1) ^ x) * 4
        + (d - (shard >> 3)) % count_dp
    )

    slab = jnp.concatenate(
        [w_router]
        + [g[:, None] for g in (g_attn, g_query, g_key, g_ffn)]
        + [jnp.zeros((rows, 128 - experts - 4), low)],
        axis=1,
    )
    expert_ids = jnp.arange(experts, dtype=jnp.int32)
    named = jnp.any(routes[:, :, None] == expert_ids, axis=1)
    names = jnp.zeros((-(-experts // 16) * 16, D), low)
    names = lax.dynamic_update_slice(names, named.astype(low).T, (0, 0))
    sync = lax.optimization_barrier
    width = D + 128
    vo = jnp.concatenate([w_value, w_out], axis=1)
    vo_y = flip(vo, 4)
    qk = ring_gather(jnp.concatenate([w_query, slab, w_key], axis=1))
    q_a, k_b = side_by_side(qk, width)
    q_a, k_b, vo, vo_y, w_down = sync((q_a, k_b, vo, vo_y, w_down))
    vo0 = jnp.concatenate([vo, vo_y], axis=0)
    q_x, k_y, vo1 = flip(q_a, 2), flip(k_b, 4), turn(vo0, 1)
    q_a, k_b = jnp.concatenate([q_a, q_x], axis=0), jnp.concatenate([k_b, k_y], axis=0)
    q_a, k_b, vo1, w_down = sync((q_a, k_b, vo1, w_down))
    q_y, k_x, vo2 = flip(q_a, 4), flip(k_b, 2), turn(vo1, 1)
    vo3 = turn(vo2, 1)
    vo = (vo0, vo1, vo2, vo3)
    v_b, o_b = side_by_side([p[:rows] for p in vo] + [p[rows:] for p in vo], D)
    q_a, k_b = jnp.concatenate([q_a, q_y], axis=0), by_x(k_b, k_x)
    q_a, k_b, v_b, o_b, w_down = sync((q_a, k_b, v_b, o_b, w_down))
    v_x, q_other, k_other = flip(v_b, 2), flip(q_a, 1), flip(k_b, 1)
    down = to_owner(w_down, place)
    v_b, held_down = by_x(v_b, v_x), jnp.concatenate(down)
    v_b, o_b, q_other, k_other, w_gate, w_up, held_down = sync(
        (v_b, o_b, q_other, k_other, w_gate, w_up, held_down)
    )
    o_x, v_other, down_far = flip(o_b, 2), flip(v_b, 1), flip(held_down, 4)
    gate = to_owner(w_gate, place)
    o_b, held_gate = by_x(o_b, o_x), jnp.concatenate(gate)
    o_b, v_b, v_other, q_a, k_b, down_far, held_gate, w_up = sync(
        (o_b, v_b, v_other, q_a, k_b, down_far, held_gate, w_up)
    )
    gate_far, up = flip(held_gate, 4), to_owner(w_up, place)
    down_own, down_give = to_both(held_down, down_far, place)
    o_other, down_got = flip(o_b, 1), flip(down_give, 1)
    o_other, q_a, k_b, v_b = sync((o_other, q_a, k_b, v_b))
    value_w, out_w = (v_b, v_other), (o_b, o_other)
    slab = jnp.concatenate([q_a[:, D:], q_other[:, D:]], axis=0)
    slab = jnp.take(slab.reshape(32, rows, 128), to_whole, axis=0).reshape(D, 128)
    query_w, key_w = (q_a[:, :D], q_other[:, :D]), (k_b, k_other)
    router_w = slab[:, :experts]
    attn_gain, query_gain, key_gain, ffn_gain = (
        slab[:, experts + i].astype(wide) for i in range(4)
    )
    segment, offset = layout(lengths[0], row_count)
    inputs = tokens.astype(wide)
    normed_f, norm_attn_pull = jax.vjp(normalize, inputs, attn_gain)
    normed_attn = reorder(normed_f.astype(low), order, True)
    half = D // 2

    def times(left, pair):
        return jnp.dot(left[:, :half], pair[0], preferred_element_type=wide) + jnp.dot(
            left[:, half:], pair[1], preferred_element_type=wide
        )

    raw_q = times(normed_attn, query_w)
    raw_k = times(normed_attn, key_w)

    frequency = THETA ** (-jnp.arange(HD // 2, dtype=wide) / (HD // 2))
    angles = offset.astype(wide)[:, None] * frequency[None, :]
    cosine, sine = jnp.cos(angles), jnp.sin(angles)
    turns = (
        jnp.concatenate([cosine, cosine], axis=1),
        jnp.concatenate([-sine, sine], axis=1),
        segment[:, None],
        segment[None, :],
    )
    head_gains = (query_gain[None], key_gain[None])
    values = times(normed_attn, value_w).astype(low)
    like = jax.ShapeDtypeStruct((row_count, D), low)
    queries, keys_rot, context = on_chip(
        attend_kernel, [like] * 3, order, raw_q, raw_k, values, *head_gains, *turns
    )
    midway = inputs + times(context, out_w)
    normed2_f, norm_ffn_pull = jax.vjp(normalize, midway, ffn_gain)
    normed_ffn = normed2_f.astype(low)
    normed_ffn, gate_far, down_got, *up = sync((normed_ffn, gate_far, down_got, *up))
    held_up = jnp.concatenate(up)
    down_w = (down_own, down_got)

    def dense_gates(values, named_here):
        logits = jnp.dot(values, router_w, preferred_element_type=wide)
        logits = jnp.where(named_here, logits, -jnp.inf)
        exp_logits = jnp.exp(logits - jnp.max(logits, axis=-1, keepdims=True))
        return exp_logits / jnp.sum(exp_logits, axis=-1, keepdims=True)

    router_wide = jnp.pad(router_w, ((0, 0), (0, 128 - experts)))

    def chunk(piece, piece_x, piece_c, piece_xc):
        return expert_chunk(
            at_owner,
            (piece, piece_x, piece_c, piece_xc),
            row_count,
            gate_w,
            up_w,
            down_w,
            router_wide,
            experts,
        )

    def add(left, right):
        return (left.astype(wide) + right.astype(wide)).astype(low)

    def both_x(own, far):
        return add(own[0], far[0]), add(own[1], far[1])

    sent0 = jnp.concatenate([normed_ffn, cotangent, names], axis=0)
    up_far = flip(held_up, 4)
    gate_own, gate_give = to_both(held_gate, gate_far, place)
    gate_got = flip(gate_give, 1)
    sent1, sent0_x, sent0_c = turn(sent0, 1), flip(sent0, 2), flip(sent0, 1)
    sent1, sent0_x, sent0_c, up_far, gate_got = sync((sent1, sent0_x, sent0_c, up_far, gate_got))
    up_own, up_give = to_both(held_up, up_far, place)
    gate_w, up_w = (gate_own, gate_got), (up_own, flip(up_give, 1))
    sent2, sent1_x, sent1_c = turn(sent1, 1), flip(sent1, 2), flip(sent1, 1)
    outs0 = chunk(sent0, sent0_x, sent0_c, flip(sent0_x, 1))
    sent2, sent1_x, sent1_c, *outs0 = sync((sent2, sent1_x, sent1_c, *outs0))
    sent3, sent2_x, sent2_c = turn(sent2, 1), flip(sent2, 2), flip(sent2, 1)
    outs1 = chunk(sent1, sent1_x, sent1_c, flip(sent1_x, 1))
    sent3, sent2_x, sent2_c, *outs1 = sync((sent3, sent2_x, sent2_c, *outs1))
    sent3_x, sent3_c = flip(sent3, 2), flip(sent3, 1)
    outs2 = chunk(sent2, sent2_x, sent2_c, flip(sent2_x, 1))
    h1_c, m1_c = flip(outs1[6], 1), flip(outs1[8], 1)
    sent3_x, sent3_c, h1_c, m1_c, *outs2 = sync((sent3_x, sent3_c, h1_c, m1_c, *outs2))
    outs3 = chunk(sent3, sent3_x, sent3_c, flip(sent3_x, 1))
    h1, m1 = both_x(outs1[5], h1_c), both_x(outs1[7], m1_c)
    h1_x, m1_x, h2_c, m2_c = flip(h1[1], 2), flip(m1[1], 2), flip(outs2[6], 1), flip(outs2[8], 1)
    h1_x, m1_x, h2_c, m2_c, *outs3 = sync((h1_x, m1_x, h2_c, m2_c, *outs3))
    outs = (outs0, outs1, outs2, outs3)
    arrived, hidden, grad_produced, grad_gate_low, grad_up_low = ([o[i] for o in outs] for i in range(5))
    ring, h2 = add(h1[0], h1_x), both_x(outs2[5], h2_c)
    ring, *h2 = sync((ring, *h2))
    ring, h2_x = turn(ring, 1), flip(h2[1], 2)
    h3_c, h0_c, m3_c = flip(outs3[6], 1), flip(outs0[6], 1), flip(outs3[8], 1)
    h3_c, arrived, grad_gate_low = sync((h3_c, arrived, grad_gate_low))
    gate_sum = contract(arrived, grad_gate_low)
    gate_got = flip(gate_sum[D // 2 :], 1)
    ring, h2_x, h3_c, h0_c, m3_c = sync((ring, h2_x, h3_c, h0_c, m3_c))
    ring, h3 = add(add(h2[0], h2_x), ring), both_x(outs3[5], h3_c)
    ring, *h3 = sync((ring, *h3))
    ring, h3_x, m0_c = turn(ring, 1), flip(h3[1], 2), flip(outs0[8], 1)
    gate_keep, gate_give = from_owner(gate_sum[: D // 2], gate_got, place)
    gate_give, arrived, grad_up_low = sync((gate_give, arrived, grad_up_low))
    gate_far = flip(gate_give, 4)
    up_sum = contract(arrived, grad_up_low)
    up_got = flip(up_sum[D // 2 :], 1)
    m1 = add(m1[0], m1_x)
    ring, h3_x, m0_c, m1 = sync((ring, h3_x, m0_c, m1))
    ring, h0 = add(add(h3[0], h3_x), ring), both_x(outs0[5], h0_c)
    ring, *h0 = sync((ring, *h0))
    ring, h0_x, m_ring = turn(ring, 1), flip(h0[1], 2), turn(m1, 1)
    up_got, hidden, grad_produced = sync((up_got, hidden, grad_produced))
    down_sum = contract(hidden, grad_produced)
    up_keep, up_give = from_owner(up_sum[: D // 2], up_got, place)
    ms = [both_x(o[7], t) for o, t in ((outs2, m2_c), (outs3, m3_c), (outs0, m0_c))]
    m_far = jnp.concatenate([t[1] for t in ms], axis=0)
    ring, h0_x, m_ring, down_sum, up_keep, up_give, gate_far, m_far = sync(
        (ring, h0_x, m_ring, down_sum, up_keep, up_give, gate_far, m_far)
    )
    n = down_sum.shape[0] // 2
    gate_sum = sync((add(gate_keep, gate_far), m_far))[0]
    up_far, gate_back, m_x = flip(up_give, 4), to_shards(gate_sum, place), flip(m_far, 2)
    down_got = flip(down_sum[n:], 1)
    down_got, ring = sync((down_got, ring))
    back = h0[0].astype(wide) + h0_x.astype(wide) + ring.astype(wide)
    grad_normed_ffn = back[:row_count]
    grad_gates = back[row_count : row_count + experts]
    grad_gates = (grad_gates[:, :row_count] + grad_gates[:, 2 * row_count : 3 * row_count]).T

    grad_out = cotangent.astype(wide)
    gates = dense_gates(normed_ffn, named)
    grad_chosen = gates * (grad_gates - jnp.sum(gates * grad_gates, axis=1, keepdims=True))
    grad_logits = grad_chosen.astype(low)
    grad_router_local = contract_rows(grad_logits, normed_ffn)
    grad_normed_ffn = grad_normed_ffn + times_transposed(grad_logits, router_w)
    grad_midway_norm, grad_ffn_gain = norm_ffn_pull(grad_normed_ffn)
    grad_midway = grad_out + grad_midway_norm
    grad_attn = grad_midway.astype(low)

    def weight_grad(left, right):
        return contract([left[:, :half]], [right]), contract([left[:, half:]], [right])

    def times_back(left, pair):
        return jnp.concatenate(
            [times_transposed(left, pair[0]), times_transposed(left, pair[1])], axis=1
        )

    out_sums = weight_grad(context, grad_attn)
    grad_context = times_back(grad_attn, out_w).astype(low)
    grad_heads, grad_query_gain, grad_key_gain = on_chip(
        attend_back_kernel,
        [jax.ShapeDtypeStruct((row_count, 3 * D), low)] + [jax.ShapeDtypeStruct((1, D), wide)] * 2,
        order,
        grad_context,
        queries,
        keys_rot,
        values,
        raw_q,
        raw_k,
        *head_gains,
        *turns,
    )
    heads_sums = weight_grad(normed_attn, grad_heads)
    down_keep, down_give = from_owner(down_sum[:n], down_got, place)
    out_own = add(out_sums[0], flip(out_sums[1], 1))
    m_x, up_far, down_keep, down_give, out_own, heads_own, heads_other, *gate_back = sync(
        (m_x, up_far, down_keep, down_give, out_own, *heads_sums, *gate_back)
    )
    grad_gate = two_experts(gate_back, place)
    m2, m3, m0 = (
        add(t[0], m_x[k * row_count : (k + 1) * row_count]) for k, t in enumerate(ms)
    )

    def x_first(own):
        n = own.shape[0] // 4
        far = jnp.concatenate([own[n : 2 * n], own[3 * n :]], axis=0)
        return jnp.concatenate([own[:n], own[2 * n : 3 * n]], axis=0), flip(far, 2)

    def half_to(own, bit):
        n = own.shape[0] // 2
        return own[:n], flip(own[n:], bit)

    up_sum = add(up_keep, up_far)
    up_back, down_far, heads_core = to_shards(up_sum, place), flip(down_give, 4), flip(heads_other, 1)
    out_own, out_far = x_first(out_own)
    query_own, key_own, value_own = (
        add(heads_own[:, k * D : (k + 1) * D], heads_core[:, k * D : (k + 1) * D]) for k in range(3)
    )
    down_far, out_far, query_own, key_own, value_own, *up_back = sync(
        (down_far, out_far, query_own, key_own, value_own, *up_back)
    )
    grad_up = two_experts(up_back, place)
    down_sum = add(down_keep, down_far)
    query_own, query_far = half_to(query_own, 4)
    key_own, key_far = x_first(key_own)
    down_back = to_shards(down_sum, place)
    down_back[0], grad_heads = sync((down_back[0], grad_heads))
    grad_normed_attn = sum(
        times_back(grad_heads[:, k * D : (k + 1) * D], w)
        for k, w in enumerate((query_w, key_w, value_w))
    )
    grad_normed_attn = reorder(grad_normed_attn, order, False)
    grad_inputs_norm, grad_attn_gain = norm_attn_pull(grad_normed_attn)
    grad_tokens = (grad_midway + grad_inputs_norm).astype(low)
    small = jnp.concatenate(
        [grad_router_local, grad_attn_gain[None], grad_query_gain, grad_key_gain, grad_ffn_gain[None]]
        + [jnp.zeros((-(experts + 4) % 8, D), wide)],
        axis=0,
    )
    small = reorder(small, order, True)
    query_far, key_far, small, down_back[1], m_ring = sync(
        (query_far, key_far, small, down_back[1], m_ring)
    )
    grad_down = two_experts(down_back, place)

    def fold(value, bit):
        n = value.shape[1] // 2
        return value[:, :n] + flip(value[:, n:], bit)

    ring = turn(add(m2, m_ring), 1)
    ring = turn(add(m3, ring), 1)
    ko_own, ko_far = half_to(
        jnp.concatenate([add(key_own, key_far), add(out_own, out_far)], axis=1), 4
    )
    value_own, value_far = x_first(value_own)
    small = fold(fold(small, 1), 4)
    ring, ko_far, value_far, small = sync((ring, ko_far, value_far, small))
    block_out = (midway + m0.astype(wide) + ring.astype(wide)).astype(low)

    def to_owners(pieces):
        return [turn(p, -k) for k, p in enumerate(pieces) if k]

    def summed(pieces):
        return sum(p.astype(wide) for p in pieces)

    def by_steps(both):
        return [both[i * rows : (i + 1) * rows] for i in range(count_dp)]

    ko = by_steps(add(ko_own, ko_far))
    ko_far = to_owners(ko)
    query_own, query_far = half_to(add(query_own, query_far), 2)
    value_own, value_far = half_to(add(value_own, value_far), 4)
    small = fold(small, 2)
    query_far, value_far, small, *ko_far = sync((query_far, value_far, small, *ko_far))
    n = small.shape[0]
    small = small.reshape(n, count_dp, rows).transpose(1, 2, 0).reshape(count_dp * rows, n)
    small = jnp.pad(small.astype(low), ((0, 0), (0, 128 - n)))
    qv = by_steps(
        jnp.concatenate([add(query_own, query_far), add(value_own, value_far), small], axis=1)
    )
    qv_ring = summed(qv[:1] + to_owners(qv))
    ko_ring = summed(ko[:1] + ko_far)
    grad_key, grad_outproj = ko_ring[:, :D], ko_ring[:, D:]
    grad_query, grad_value = qv_ring[:, :D], qv_ring[:, D : 2 * D]
    small = qv_ring[:, 2 * D :]
    return (
        block_out,
        grad_tokens,
        grad_query,
        grad_key,
        grad_value,
        grad_outproj,
        small[:, :experts],
        grad_gate,
        grad_up,
        grad_down,
        small[:, experts],
        small[:, experts + 1],
        small[:, experts + 2],
        small[:, experts + 3],
    )


def solution(mesh):
    in_specs = (
        P(("dp", "expert"), None),
        P(("dp", "expert"), None),
        P(("dp", "expert"), None),
        P(("dp", "expert"), None),
        P(("dp", "expert"), None),
        P(("dp", "expert"), None),
        P(("dp", "expert"), None),
        P(("dp", "expert"), None),
        P(("dp", "expert"), None),
        P("expert", "dp", None),
        P("expert", "dp", None),
        P("expert", "dp", None),
        P(("dp", "expert")),
        P(("dp", "expert")),
        P(("dp", "expert")),
        P(("dp", "expert")),
    )
    out_specs = (
        P(("dp", "expert"), None),
        P(("dp", "expert"), None),
        P(("dp", "expert"), None),
        P(("dp", "expert"), None),
        P(("dp", "expert"), None),
        P(("dp", "expert"), None),
        P(("dp", "expert"), None),
        P("expert", "dp", None),
        P("expert", "dp", None),
        P("expert", "dp", None),
        P(("dp", "expert")),
        P(("dp", "expert")),
        P(("dp", "expert")),
        P(("dp", "expert")),
    )
    local = by_links if (mesh.shape["dp"], mesh.shape["expert"]) == (4, 8) else by_axes
    return jax.shard_map(local, mesh=mesh, in_specs=in_specs, out_specs=out_specs, check_vma=False)
```

```python
import functools

import jax
import jax.numpy as jnp
from jax import lax
from jax.experimental import pallas as pl
from jax.experimental.pallas import tpu as pltpu
from jax.sharding import PartitionSpec as P

D = 2048
HEADS = 16
HD = 128


EPS = 1e-05
THETA = 50000.0


def normalize(v, gain):
    return v * lax.rsqrt(jnp.mean(v * v, axis=-1, keepdims=True) + EPS) * gain


def layout(lengths_row, row_count):
    seq_ends = jnp.cumsum(lengths_row)
    position = jnp.arange(row_count, dtype=jnp.int32)
    segment = jnp.sum((position[:, None] >= seq_ends[None, :]).astype(jnp.int32), axis=1)
    seq_starts = seq_ends - lengths_row
    labels = jnp.arange(lengths_row.shape[0], dtype=jnp.int32)
    seq_start = jnp.sum(
        jnp.where(segment[:, None] == labels[None, :], seq_starts[None, :], 0), axis=1
    )
    return (segment, position - seq_start)


def rotate(v, offset):
    half_dim = v.shape[-1] // 2
    frequency = THETA ** (-jnp.arange(half_dim).astype(v.dtype) / half_dim)
    angles = offset.astype(v.dtype)[:, None] * frequency[None, :]
    cosine = jnp.cos(angles)[:, None, :]
    sine_part = jnp.sin(angles)[:, None, :]
    first_half = v[..., :half_dim]
    second_half = v[..., half_dim:]
    return jnp.concatenate(
        [
            first_half * cosine - second_half * sine_part,
            second_half * cosine + first_half * sine_part,
        ],
        axis=-1,
    )


def head_prep(raw_q, raw_k, gain_q, gain_k, offset):
    row_count = raw_q.shape[0]
    queries = rotate(
        normalize(raw_q.reshape(row_count, HEADS, HD), gain_q.reshape(HEADS, HD)), offset
    )
    keys_rot = rotate(
        normalize(raw_k.reshape(row_count, HEADS, HD), gain_k.reshape(HEADS, HD)), offset
    )
    return (queries, keys_rot)


def route_softmax(chosen):
    peak = jnp.max(chosen, axis=-1, keepdims=True)
    exp_scores = jnp.exp(chosen - peak)
    return exp_scores / jnp.sum(exp_scores, axis=-1, keepdims=True)


def swiglu(gate_act, up_act):
    return jax.nn.silu(gate_act) * up_act


def slots(flat_routes, expert_count, capacity):
    one_hot = (flat_routes[:, None] == jnp.arange(expert_count, dtype=jnp.int32)[None, :]).astype(
        jnp.int32
    )
    slot_rank = jnp.sum((jnp.cumsum(one_hot, axis=0) - one_hot) * one_hot, axis=1)
    return flat_routes * capacity + slot_rank


def contract_rows(left, right):
    return lax.dot_general(
        left, right, (((0,), (0,)), ((), ())), preferred_element_type=jnp.float32
    )


def times_transposed(left, right):
    return lax.dot_general(
        left, right, (((1,), (1,)), ((), ())), preferred_element_type=jnp.float32
    )


def by_axes(
    tokens,
    cotangent,
    lengths,
    routes,
    w_query,
    w_key,
    w_value,
    w_out,
    w_router,
    w_gate,
    w_up,
    w_down,
    g_attn,
    g_query,
    g_key,
    g_ffn,
):
    row_count = tokens.shape[0]
    top_count = routes.shape[1]
    local_experts = w_gate.shape[0]
    owners = lax.axis_size("expert")
    experts = local_experts * owners
    capacity = row_count * top_count * 5 // (4 * experts)
    score_scale = HD ** (-0.5)
    segment, offset = layout(lengths[0], row_count)
    seq_mask = (segment[:, None] == segment[None, :])[None]
    dense = (
        lax.all_gather(w_query, ("dp", "expert"), axis=0, tiled=True),
        lax.all_gather(w_key, ("dp", "expert"), axis=0, tiled=True),
        lax.all_gather(w_value, ("dp", "expert"), axis=0, tiled=True),
        lax.all_gather(w_out, ("dp", "expert"), axis=0, tiled=True),
        lax.all_gather(w_router, ("dp", "expert"), axis=0, tiled=True),
        lax.all_gather(g_attn, ("dp", "expert"), axis=0, tiled=True),
        lax.all_gather(g_query, ("dp", "expert"), axis=0, tiled=True),
        lax.all_gather(g_key, ("dp", "expert"), axis=0, tiled=True),
        lax.all_gather(g_ffn, ("dp", "expert"), axis=0, tiled=True),
    )
    query_w, key_w, value_w, out_w, router_w, attn_gain, query_gain, key_gain, ffn_gain = dense
    expert_full = (
        lax.all_gather(w_gate, "dp", axis=1, tiled=True),
        lax.all_gather(w_up, "dp", axis=1, tiled=True),
        lax.all_gather(w_down, "dp", axis=1, tiled=True),
    )
    gate_full, up_full, down_full = expert_full
    inputs = tokens.astype(jnp.float32)
    normed_f, norm_attn_pull = jax.vjp(normalize, inputs, attn_gain.astype(jnp.float32))
    normed_attn = normed_f.astype(jnp.bfloat16)
    raw_q = jnp.dot(normed_attn, query_w, preferred_element_type=jnp.float32)
    raw_k = jnp.dot(normed_attn, key_w, preferred_element_type=jnp.float32)
    values = jnp.dot(normed_attn, value_w, preferred_element_type=jnp.float32).astype(jnp.bfloat16)
    value_heads = values.reshape(row_count, HEADS, HD)

    def prep_local(first, second, first_gain, second_gain):
        return head_prep(first, second, first_gain, second_gain, offset)

    rotated, heads_pull = jax.vjp(
        prep_local, raw_q, raw_k, query_gain.astype(jnp.float32), key_gain.astype(jnp.float32)
    )
    queries = rotated[0].astype(jnp.bfloat16)
    keys_rot = rotated[1].astype(jnp.bfloat16)
    scores = (
        jnp.einsum("qhd,khd->hqk", queries, keys_rot, preferred_element_type=jnp.float32)
        * score_scale
    )
    scores = jnp.where(seq_mask, scores, -1e30)
    peak = jnp.max(scores, axis=-1, keepdims=True)
    exp_scores = jnp.exp(scores - peak)
    exp_total = jnp.sum(exp_scores, axis=-1, keepdims=True)
    log_total = peak + jnp.log(exp_total)
    probs_low = (exp_scores / exp_total).astype(jnp.bfloat16)
    context = (
        jnp.einsum("hqk,khd->qhd", probs_low, value_heads, preferred_element_type=jnp.float32)
        .astype(jnp.bfloat16)
        .reshape(row_count, D)
    )
    midway = inputs + jnp.dot(context, out_w, preferred_element_type=jnp.float32)
    normed2_f, norm_ffn_pull = jax.vjp(normalize, midway, ffn_gain.astype(jnp.float32))
    normed_ffn = normed2_f.astype(jnp.bfloat16)
    logits = jnp.dot(normed_ffn, router_w, preferred_element_type=jnp.float32)
    chosen = jnp.take_along_axis(logits, routes, axis=1)
    gates, gates_pull = jax.vjp(route_softmax, chosen)
    slot_index = slots(routes.reshape(-1), experts, capacity)
    sent_rows = (
        jnp.zeros((experts * capacity, D), jnp.bfloat16)
        .at[slot_index]
        .set(jnp.repeat(normed_ffn, top_count, axis=0))
    )
    sent_rows = sent_rows.reshape(owners, local_experts, capacity, D)
    arrived = lax.all_to_all(sent_rows, "expert", split_axis=0, concat_axis=2, tiled=True).reshape(
        local_experts, owners * capacity, D
    )
    gate_act = jnp.einsum("erd,edf->erf", arrived, gate_full, preferred_element_type=jnp.float32)
    up_act = jnp.einsum("erd,edf->erf", arrived, up_full, preferred_element_type=jnp.float32)
    hidden = swiglu(gate_act, up_act).astype(jnp.bfloat16)
    produced = jnp.einsum(
        "erf,efd->erd", hidden, down_full, preferred_element_type=jnp.float32
    ).astype(jnp.bfloat16)
    returned = lax.all_to_all(
        produced.reshape(1, local_experts, owners * capacity, D),
        "expert",
        split_axis=2,
        concat_axis=0,
        tiled=True,
    ).reshape(experts * capacity, D)
    picked = returned[slot_index].reshape(row_count, top_count, D).astype(jnp.float32)
    block_out = (midway + jnp.sum(gates[:, :, None] * picked, axis=1)).astype(jnp.bfloat16)
    grad_out = cotangent.astype(jnp.float32)
    grad_gates = jnp.sum(grad_out[:, None, :] * picked, axis=2)
    grad_picked = (
        (gates[:, :, None] * grad_out[:, None, :])
        .astype(jnp.bfloat16)
        .reshape(row_count * top_count, D)
    )
    grad_sent = jnp.zeros((experts * capacity, D), jnp.bfloat16).at[slot_index].set(grad_picked)
    grad_sent = grad_sent.reshape(owners, local_experts, capacity, D)
    grad_arrived = lax.all_to_all(
        grad_sent, "expert", split_axis=0, concat_axis=2, tiled=True
    ).reshape(local_experts, owners * capacity, D)
    gate_back, up_back, down_back = (
        lax.all_gather(w_gate, "dp", axis=1, tiled=True),
        lax.all_gather(w_up, "dp", axis=1, tiled=True),
        lax.all_gather(w_down, "dp", axis=1, tiled=True),
    )
    grad_hidden = jnp.einsum(
        "erd,efd->erf", grad_arrived, down_back, preferred_element_type=jnp.float32
    )
    grad_down_local = jnp.einsum(
        "erf,erd->efd", hidden, grad_arrived, preferred_element_type=jnp.float32
    )
    act_unused, act_pull = jax.vjp(swiglu, gate_act, up_act)
    grad_gate_act, grad_up_act = act_pull(grad_hidden)
    grad_gate_low = grad_gate_act.astype(jnp.bfloat16)
    grad_up_low = grad_up_act.astype(jnp.bfloat16)
    grad_gate_local = jnp.einsum(
        "erd,erf->edf", arrived, grad_gate_low, preferred_element_type=jnp.float32
    )
    grad_up_local = jnp.einsum(
        "erd,erf->edf", arrived, grad_up_low, preferred_element_type=jnp.float32
    )
    grad_arrival = jnp.einsum(
        "erf,edf->erd", grad_gate_low, gate_back, preferred_element_type=jnp.float32
    )
    grad_arrival = grad_arrival + jnp.einsum(
        "erf,edf->erd", grad_up_low, up_back, preferred_element_type=jnp.float32
    )
    grad_arrival = grad_arrival.astype(jnp.bfloat16).reshape(1, local_experts, owners * capacity, D)
    grad_back = lax.all_to_all(
        grad_arrival, "expert", split_axis=2, concat_axis=0, tiled=True
    ).reshape(experts * capacity, D)
    grad_normed_ffn = jnp.sum(
        grad_back[slot_index].reshape(row_count, top_count, D).astype(jnp.float32), axis=1
    )
    expert_grads = (
        lax.psum_scatter(grad_gate_local, "dp", scatter_dimension=1, tiled=True),
        lax.psum_scatter(grad_up_local, "dp", scatter_dimension=1, tiled=True),
        lax.psum_scatter(grad_down_local, "dp", scatter_dimension=1, tiled=True),
    )
    grad_chosen = gates_pull(grad_gates)[0]
    expert_ids = jnp.arange(experts, dtype=jnp.int32)
    grad_logits = jnp.sum(
        jnp.where(routes[:, :, None] == expert_ids[None, None, :], grad_chosen[:, :, None], 0.0),
        axis=1,
    ).astype(jnp.bfloat16)
    grad_router_local = contract_rows(normed_ffn, grad_logits)
    dense_back = (
        lax.all_gather(w_query, ("dp", "expert"), axis=0, tiled=True),
        lax.all_gather(w_key, ("dp", "expert"), axis=0, tiled=True),
        lax.all_gather(w_value, ("dp", "expert"), axis=0, tiled=True),
        lax.all_gather(w_out, ("dp", "expert"), axis=0, tiled=True),
        lax.all_gather(w_router, ("dp", "expert"), axis=0, tiled=True),
    )
    query_back, key_back, value_back, out_back, router_back = dense_back
    grad_normed_ffn = grad_normed_ffn + times_transposed(grad_logits, router_back)
    grad_midway_norm, grad_ffn_gain = norm_ffn_pull(grad_normed_ffn)
    grad_midway = grad_out + grad_midway_norm
    grad_attn = grad_midway.astype(jnp.bfloat16)
    grad_out_local = contract_rows(context, grad_attn)
    grad_context = (
        times_transposed(grad_attn, out_back).astype(jnp.bfloat16).reshape(row_count, HEADS, HD)
    )
    probs = jnp.where(seq_mask, jnp.exp(scores - log_total), 0.0)
    grad_probs = jnp.einsum(
        "qhd,khd->hqk", grad_context, value_heads, preferred_element_type=jnp.float32
    )
    grad_scores = (
        probs * (grad_probs - jnp.sum(grad_probs * probs, axis=-1, keepdims=True))
    ).astype(jnp.bfloat16)
    grad_values = (
        jnp.einsum("hqk,qhd->khd", probs_low, grad_context, preferred_element_type=jnp.float32)
        .astype(jnp.bfloat16)
        .reshape(row_count, D)
    )
    grad_queries = (
        jnp.einsum("hqk,khd->qhd", grad_scores, keys_rot, preferred_element_type=jnp.float32)
        * score_scale
    )
    grad_keys = (
        jnp.einsum("hqk,qhd->khd", grad_scores, queries, preferred_element_type=jnp.float32)
        * score_scale
    )
    grad_raw_q, grad_raw_k, grad_query_gain, grad_key_gain = heads_pull((grad_queries, grad_keys))
    grad_raw_q = grad_raw_q.astype(jnp.bfloat16)
    grad_raw_k = grad_raw_k.astype(jnp.bfloat16)
    grad_query_local = contract_rows(normed_attn, grad_raw_q)
    grad_key_local = contract_rows(normed_attn, grad_raw_k)
    grad_value_local = contract_rows(normed_attn, grad_values)
    grad_normed_attn = (
        times_transposed(grad_raw_q, query_back)
        + times_transposed(grad_raw_k, key_back)
        + times_transposed(grad_values, value_back)
    )
    grad_inputs_norm, grad_attn_gain = norm_attn_pull(grad_normed_attn)
    grad_tokens = (grad_midway + grad_inputs_norm).astype(jnp.bfloat16)
    dense_grads = (
        lax.psum_scatter(grad_query_local, ("dp", "expert"), scatter_dimension=0, tiled=True),
        lax.psum_scatter(grad_key_local, ("dp", "expert"), scatter_dimension=0, tiled=True),
        lax.psum_scatter(grad_value_local, ("dp", "expert"), scatter_dimension=0, tiled=True),
        lax.psum_scatter(grad_out_local, ("dp", "expert"), scatter_dimension=0, tiled=True),
        lax.psum_scatter(grad_router_local, ("dp", "expert"), scatter_dimension=0, tiled=True),
        lax.psum_scatter(grad_attn_gain, ("dp", "expert"), scatter_dimension=0, tiled=True),
        lax.psum_scatter(grad_query_gain, ("dp", "expert"), scatter_dimension=0, tiled=True),
        lax.psum_scatter(grad_key_gain, ("dp", "expert"), scatter_dimension=0, tiled=True),
        lax.psum_scatter(grad_ffn_gain, ("dp", "expert"), scatter_dimension=0, tiled=True),
    )
    return (
        block_out,
        grad_tokens,
        dense_grads[0],
        dense_grads[1],
        dense_grads[2],
        dense_grads[3],
        dense_grads[4],
        expert_grads[0],
        expert_grads[1],
        expert_grads[2],
        dense_grads[5],
        dense_grads[6],
        dense_grads[7],
        dense_grads[8],
    )


SLOTS = 128
SMALL = pl.CostEstimate(flops=1, bytes_accessed=1, transcendentals=0)


def flip(value, bit):
    count = lax.axis_size("expert")
    return lax.ppermute(value, "expert", [(i, i ^ bit) for i in range(count)])


def turn(value, step):
    count = lax.axis_size("dp")
    return lax.ppermute(value, "dp", [(i, (i + step) % count) for i in range(count)])


def order_kernel(to_own, order_ref, v_ref, o_ref):
    half = 64
    lanes = v_ref.shape[1] // 2
    groups = v_ref.shape[1] // 128
    odd = order_ref[groups] == 1
    for pair in range(groups // 2):
        first = pl.ds(pl.multiple_of(order_ref[2 * pair] * 128, 128), 128)
        second = pl.ds(pl.multiple_of(order_ref[2 * pair + 1] * 128, 128), 128)
        if to_own:
            a = v_ref[:, first].astype(jnp.float32)
            b = v_ref[:, second].astype(jnp.float32)
            low = jnp.concatenate([a[:, :half], b[:, :half]], axis=1)
            high = jnp.concatenate([a[:, half:], b[:, half:]], axis=1)
            o_ref[:, pair * 128 : pair * 128 + 128] = jnp.where(odd, high, low).astype(o_ref.dtype)
            o_ref[:, lanes + pair * 128 : lanes + pair * 128 + 128] = jnp.where(
                odd, low, high
            ).astype(o_ref.dtype)
        else:
            low = v_ref[:, pair * 128 : pair * 128 + 128].astype(jnp.float32)
            high = v_ref[:, lanes + pair * 128 : lanes + pair * 128 + 128].astype(jnp.float32)
            low, high = jnp.where(odd, high, low), jnp.where(odd, low, high)
            o_ref[:, first] = jnp.concatenate([low[:, :half], high[:, :half]], axis=1).astype(
                o_ref.dtype
            )
            o_ref[:, second] = jnp.concatenate([low[:, half:], high[:, half:]], axis=1).astype(
                o_ref.dtype
            )


def reorder(value, order, to_own):
    return pl.pallas_call(
        functools.partial(order_kernel, to_own),
        out_shape=jax.ShapeDtypeStruct(value.shape, value.dtype),
        in_specs=[
            pl.BlockSpec(memory_space=pltpu.SMEM),
            pl.BlockSpec(memory_space=pltpu.VMEM),
        ],
        out_specs=pl.BlockSpec(memory_space=pltpu.VMEM),
        compiler_params=pltpu.CompilerParams(vmem_limit_bytes=16 * 1024 * 1024),
        cost_estimate=pl.CostEstimate(flops=0, bytes_accessed=4 * value.size, transcendentals=0),
    )(order, value)


def ring_gather(value):
    pieces = [value]
    for _ in range(lax.axis_size("dp") - 1):
        pieces.append(turn(pieces[-1], 1))
    return pieces


def ring_scatter(pieces):
    total = pieces[-1]
    for piece in pieces[-2::-1]:
        total = turn(total, -1).astype(jnp.float32) + piece.astype(jnp.float32)
        if piece is not pieces[0]:
            total = total.astype(piece.dtype)
    return total


def side_by_side(pieces, width):
    return (
        jnp.concatenate([p[:, :width] for p in pieces], axis=0),
        jnp.concatenate([p[:, width:] for p in pieces], axis=0),
    )


def by_x(own, far):
    n = own.shape[0] // 2
    return jnp.concatenate([own[:n], far[:n], own[n:], far[n:]], axis=0)


def ring_scatter_up(pieces):
    low, wide = pieces[0].dtype, jnp.float32
    total = pieces[1]
    for piece in pieces[2:]:
        total = (turn(total, 1).astype(wide) + piece.astype(wide)).astype(low)
    return turn(total, 1).astype(wide) + pieces[0].astype(wide)


def expert_rounds(count_dp, count_expert):
    rounds = []
    for r in range(2):
        pairs = []
        for d in range(count_dp):
            for e in range(count_expert):
                goal = 2 * (e & 1) + (d // 2 + r) % 2
                pairs.append((d * count_expert + e, goal * count_expert + (e & ~1) + d % 2))
        rounds.append(pairs)
    return rounds


def owner_pieces(weight, place):
    d, c, x, y = place
    return [lax.dynamic_index_in_dim(weight, (d // 2 + r) % 2, 0, keepdims=False) for r in range(2)]


def to_owner(pieces):
    rounds = expert_rounds(lax.axis_size("dp"), lax.axis_size("expert"))
    return [lax.ppermute(p, ("dp", "expert"), pairs) for p, pairs in zip(pieces, rounds)]


def to_both(held, far, place):
    d, c, x, y = place
    return jnp.where(y == c, held, far), jnp.where(y == c, far, held)


def from_owner(keep, got, place):
    d, c, x, y = place
    return jnp.where(y == c, keep, got), jnp.where(y == c, got, keep)


def to_shards(parts):
    rounds = expert_rounds(lax.axis_size("dp"), lax.axis_size("expert"))
    return [
        lax.ppermute(part, ("dp", "expert"), [(b, a) for a, b in pairs])
        for part, pairs in zip(parts, rounds)
    ]


def two_experts(pieces, place):
    d, c, x, y = place
    first, second = (p.astype(jnp.float32) for p in pieces)
    own = d // 2 == 0
    return jnp.stack([jnp.where(own, first, second), jnp.where(own, second, first)])


def contract_kernel(count, *refs):
    out_ref = refs[-1]
    out_ref[...] = sum(
        lax.dot_general(
            left_ref[...],
            right_ref[...],
            (((0,), (0,)), ((), ())),
            preferred_element_type=jnp.float32,
        )
        for left_ref, right_ref in zip(refs[:count], refs[count : 2 * count])
    ).astype(out_ref.dtype)


def contract(lefts, rights, low=jnp.bfloat16):
    depth, width = lefts[0].shape
    across = rights[0].shape[1]
    block = 512
    return pl.pallas_call(
        functools.partial(contract_kernel, len(lefts)),
        grid=(width // block,),
        in_specs=[pl.BlockSpec((depth, block), lambda i: (0, i))] * len(lefts)
        + [pl.BlockSpec((depth, across), lambda i: (0, 0))] * len(rights),
        out_specs=pl.BlockSpec((block, across), lambda i: (i, 0)),
        out_shape=jax.ShapeDtypeStruct((width, across), low),
        compiler_params=pltpu.CompilerParams(vmem_limit_bytes=48 * 1024 * 1024),
        cost_estimate=SMALL,
    )(*lefts, *rights)


def add_contract_kernel(firsts, left_ref, right_ref, got_ref, *out_refs):
    step = pl.program_id(0)
    width = out_refs[0].shape[1]
    total = lax.dot_general(
        left_ref[...], right_ref[...], (((0,), (0,)), ((), ())), preferred_element_type=jnp.float32
    )
    total = (total + got_ref[...].astype(jnp.float32)).astype(got_ref.dtype)
    for n, first in enumerate(firsts):
        far = step >= 2 if first == "y" else step % 2 == 1
        part = total[:, n * width : (n + 1) * width]

        @pl.when(jnp.logical_not(far))
        def _(n=n, part=part):
            out_refs[2 * n][...] = part

        @pl.when(far)
        def _(n=n, part=part):
            out_refs[2 * n + 1][...] = part


def add_contract(left, right, got, firsts):
    depth, rows = left.shape
    block = rows // 4
    width = right.shape[1] // len(firsts)
    outs, specs = [], []
    for first in firsts:
        if first == "y":
            maps = (lambda i: (jnp.minimum(i, 1), 0)), (lambda i: (jnp.maximum(i - 2, 0), 0))
        else:
            maps = (lambda i: (i // 2, 0)), (lambda i: (i // 2, 0))
        outs += [jax.ShapeDtypeStruct((2 * block, width), got.dtype)] * 2
        specs += [pl.BlockSpec((block, width), index_map) for index_map in maps]
    return pl.pallas_call(
        functools.partial(add_contract_kernel, firsts),
        grid=(4,),
        in_specs=[
            pl.BlockSpec((depth, block), lambda i: (0, i)),
            pl.BlockSpec((depth, right.shape[1]), lambda i: (0, 0)),
            pl.BlockSpec((block, right.shape[1]), lambda i: (i, 0)),
        ],
        out_specs=specs,
        out_shape=outs,
        compiler_params=pltpu.CompilerParams(vmem_limit_bytes=48 * 1024 * 1024),
        cost_estimate=SMALL,
    )(left, right, got)


def head_norm(v):
    return lax.rsqrt(jnp.mean(v * v, axis=-1, keepdims=True) + EPS)


def dot32(left, right, dims):
    return lax.dot_general(
        left, right, ((dims[:1], dims[1:]), ((), ())), preferred_element_type=jnp.float32
    )


def masked_softmax(q, k, same):
    scores = jnp.where(same, dot32(q, k, (1, 1)) * HD ** (-0.5), -1e30)
    weights = jnp.exp(scores - jnp.max(scores, axis=-1, keepdims=True))
    return weights / jnp.sum(weights, axis=-1, keepdims=True)


def attend_kernel(
    order_ref, raw_q, raw_k, v_ref, gain_q, gain_k, cos_ref, sin_ref, seg_c, seg_r, q_ref, k_ref, o_ref
):
    low = jnp.bfloat16
    same = seg_c[...] == seg_r[...]
    lanes = o_ref.shape[1] // 2
    groups = lanes // 64
    odd = order_ref[groups] == 1

    def head(h):
        cols = pl.ds(pl.multiple_of(h * HD, HD), HD)

        def prepared(raw, gain):
            v = raw[:, cols]
            v = v * head_norm(v) * gain[:, cols]
            return (v * cos_ref[...] + pltpu.roll(v, HD // 2, 1) * sin_ref[...]).astype(low)

        q, k = prepared(raw_q, gain_q), prepared(raw_k, gain_k)
        q_ref[:, cols], k_ref[:, cols] = q, k
        probs = masked_softmax(q, k, same).astype(low)
        return dot32(probs, v_ref[:, cols], (1, 0))

    @pl.loop(0, groups // 2)
    def _(pair):
        a, b = head(order_ref[2 * pair]), head(order_ref[2 * pair + 1])
        first = jnp.concatenate([a[:, :64], b[:, :64]], axis=1)
        second = jnp.concatenate([a[:, 64:], b[:, 64:]], axis=1)
        cols = pl.ds(pl.multiple_of(pair * 128, 128), 128)
        o_ref[:, cols] = jnp.where(odd, second, first).astype(low)
        cols = pl.ds(pl.multiple_of(lanes + pair * 128, 128), 128)
        o_ref[:, cols] = jnp.where(odd, first, second).astype(low)


def attend_back_kernel(
    order_ref,
    grad_ref,
    q_ref,
    k_ref,
    v_ref,
    raw_q,
    raw_k,
    gain_q,
    gain_k,
    cos_ref,
    sin_ref,
    seg_c,
    seg_r,
    d_ref,
    gq_ref,
    gk_ref,
):
    low, wide = jnp.bfloat16, jnp.float32
    same = seg_c[...] == seg_r[...]
    lanes = grad_ref.shape[1] // 2
    groups = lanes // 64
    odd = order_ref[groups] == 1
    scale = HD ** (-0.5)

    def back(grad, raw, gain, at, g_ref, cols):
        grad = grad * cos_ref[...] + pltpu.roll(grad * sin_ref[...], HD // 2, 1)
        v = raw[:, cols]
        r = head_norm(v)
        g_ref[:, cols] = jnp.sum(grad * v * r, axis=0, keepdims=True)
        grad = grad * gain[:, cols]
        d_ref[:, at] = (
            r * grad - v * (r * r * r) * jnp.mean(grad * v, axis=-1, keepdims=True)
        ).astype(low)

    def head(h, grad):
        cols, at_k, at_v = (
            pl.ds(pl.multiple_of(h * HD + n * 2 * lanes, HD), HD) for n in range(3)
        )
        q, k = q_ref[:, cols], k_ref[:, cols]
        probs = jnp.where(same, masked_softmax(q, k, same), 0.0)
        grad_probs = dot32(grad, v_ref[:, cols], (1, 1))
        grad_scores = probs * (grad_probs - jnp.sum(grad_probs * probs, axis=-1, keepdims=True))
        grad_scores = grad_scores.astype(low)
        d_ref[:, at_v] = dot32(probs.astype(low), grad, (0, 0)).astype(low)
        back(dot32(grad_scores, k, (1, 0)) * scale, raw_q, gain_q, cols, gq_ref, cols)
        back(dot32(grad_scores, q, (0, 0)) * scale, raw_k, gain_k, at_k, gk_ref, cols)

    @pl.loop(0, groups // 2)
    def _(pair):
        cols = pl.ds(pl.multiple_of(pair * 128, 128), 128)
        first = grad_ref[:, cols].astype(wide)
        cols = pl.ds(pl.multiple_of(lanes + pair * 128, 128), 128)
        second = grad_ref[:, cols].astype(wide)
        first, second = jnp.where(odd, second, first), jnp.where(odd, first, second)
        for n in range(2):
            part = slice(64 * n, 64 * n + 64)
            grad = jnp.concatenate([first[:, part], second[:, part]], axis=1).astype(low)
            head(order_ref[2 * pair + n], grad)


def on_chip(kernel, outs, *args):
    vmem = pl.BlockSpec(memory_space=pltpu.VMEM)
    return pl.pallas_call(
        kernel,
        out_shape=outs,
        in_specs=[pl.BlockSpec(memory_space=pltpu.SMEM)] + [vmem] * (len(args) - 1),
        out_specs=[vmem] * len(outs),
        compiler_params=pltpu.CompilerParams(vmem_limit_bytes=32 * 1024 * 1024),
        cost_estimate=SMALL,
    )(*args)


def expert_kernel(experts, count, tokens, *refs):
    low, wide = jnp.bfloat16, jnp.float32
    place_ref, refs = refs[0], refs[1:]
    in_refs, refs = refs[:count], refs[count:]
    gate_refs, up_refs, down_refs, router_ref, refs = refs[:2], refs[2:4], refs[4:6], refs[6], refs[7:]
    x_ref, hid_ref, dy_ref, da_ref, du_ref, refs = *refs[:5], refs[5:]
    dh_refs, out_refs, refs = refs[:2], refs[2:4], refs[4:]
    pair = count // 2
    pick_ref, turned_ref, c_ref, a_ref, u_ref, y_ref, dx_ref = refs
    expert = place_ref[0]
    width = in_refs[0].shape[1]
    inner = hid_ref.shape[1]
    name_rows = in_refs[0].shape[0] - 2 * tokens
    tile = 256
    deep, flat = width // 4, inner // 4

    def dot(left, right, dims):
        return lax.dot_general(left, right, ((dims[:1], dims[1:]), ((), ())), preferred_element_type=wide)

    def slice_at(pos, size):
        return pl.ds(pl.multiple_of(place_ref[1 + pos] * size, size), size)

    before = lax.broadcasted_iota(jnp.int32, (tokens, tokens), 0)
    upto = lax.broadcasted_iota(jnp.int32, (tokens, tokens), 1)
    upto = jnp.where(before <= upto, 1.0, 0.0).astype(low)
    name_row = lax.broadcasted_iota(jnp.int32, (name_rows, tokens), 0)
    slot = lax.broadcasted_iota(jnp.int32, (SLOTS, tokens), 0)
    lane = lax.broadcasted_iota(jnp.int32, (SLOTS, 128), 1)
    gates = []
    for b in range(count):
        named = in_refs[b][2 * tokens :, :tokens]
        own = jnp.sum(jnp.where(name_row == expert, named.astype(wide), 0.0), axis=0, keepdims=True)
        rank = dot(jnp.broadcast_to(own, (16, tokens)).astype(low), upto, (1, 0))[:1]
        chosen = (rank.astype(jnp.int32) - 1 == slot) & (own > 0.5)
        picks = jnp.where(chosen, 1.0, 0.0)
        turned_ref[b] = picks.T.astype(low)
        picks = picks.astype(low)
        rows = pl.ds(b * SLOTS, SLOTS)
        pick_ref[b] = picks
        logits = jnp.zeros((SLOTS, 128), wide)
        for pos in range(4):
            x = dot(picks, in_refs[b][:tokens, slice_at(pos, deep)], (1, 0)).astype(low)
            x_ref[rows, pos * deep : (pos + 1) * deep] = x
            logits += dot(x, router_ref[slice_at(pos, deep), :], (1, 0))
        c_ref[rows] = dot(picks, in_refs[b][tokens : 2 * tokens], (1, 0)).astype(low)
        named = jnp.concatenate([named, jnp.zeros((128 - name_rows, tokens), low)], axis=0)
        named = dot(picks, named, (1, 1)) > 0.5
        logits = jnp.where(named, logits, -1e30)
        weights = jnp.exp(logits - jnp.max(logits, axis=1, keepdims=True))
        total = jnp.sum(weights, axis=1, keepdims=True)
        gates.append(jnp.sum(jnp.where(lane == expert, weights, 0.0), axis=1, keepdims=True) / total)
    gate = jnp.concatenate(gates, axis=0)

    @pl.loop(0, 4)
    def _(pos):
        cols = slice_at(pos, flat)
        a, u = (
            sum(
                dot(x_ref[:, h * (width // 2) : (h + 1) * (width // 2)], w_refs[h][:, cols], (1, 0))
                for h in range(2)
            )
            for w_refs in (gate_refs, up_refs)
        )
        cols = pl.ds(pl.multiple_of(pos * flat, flat), flat)
        a_ref[:, cols] = a
        u_ref[:, cols] = u
        hid_ref[:, cols] = (a / (1.0 + jnp.exp(-a)) * u).astype(low)

    def forward(j, dgate):
        cols = pl.ds(pl.multiple_of(j * tile, tile), tile)
        y = sum(
            dot(hid_ref[:, h * (inner // 2) : (h + 1) * (inner // 2)], down_refs[h][:, cols], (1, 0))
            for h in range(2)
        )
        y = y.astype(low).astype(wide)
        c = c_ref[:, cols].astype(wide)
        y_ref[...] = (gate * y).astype(low)
        dy_ref[:, cols] = (gate * c).astype(low)
        for b in range(count):
            out_refs[b // pair][b % pair, :, cols] = dot(
                turned_ref[b], y_ref[pl.ds(b * SLOTS, SLOTS)], (1, 0)
            ).astype(low)
        return dgate + jnp.sum(c * y, axis=1, keepdims=True)

    dgate = lax.fori_loop(0, width // tile, forward, jnp.zeros((count * SLOTS, 1), wide))
    for b in range(count):
        rows = dgate[b * SLOTS : (b + 1) * SLOTS]
        rows = jnp.sum(jnp.where(pick_ref[b].astype(wide) > 0.5, rows, 0.0), axis=0, keepdims=True)
        rows = jnp.where(name_row == expert, rows, 0.0)
        high = rows.astype(low)
        names = pl.ds(tokens, name_rows)
        dh_ref = dh_refs[b // pair]
        dh_ref[b % pair, names, :] = jnp.zeros((name_rows, width), low)
        dh_ref[b % pair, names, :tokens] = high
        dh_ref[b % pair, names, 2 * tokens : 3 * tokens] = (rows - high.astype(wide)).astype(low)

    for h in range(2):

        @pl.loop(0, 2)
        def _(r, h=h):
            dhid = dot(
                dy_ref[...], down_refs[h][pl.ds(pl.multiple_of(r * flat, flat), flat), :], (1, 1)
            )
            pos = 2 * h + r
            cols = pl.ds(pl.multiple_of(pos * flat, flat), flat)
            a, u = a_ref[:, cols], u_ref[:, cols]
            s = 1.0 / (1.0 + jnp.exp(-a))
            cols = slice_at(pos, flat)
            da_ref[:, cols] = (dhid * u * (s * (1.0 + a * (1.0 - s)))).astype(low)
            du_ref[:, cols] = (dhid * (a * s)).astype(low)

    for h in range(2):

        @pl.loop(0, width // (2 * tile))
        def _(i, h=h):
            rows = pl.ds(pl.multiple_of(i * tile, tile), tile)
            dx = dot(da_ref[...], gate_refs[h][rows, :], (1, 1)) + dot(
                du_ref[...], up_refs[h][rows, :], (1, 1)
            )
            dx_ref[...] = dx.astype(low)
            per = deep // tile
            start = place_ref[1 + 2 * h + i // per] * deep + (i % per) * tile
            cols = pl.ds(pl.multiple_of(start, tile), tile)
            for b in range(count):
                dh_refs[b // pair][b % pair, :tokens, cols] = dot(
                    turned_ref[b], dx_ref[pl.ds(b * SLOTS, SLOTS)], (1, 0)
                ).astype(low)


def expert_chunk(place, blocks, tokens, gate_w, up_w, down_w, router_w, experts):
    low, wide = jnp.bfloat16, jnp.float32
    count = len(blocks)
    width = blocks[0].shape[1]
    inner = gate_w[0].shape[1]
    rows = count * SLOTS
    vmem = pl.BlockSpec(memory_space=pltpu.VMEM)
    outs = [
        jax.ShapeDtypeStruct((rows, width), low),
        jax.ShapeDtypeStruct((rows, inner), low),
        jax.ShapeDtypeStruct((rows, width), low),
        jax.ShapeDtypeStruct((rows, inner), low),
        jax.ShapeDtypeStruct((rows, inner), low),
        *[jax.ShapeDtypeStruct((count // 2, blocks[0].shape[0] - tokens, width), low)] * 2,
        *[jax.ShapeDtypeStruct((count // 2, tokens, width), low)] * 2,
    ]
    return pl.pallas_call(
        functools.partial(expert_kernel, experts, count, tokens),
        out_shape=outs,
        in_specs=[pl.BlockSpec(memory_space=pltpu.SMEM)] + [vmem] * (count + 7),
        out_specs=[vmem] * len(outs),
        scratch_shapes=[
            pltpu.VMEM((count, SLOTS, tokens), low),
            pltpu.VMEM((count, tokens, SLOTS), low),
            pltpu.VMEM((rows, width), low),
            pltpu.VMEM((rows, inner), wide),
            pltpu.VMEM((rows, inner), wide),
            pltpu.VMEM((rows, 256), low),
            pltpu.VMEM((rows, 256), low),
        ],
        compiler_params=pltpu.CompilerParams(vmem_limit_bytes=58 * 1024 * 1024),
        cost_estimate=SMALL,
    )(place, *blocks, *gate_w, *up_w, *down_w, router_w)


def by_links(
    tokens,
    cotangent,
    lengths,
    routes,
    w_query,
    w_key,
    w_value,
    w_out,
    w_router,
    w_gate,
    w_up,
    w_down,
    g_attn,
    g_query,
    g_key,
    g_ffn,
):
    low, wide = jnp.bfloat16, jnp.float32
    row_count = tokens.shape[0]
    rows = w_query.shape[0]
    experts = w_router.shape[1]
    count_dp = lax.axis_size("dp")
    score_scale = HD ** (-0.5)
    d = lax.axis_index("dp")
    e = lax.axis_index("expert")
    c, x, y = e & 1, (e >> 1) & 1, e >> 2
    place = (d, c, x, y)
    own_expert = 8 * c + 4 * x + d
    at_owner = jnp.stack(
        [own_expert] + [2 * ((d + r) % 2) + (c ^ h) for h in range(2) for r in range(2)]
    ).astype(jnp.int32)
    group = jnp.arange(16, dtype=jnp.int32)
    group_order = (
        ((d - (group & 3)) % count_dp) * 4 + ((((group >> 3) & 1) ^ y) * 2 + (((group >> 2) & 1) ^ x))
    )
    order = jnp.concatenate([group_order, c[None]]).astype(jnp.int32)
    shard = jnp.arange(32, dtype=jnp.int32)
    to_whole = (
        (((shard & 1) ^ c) * 16)
        + (((shard >> 2) & 1) ^ y) * 8
        + (((shard >> 1) & 1) ^ x) * 4
        + (d - (shard >> 3)) % count_dp
    )

    slab = jnp.concatenate(
        [w_router]
        + [g[:, None] for g in (g_attn, g_query, g_key, g_ffn)]
        + [jnp.zeros((rows, 128 - experts - 4), low)],
        axis=1,
    )
    expert_ids = jnp.arange(experts, dtype=jnp.int32)
    named = jnp.any(routes[:, :, None] == expert_ids, axis=1)
    names = jnp.zeros((-(-experts // 16) * 16, D), low)
    names = lax.dynamic_update_slice(names, named.astype(low).T, (0, 0))
    sync = lax.optimization_barrier
    width = D + 128
    vo = jnp.concatenate([w_value, w_out], axis=1)
    vo_y = flip(vo, 4)
    qk = ring_gather(jnp.concatenate([w_query, slab, w_key], axis=1))
    q_a, k_b = side_by_side(qk, width)
    q_a, k_b, vo, vo_y, w_down = sync((q_a, k_b, vo, vo_y, w_down))
    vo0 = jnp.concatenate([vo, vo_y], axis=0)
    q_x, k_y, vo1 = flip(q_a, 2), flip(k_b, 4), turn(vo0, 1)
    q_a, k_b = jnp.concatenate([q_a, q_x], axis=0), jnp.concatenate([k_b, k_y], axis=0)
    q_a, k_b, vo1, w_down = sync((q_a, k_b, vo1, w_down))
    q_y, k_x, vo2 = flip(q_a, 4), flip(k_b, 2), turn(vo1, 1)
    vo3 = turn(vo2, 1)
    vo = (vo0, vo1, vo2, vo3)
    v_b, o_b = side_by_side([p[:rows] for p in vo] + [p[rows:] for p in vo], D)
    q_a, k_b = jnp.concatenate([q_a, q_y], axis=0), by_x(k_b, k_x)
    q_a, k_b, v_b, o_b, *down = sync((q_a, k_b, v_b, o_b, *owner_pieces(w_down, place)))
    v_x, q_other, k_other = flip(v_b, 2), flip(q_a, 1), flip(k_b, 1)
    v_b, held_down = by_x(v_b, v_x), jnp.concatenate(to_owner(down))
    v_b, o_b, q_other, k_other, held_down, *gate = sync(
        (v_b, o_b, q_other, k_other, held_down, *owner_pieces(w_gate, place))
    )
    o_x, v_other, down_far = flip(o_b, 2), flip(v_b, 1), flip(held_down, 4)
    gate = to_owner(gate)
    v_other, q_a, q_other, k_b, k_other, v_b = sync((v_other, q_a, q_other, k_b, k_other, v_b))
    value_w = (v_b, v_other)
    slab = jnp.concatenate([q_a[:, D:], q_other[:, D:]], axis=0)
    slab = jnp.take(slab.reshape(32, rows, 128), to_whole, axis=0).reshape(D, 128)
    query_w, key_w = (q_a[:, :D], q_other[:, :D]), (k_b, k_other)
    router_w = slab[:, :experts]
    attn_gain, query_gain, key_gain, ffn_gain = (
        slab[:, experts + i].astype(wide) for i in range(4)
    )
    segment, offset = layout(lengths[0], row_count)
    inputs = tokens.astype(wide)
    normed_f, norm_attn_pull = jax.vjp(normalize, inputs, attn_gain)
    normed_attn = reorder(normed_f.astype(low), order, True)
    half = D // 2

    def times(left, pair):
        return jnp.dot(left[:, :half], pair[0], preferred_element_type=wide) + jnp.dot(
            left[:, half:], pair[1], preferred_element_type=wide
        )

    raw_q = times(normed_attn, query_w)
    raw_k = times(normed_attn, key_w)

    frequency = THETA ** (-jnp.arange(HD // 2, dtype=wide) / (HD // 2))
    angles = offset.astype(wide)[:, None] * frequency[None, :]
    cosine, sine = jnp.cos(angles), jnp.sin(angles)
    turns = (
        jnp.concatenate([cosine, cosine], axis=1),
        jnp.concatenate([-sine, sine], axis=1),
        segment[:, None],
        segment[None, :],
    )
    head_gains = (query_gain[None], key_gain[None])
    values = times(normed_attn, value_w).astype(low)
    raw_q, raw_k, values, o_x, down_far, *gate = sync((raw_q, raw_k, values, o_x, down_far, *gate))
    o_b, held_gate = by_x(o_b, o_x), jnp.concatenate(gate)
    down_own, down_give = to_both(held_down, down_far, place)
    o_b, held_gate, down_give, raw_q, raw_k, values, *up = sync(
        (o_b, held_gate, down_give, raw_q, raw_k, values, *owner_pieces(w_up, place))
    )
    gate_far, up = flip(held_gate, 4), to_owner(up)
    o_other, down_got = flip(o_b, 1), flip(down_give, 1)
    o_other, raw_q, raw_k, values = sync((o_other, raw_q, raw_k, values))
    out_w = (o_b, o_other)
    like = jax.ShapeDtypeStruct((row_count, D), low)
    queries, keys_rot, context = on_chip(
        attend_kernel, [like] * 3, order, raw_q, raw_k, values, *head_gains, *turns
    )
    midway = inputs + times(context, out_w)
    normed2_f, norm_ffn_pull = jax.vjp(normalize, midway, ffn_gain)
    normed_ffn = normed2_f.astype(low)
    normed_ffn, gate_far, down_got, *up = sync((normed_ffn, gate_far, down_got, *up))
    held_up = jnp.concatenate(up)
    down_w = (down_own, down_got)

    def dense_gates(values, named_here):
        logits = jnp.dot(values, router_w, preferred_element_type=wide)
        logits = jnp.where(named_here, logits, -jnp.inf)
        exp_logits = jnp.exp(logits - jnp.max(logits, axis=-1, keepdims=True))
        return exp_logits / jnp.sum(exp_logits, axis=-1, keepdims=True)

    router_wide = jnp.pad(router_w, ((0, 0), (0, 128 - experts)))

    def chunk(piece, piece_x, piece_c, piece_xc):
        return expert_chunk(
            at_owner,
            (piece, piece_x, piece_c, piece_xc),
            row_count,
            gate_w,
            up_w,
            down_w,
            router_wide,
            experts,
        )

    def add(left, right):
        return (left.astype(wide) + right.astype(wide)).astype(low)

    def both_x(own, far):
        return add(own[0], far[0]), add(own[1], far[1])

    sent0 = jnp.concatenate([normed_ffn, cotangent, names], axis=0)
    up_far = flip(held_up, 4)
    gate_own, gate_give = to_both(held_gate, gate_far, place)
    gate_got = flip(gate_give, 1)
    sent1, sent0_x, sent0_c = turn(sent0, 1), flip(sent0, 2), flip(sent0, 1)
    sent1, sent0_x, sent0_c, up_far, gate_got = sync((sent1, sent0_x, sent0_c, up_far, gate_got))
    up_own, up_give = to_both(held_up, up_far, place)
    gate_w, up_w = (gate_own, gate_got), (up_own, flip(up_give, 1))
    sent2, sent1_x, sent1_c = turn(sent1, 1), flip(sent1, 2), flip(sent1, 1)
    outs0 = chunk(sent0, sent0_x, sent0_c, flip(sent0_x, 1))
    sent2, sent1_x, sent1_c, *outs0 = sync((sent2, sent1_x, sent1_c, *outs0))
    sent3, sent2_x, sent2_c = turn(sent2, 1), flip(sent2, 2), flip(sent2, 1)
    outs1 = chunk(sent1, sent1_x, sent1_c, flip(sent1_x, 1))
    sent3, sent2_x, sent2_c, *outs1 = sync((sent3, sent2_x, sent2_c, *outs1))
    sent3_x, sent3_c = flip(sent3, 2), flip(sent3, 1)
    outs2 = chunk(sent2, sent2_x, sent2_c, flip(sent2_x, 1))
    h1_c, m1_c = flip(outs1[6], 1), flip(outs1[8], 1)
    sent3_x, sent3_c, h1_c, m1_c, *outs2 = sync((sent3_x, sent3_c, h1_c, m1_c, *outs2))
    outs3 = chunk(sent3, sent3_x, sent3_c, flip(sent3_x, 1))
    h1, m1 = both_x(outs1[5], h1_c), both_x(outs1[7], m1_c)
    h1_x, m1_x, h2_c, m2_c = flip(h1[1], 2), flip(m1[1], 2), flip(outs2[6], 1), flip(outs2[8], 1)
    h1_x, m1_x, h2_c, m2_c, *outs3 = sync((h1_x, m1_x, h2_c, m2_c, *outs3))
    outs = (outs0, outs1, outs2, outs3)
    arrived, hidden, grad_produced, grad_gate_low, grad_up_low = ([o[i] for o in outs] for i in range(5))
    ring, h2 = add(h1[0], h1_x), both_x(outs2[5], h2_c)
    ring, *h2 = sync((ring, *h2))
    ring, h2_x = turn(ring, 1), flip(h2[1], 2)
    h3_c, h0_c, m3_c = flip(outs3[6], 1), flip(outs0[6], 1), flip(outs3[8], 1)
    h3_c, arrived, grad_gate_low = sync((h3_c, arrived, grad_gate_low))
    gate_sum = contract(arrived, grad_gate_low)
    gate_got = flip(gate_sum[D // 2 :], 1)
    ring, h2_x, h3_c, h0_c, m3_c = sync((ring, h2_x, h3_c, h0_c, m3_c))
    ring, h3 = add(add(h2[0], h2_x), ring), both_x(outs3[5], h3_c)
    ring, *h3 = sync((ring, *h3))
    ring, h3_x, m0_c = turn(ring, 1), flip(h3[1], 2), flip(outs0[8], 1)
    gate_keep, gate_give = from_owner(gate_sum[: D // 2], gate_got, place)
    gate_give, arrived, grad_up_low = sync((gate_give, arrived, grad_up_low))
    gate_far = flip(gate_give, 4)
    up_sum = contract(arrived, grad_up_low)
    up_got = flip(up_sum[D // 2 :], 1)
    m1 = add(m1[0], m1_x)
    ring, h3_x, m0_c, m1 = sync((ring, h3_x, m0_c, m1))
    ring, h0 = add(add(h3[0], h3_x), ring), both_x(outs0[5], h0_c)
    ring, *h0 = sync((ring, *h0))
    ring, h0_x, m_ring = turn(ring, 1), flip(h0[1], 2), turn(m1, 1)
    up_got, hidden, grad_produced = sync((up_got, hidden, grad_produced))
    down_sum = contract(hidden, grad_produced)
    up_keep, up_give = from_owner(up_sum[: D // 2], up_got, place)
    ms = [both_x(o[7], t) for o, t in ((outs2, m2_c), (outs3, m3_c), (outs0, m0_c))]
    m_far = jnp.concatenate([t[1] for t in ms], axis=0)
    ring, h0_x, m_ring, down_sum, up_keep, up_give, gate_far, m_far = sync(
        (ring, h0_x, m_ring, down_sum, up_keep, up_give, gate_far, m_far)
    )
    def two(value):
        n = value.shape[0] // 2
        return value[:n], value[n:]

    def halves_sum(left, right):
        return [add(a, b) for a, b in zip(two(left), two(right))]

    down_mine, down_other = two(down_sum)
    ring, h0_x, m_far, up_give, down_mine, down_other, *gate_parts = sync(
        (ring, h0_x, m_far, up_give, down_mine, down_other, *halves_sum(gate_keep, gate_far))
    )
    down_got = flip(down_other, 1)
    gate_back, up_far, m_x = to_shards(gate_parts), flip(up_give, 4), flip(m_far, 2)
    down_got, ring, h0_x = sync((down_got, ring, h0_x))
    back = h0[0].astype(wide) + h0_x.astype(wide) + ring.astype(wide)
    grad_normed_ffn = back[:row_count]
    grad_gates = back[row_count : row_count + experts]
    grad_gates = (grad_gates[:, :row_count] + grad_gates[:, 2 * row_count : 3 * row_count]).T

    grad_out = cotangent.astype(wide)
    gates = dense_gates(normed_ffn, named)
    grad_chosen = gates * (grad_gates - jnp.sum(gates * grad_gates, axis=1, keepdims=True))
    grad_logits = grad_chosen.astype(low)
    grad_router_local = contract_rows(grad_logits, normed_ffn)
    grad_normed_ffn = grad_normed_ffn + times_transposed(grad_logits, router_w)
    grad_midway_norm, grad_ffn_gain = norm_ffn_pull(grad_normed_ffn)
    grad_midway = grad_out + grad_midway_norm
    grad_attn = grad_midway.astype(low)

    def times_back(left, pair):
        return jnp.concatenate(
            [times_transposed(left, pair[0]), times_transposed(left, pair[1])], axis=1
        )

    out_core = flip(contract([context[:, half:]], [grad_attn]), 1)
    grad_context = times_back(grad_attn, out_w).astype(low)
    grad_heads, grad_query_gain, grad_key_gain = on_chip(
        attend_back_kernel,
        [jax.ShapeDtypeStruct((row_count, 3 * D), low)] + [jax.ShapeDtypeStruct((1, D), wide)] * 2,
        order,
        grad_context,
        queries,
        keys_rot,
        values,
        raw_q,
        raw_k,
        *head_gains,
        *turns,
    )
    heads_other = contract([normed_attn[:, half:]], [grad_heads])
    down_keep, down_give = from_owner(down_mine, down_got, place)
    out_own, out_far = add_contract(context[:, :half], grad_attn, out_core, ("x",))
    m_x, up_far, down_keep, down_give, out_own, out_far, heads_other, *gate_back = sync(
        (m_x, up_far, down_keep, down_give, out_own, out_far, heads_other, *gate_back)
    )
    grad_gate = two_experts(gate_back, place)
    m2, m3, m0 = (
        add(t[0], m_x[k * row_count : (k + 1) * row_count]) for k, t in enumerate(ms)
    )

    def fold(value, bit):
        n = value.shape[1] // 2
        return value[:, :n] + flip(value[:, n:], bit)

    out_far, down_give, heads_other, *up_parts = sync(
        (out_far, down_give, heads_other, *halves_sum(up_keep, up_far))
    )
    up_back, down_far = to_shards(up_parts), flip(down_give, 4)
    out_far, heads_core = flip(out_far, 2), flip(heads_other, 1)
    heads_core, grad_heads = sync((heads_core, grad_heads))
    query_own, query_far, key_own, key_far, value_own, value_far = add_contract(
        normed_attn[:, :half], grad_heads, heads_core, ("y", "x", "x")
    )
    grad_normed_attn = sum(
        times_back(grad_heads[:, k * D : (k + 1) * D], w)
        for k, w in enumerate((query_w, key_w, value_w))
    )
    grad_normed_attn = reorder(grad_normed_attn, order, False)
    grad_inputs_norm, grad_attn_gain = norm_attn_pull(grad_normed_attn)
    grad_tokens = (grad_midway + grad_inputs_norm).astype(low)
    small = jnp.concatenate(
        [grad_router_local, grad_attn_gain[None], grad_query_gain, grad_key_gain, grad_ffn_gain[None]]
        + [jnp.zeros((-(experts + 4) % 8, D), wide)],
        axis=0,
    )
    small = reorder(small, order, True)
    down_far, out_far, small, *parts = sync(
        (down_far, out_far, small, query_own, query_far, key_own, key_far, value_own, value_far, *up_back)
    )
    query_own, query_far, key_own, key_far, value_own, value_far, *up_back = parts
    grad_up = two_experts(up_back, place)
    out_own, out_far = halves_sum(out_own, out_far)
    query_far, key_far, value_far, out_own, out_far, *down_parts = sync(
        (query_far, key_far, value_far, out_own, out_far, *halves_sum(down_keep, down_far))
    )
    query_far, key_far, down_back = flip(query_far, 4), flip(key_far, 2), to_shards(down_parts)
    small = fold(small, 1)
    query_far, key_far, small, m_ring, *down_back = sync(
        (query_far, key_far, small, m_ring, *down_back)
    )
    grad_down = two_experts(down_back, place)

    key_own, key_far = halves_sum(key_own, key_far)
    query_own, query_far = halves_sum(query_own, query_far)
    ring, key_far, out_far, value_far, query_far = sync(
        (add(m2, m_ring), key_far, out_far, value_far, query_far)
    )
    ring, key_far, out_far, value_far = (
        turn(ring, 1), flip(key_far, 4), flip(out_far, 4), flip(value_far, 2)
    )
    ring = turn(add(m3, ring), 1)
    small = fold(small, 4)
    ring, key_far, out_far, value_far, small = sync((ring, key_far, out_far, value_far, small))
    block_out = (midway + m0.astype(wide) + ring.astype(wide)).astype(low)
    value_own, value_far = halves_sum(value_own, value_far)

    def by_steps(both):
        return [both[i * rows : (i + 1) * rows] for i in range(count_dp)]

    ko = by_steps(jnp.concatenate([add(key_own, key_far), add(out_own, out_far)], axis=1))
    value_far, *ko = sync((value_far, *ko))
    ko_ring, query_far, value_far = turn(ko[3], -1), flip(query_far, 2), flip(value_far, 4)
    ko_ring = turn(add(ko[2], ko_ring), -1)
    small = fold(small, 2)
    query_far, value_far, small, ko_ring = sync((query_far, value_far, small, ko_ring))
    n = small.shape[0]
    small = small.reshape(n, count_dp, rows).transpose(1, 2, 0).reshape(count_dp * rows, n)
    small = jnp.pad(small.astype(low), ((0, 0), (0, 128 - n)))
    qv = by_steps(
        jnp.concatenate([add(query_own, query_far), add(value_own, value_far), small], axis=1)
    )
    ko_ring, qv_ring = turn(add(ko[1], ko_ring), -1), turn(qv[3], -1)
    ko_ring, qv_ring = sync((ko_ring, qv_ring))
    ko_ring = ko_ring.astype(wide) + ko[0].astype(wide)
    qv_ring = turn(add(qv[2], qv_ring), -1)
    qv_ring = turn(add(qv[1], qv_ring), -1).astype(wide) + qv[0].astype(wide)
    grad_key, grad_outproj = ko_ring[:, :D], ko_ring[:, D:]
    grad_query, grad_value = qv_ring[:, :D], qv_ring[:, D : 2 * D]
    small = qv_ring[:, 2 * D :]
    return (
        block_out,
        grad_tokens,
        grad_query,
        grad_key,
        grad_value,
        grad_outproj,
        small[:, :experts],
        grad_gate,
        grad_up,
        grad_down,
        small[:, experts],
        small[:, experts + 1],
        small[:, experts + 2],
        small[:, experts + 3],
    )


def solution(mesh):
    in_specs = (
        P(("dp", "expert"), None),
        P(("dp", "expert"), None),
        P(("dp", "expert"), None),
        P(("dp", "expert"), None),
        P(("dp", "expert"), None),
        P(("dp", "expert"), None),
        P(("dp", "expert"), None),
        P(("dp", "expert"), None),
        P(("dp", "expert"), None),
        P("expert", "dp", None),
        P("expert", "dp", None),
        P("expert", "dp", None),
        P(("dp", "expert")),
        P(("dp", "expert")),
        P(("dp", "expert")),
        P(("dp", "expert")),
    )
    out_specs = (
        P(("dp", "expert"), None),
        P(("dp", "expert"), None),
        P(("dp", "expert"), None),
        P(("dp", "expert"), None),
        P(("dp", "expert"), None),
        P(("dp", "expert"), None),
        P(("dp", "expert"), None),
        P("expert", "dp", None),
        P("expert", "dp", None),
        P("expert", "dp", None),
        P(("dp", "expert")),
        P(("dp", "expert")),
        P(("dp", "expert")),
        P(("dp", "expert")),
    )
    local = by_links if (mesh.shape["dp"], mesh.shape["expert"]) == (4, 8) else by_axes
    return jax.shard_map(local, mesh=mesh, in_specs=in_specs, out_specs=out_specs, check_vma=False)
```

```python
import functools

import jax
import jax.numpy as jnp
from jax import lax
from jax.experimental import pallas as pl
from jax.experimental.pallas import tpu as pltpu
from jax.sharding import PartitionSpec as P

D = 2048
HEADS = 16
HD = 128


EPS = 1e-05
THETA = 50000.0


def normalize(v, gain):
    return v * lax.rsqrt(jnp.mean(v * v, axis=-1, keepdims=True) + EPS) * gain


def layout(lengths_row, row_count):
    seq_ends = jnp.cumsum(lengths_row)
    position = jnp.arange(row_count, dtype=jnp.int32)
    segment = jnp.sum((position[:, None] >= seq_ends[None, :]).astype(jnp.int32), axis=1)
    seq_starts = seq_ends - lengths_row
    labels = jnp.arange(lengths_row.shape[0], dtype=jnp.int32)
    seq_start = jnp.sum(
        jnp.where(segment[:, None] == labels[None, :], seq_starts[None, :], 0), axis=1
    )
    return (segment, position - seq_start)


def rotate(v, offset):
    half_dim = v.shape[-1] // 2
    frequency = THETA ** (-jnp.arange(half_dim).astype(v.dtype) / half_dim)
    angles = offset.astype(v.dtype)[:, None] * frequency[None, :]
    cosine = jnp.cos(angles)[:, None, :]
    sine_part = jnp.sin(angles)[:, None, :]
    first_half = v[..., :half_dim]
    second_half = v[..., half_dim:]
    return jnp.concatenate(
        [
            first_half * cosine - second_half * sine_part,
            second_half * cosine + first_half * sine_part,
        ],
        axis=-1,
    )


def head_prep(raw_q, raw_k, gain_q, gain_k, offset):
    row_count = raw_q.shape[0]
    queries = rotate(
        normalize(raw_q.reshape(row_count, HEADS, HD), gain_q.reshape(HEADS, HD)), offset
    )
    keys_rot = rotate(
        normalize(raw_k.reshape(row_count, HEADS, HD), gain_k.reshape(HEADS, HD)), offset
    )
    return (queries, keys_rot)


def route_softmax(chosen):
    peak = jnp.max(chosen, axis=-1, keepdims=True)
    exp_scores = jnp.exp(chosen - peak)
    return exp_scores / jnp.sum(exp_scores, axis=-1, keepdims=True)


def swiglu(gate_act, up_act):
    return jax.nn.silu(gate_act) * up_act


def slots(flat_routes, expert_count, capacity):
    one_hot = (flat_routes[:, None] == jnp.arange(expert_count, dtype=jnp.int32)[None, :]).astype(
        jnp.int32
    )
    slot_rank = jnp.sum((jnp.cumsum(one_hot, axis=0) - one_hot) * one_hot, axis=1)
    return flat_routes * capacity + slot_rank


def contract_rows(left, right):
    return lax.dot_general(
        left, right, (((0,), (0,)), ((), ())), preferred_element_type=jnp.float32
    )


def times_transposed(left, right):
    return lax.dot_general(
        left, right, (((1,), (1,)), ((), ())), preferred_element_type=jnp.float32
    )


def by_axes(
    tokens,
    cotangent,
    lengths,
    routes,
    w_query,
    w_key,
    w_value,
    w_out,
    w_router,
    w_gate,
    w_up,
    w_down,
    g_attn,
    g_query,
    g_key,
    g_ffn,
):
    row_count = tokens.shape[0]
    top_count = routes.shape[1]
    local_experts = w_gate.shape[0]
    owners = lax.axis_size("expert")
    experts = local_experts * owners
    capacity = row_count * top_count * 5 // (4 * experts)
    score_scale = HD ** (-0.5)
    segment, offset = layout(lengths[0], row_count)
    seq_mask = (segment[:, None] == segment[None, :])[None]
    dense = (
        lax.all_gather(w_query, ("dp", "expert"), axis=0, tiled=True),
        lax.all_gather(w_key, ("dp", "expert"), axis=0, tiled=True),
        lax.all_gather(w_value, ("dp", "expert"), axis=0, tiled=True),
        lax.all_gather(w_out, ("dp", "expert"), axis=0, tiled=True),
        lax.all_gather(w_router, ("dp", "expert"), axis=0, tiled=True),
        lax.all_gather(g_attn, ("dp", "expert"), axis=0, tiled=True),
        lax.all_gather(g_query, ("dp", "expert"), axis=0, tiled=True),
        lax.all_gather(g_key, ("dp", "expert"), axis=0, tiled=True),
        lax.all_gather(g_ffn, ("dp", "expert"), axis=0, tiled=True),
    )
    query_w, key_w, value_w, out_w, router_w, attn_gain, query_gain, key_gain, ffn_gain = dense
    expert_full = (
        lax.all_gather(w_gate, "dp", axis=1, tiled=True),
        lax.all_gather(w_up, "dp", axis=1, tiled=True),
        lax.all_gather(w_down, "dp", axis=1, tiled=True),
    )
    gate_full, up_full, down_full = expert_full
    inputs = tokens.astype(jnp.float32)
    normed_f, norm_attn_pull = jax.vjp(normalize, inputs, attn_gain.astype(jnp.float32))
    normed_attn = normed_f.astype(jnp.bfloat16)
    raw_q = jnp.dot(normed_attn, query_w, preferred_element_type=jnp.float32)
    raw_k = jnp.dot(normed_attn, key_w, preferred_element_type=jnp.float32)
    values = jnp.dot(normed_attn, value_w, preferred_element_type=jnp.float32).astype(jnp.bfloat16)
    value_heads = values.reshape(row_count, HEADS, HD)

    def prep_local(first, second, first_gain, second_gain):
        return head_prep(first, second, first_gain, second_gain, offset)

    rotated, heads_pull = jax.vjp(
        prep_local, raw_q, raw_k, query_gain.astype(jnp.float32), key_gain.astype(jnp.float32)
    )
    queries = rotated[0].astype(jnp.bfloat16)
    keys_rot = rotated[1].astype(jnp.bfloat16)
    scores = (
        jnp.einsum("qhd,khd->hqk", queries, keys_rot, preferred_element_type=jnp.float32)
        * score_scale
    )
    scores = jnp.where(seq_mask, scores, -1e30)
    peak = jnp.max(scores, axis=-1, keepdims=True)
    exp_scores = jnp.exp(scores - peak)
    exp_total = jnp.sum(exp_scores, axis=-1, keepdims=True)
    log_total = peak + jnp.log(exp_total)
    probs_low = (exp_scores / exp_total).astype(jnp.bfloat16)
    context = (
        jnp.einsum("hqk,khd->qhd", probs_low, value_heads, preferred_element_type=jnp.float32)
        .astype(jnp.bfloat16)
        .reshape(row_count, D)
    )
    midway = inputs + jnp.dot(context, out_w, preferred_element_type=jnp.float32)
    normed2_f, norm_ffn_pull = jax.vjp(normalize, midway, ffn_gain.astype(jnp.float32))
    normed_ffn = normed2_f.astype(jnp.bfloat16)
    logits = jnp.dot(normed_ffn, router_w, preferred_element_type=jnp.float32)
    chosen = jnp.take_along_axis(logits, routes, axis=1)
    gates, gates_pull = jax.vjp(route_softmax, chosen)
    slot_index = slots(routes.reshape(-1), experts, capacity)
    sent_rows = (
        jnp.zeros((experts * capacity, D), jnp.bfloat16)
        .at[slot_index]
        .set(jnp.repeat(normed_ffn, top_count, axis=0))
    )
    sent_rows = sent_rows.reshape(owners, local_experts, capacity, D)
    arrived = lax.all_to_all(sent_rows, "expert", split_axis=0, concat_axis=2, tiled=True).reshape(
        local_experts, owners * capacity, D
    )
    gate_act = jnp.einsum("erd,edf->erf", arrived, gate_full, preferred_element_type=jnp.float32)
    up_act = jnp.einsum("erd,edf->erf", arrived, up_full, preferred_element_type=jnp.float32)
    hidden = swiglu(gate_act, up_act).astype(jnp.bfloat16)
    produced = jnp.einsum(
        "erf,efd->erd", hidden, down_full, preferred_element_type=jnp.float32
    ).astype(jnp.bfloat16)
    returned = lax.all_to_all(
        produced.reshape(1, local_experts, owners * capacity, D),
        "expert",
        split_axis=2,
        concat_axis=0,
        tiled=True,
    ).reshape(experts * capacity, D)
    picked = returned[slot_index].reshape(row_count, top_count, D).astype(jnp.float32)
    block_out = (midway + jnp.sum(gates[:, :, None] * picked, axis=1)).astype(jnp.bfloat16)
    grad_out = cotangent.astype(jnp.float32)
    grad_gates = jnp.sum(grad_out[:, None, :] * picked, axis=2)
    grad_picked = (
        (gates[:, :, None] * grad_out[:, None, :])
        .astype(jnp.bfloat16)
        .reshape(row_count * top_count, D)
    )
    grad_sent = jnp.zeros((experts * capacity, D), jnp.bfloat16).at[slot_index].set(grad_picked)
    grad_sent = grad_sent.reshape(owners, local_experts, capacity, D)
    grad_arrived = lax.all_to_all(
        grad_sent, "expert", split_axis=0, concat_axis=2, tiled=True
    ).reshape(local_experts, owners * capacity, D)
    gate_back, up_back, down_back = (
        lax.all_gather(w_gate, "dp", axis=1, tiled=True),
        lax.all_gather(w_up, "dp", axis=1, tiled=True),
        lax.all_gather(w_down, "dp", axis=1, tiled=True),
    )
    grad_hidden = jnp.einsum(
        "erd,efd->erf", grad_arrived, down_back, preferred_element_type=jnp.float32
    )
    grad_down_local = jnp.einsum(
        "erf,erd->efd", hidden, grad_arrived, preferred_element_type=jnp.float32
    )
    act_unused, act_pull = jax.vjp(swiglu, gate_act, up_act)
    grad_gate_act, grad_up_act = act_pull(grad_hidden)
    grad_gate_low = grad_gate_act.astype(jnp.bfloat16)
    grad_up_low = grad_up_act.astype(jnp.bfloat16)
    grad_gate_local = jnp.einsum(
        "erd,erf->edf", arrived, grad_gate_low, preferred_element_type=jnp.float32
    )
    grad_up_local = jnp.einsum(
        "erd,erf->edf", arrived, grad_up_low, preferred_element_type=jnp.float32
    )
    grad_arrival = jnp.einsum(
        "erf,edf->erd", grad_gate_low, gate_back, preferred_element_type=jnp.float32
    )
    grad_arrival = grad_arrival + jnp.einsum(
        "erf,edf->erd", grad_up_low, up_back, preferred_element_type=jnp.float32
    )
    grad_arrival = grad_arrival.astype(jnp.bfloat16).reshape(1, local_experts, owners * capacity, D)
    grad_back = lax.all_to_all(
        grad_arrival, "expert", split_axis=2, concat_axis=0, tiled=True
    ).reshape(experts * capacity, D)
    grad_normed_ffn = jnp.sum(
        grad_back[slot_index].reshape(row_count, top_count, D).astype(jnp.float32), axis=1
    )
    expert_grads = (
        lax.psum_scatter(grad_gate_local, "dp", scatter_dimension=1, tiled=True),
        lax.psum_scatter(grad_up_local, "dp", scatter_dimension=1, tiled=True),
        lax.psum_scatter(grad_down_local, "dp", scatter_dimension=1, tiled=True),
    )
    grad_chosen = gates_pull(grad_gates)[0]
    expert_ids = jnp.arange(experts, dtype=jnp.int32)
    grad_logits = jnp.sum(
        jnp.where(routes[:, :, None] == expert_ids[None, None, :], grad_chosen[:, :, None], 0.0),
        axis=1,
    ).astype(jnp.bfloat16)
    grad_router_local = contract_rows(normed_ffn, grad_logits)
    dense_back = (
        lax.all_gather(w_query, ("dp", "expert"), axis=0, tiled=True),
        lax.all_gather(w_key, ("dp", "expert"), axis=0, tiled=True),
        lax.all_gather(w_value, ("dp", "expert"), axis=0, tiled=True),
        lax.all_gather(w_out, ("dp", "expert"), axis=0, tiled=True),
        lax.all_gather(w_router, ("dp", "expert"), axis=0, tiled=True),
    )
    query_back, key_back, value_back, out_back, router_back = dense_back
    grad_normed_ffn = grad_normed_ffn + times_transposed(grad_logits, router_back)
    grad_midway_norm, grad_ffn_gain = norm_ffn_pull(grad_normed_ffn)
    grad_midway = grad_out + grad_midway_norm
    grad_attn = grad_midway.astype(jnp.bfloat16)
    grad_out_local = contract_rows(context, grad_attn)
    grad_context = (
        times_transposed(grad_attn, out_back).astype(jnp.bfloat16).reshape(row_count, HEADS, HD)
    )
    probs = jnp.where(seq_mask, jnp.exp(scores - log_total), 0.0)
    grad_probs = jnp.einsum(
        "qhd,khd->hqk", grad_context, value_heads, preferred_element_type=jnp.float32
    )
    grad_scores = (
        probs * (grad_probs - jnp.sum(grad_probs * probs, axis=-1, keepdims=True))
    ).astype(jnp.bfloat16)
    grad_values = (
        jnp.einsum("hqk,qhd->khd", probs_low, grad_context, preferred_element_type=jnp.float32)
        .astype(jnp.bfloat16)
        .reshape(row_count, D)
    )
    grad_queries = (
        jnp.einsum("hqk,khd->qhd", grad_scores, keys_rot, preferred_element_type=jnp.float32)
        * score_scale
    )
    grad_keys = (
        jnp.einsum("hqk,qhd->khd", grad_scores, queries, preferred_element_type=jnp.float32)
        * score_scale
    )
    grad_raw_q, grad_raw_k, grad_query_gain, grad_key_gain = heads_pull((grad_queries, grad_keys))
    grad_raw_q = grad_raw_q.astype(jnp.bfloat16)
    grad_raw_k = grad_raw_k.astype(jnp.bfloat16)
    grad_query_local = contract_rows(normed_attn, grad_raw_q)
    grad_key_local = contract_rows(normed_attn, grad_raw_k)
    grad_value_local = contract_rows(normed_attn, grad_values)
    grad_normed_attn = (
        times_transposed(grad_raw_q, query_back)
        + times_transposed(grad_raw_k, key_back)
        + times_transposed(grad_values, value_back)
    )
    grad_inputs_norm, grad_attn_gain = norm_attn_pull(grad_normed_attn)
    grad_tokens = (grad_midway + grad_inputs_norm).astype(jnp.bfloat16)
    dense_grads = (
        lax.psum_scatter(grad_query_local, ("dp", "expert"), scatter_dimension=0, tiled=True),
        lax.psum_scatter(grad_key_local, ("dp", "expert"), scatter_dimension=0, tiled=True),
        lax.psum_scatter(grad_value_local, ("dp", "expert"), scatter_dimension=0, tiled=True),
        lax.psum_scatter(grad_out_local, ("dp", "expert"), scatter_dimension=0, tiled=True),
        lax.psum_scatter(grad_router_local, ("dp", "expert"), scatter_dimension=0, tiled=True),
        lax.psum_scatter(grad_attn_gain, ("dp", "expert"), scatter_dimension=0, tiled=True),
        lax.psum_scatter(grad_query_gain, ("dp", "expert"), scatter_dimension=0, tiled=True),
        lax.psum_scatter(grad_key_gain, ("dp", "expert"), scatter_dimension=0, tiled=True),
        lax.psum_scatter(grad_ffn_gain, ("dp", "expert"), scatter_dimension=0, tiled=True),
    )
    return (
        block_out,
        grad_tokens,
        dense_grads[0],
        dense_grads[1],
        dense_grads[2],
        dense_grads[3],
        dense_grads[4],
        expert_grads[0],
        expert_grads[1],
        expert_grads[2],
        dense_grads[5],
        dense_grads[6],
        dense_grads[7],
        dense_grads[8],
    )


SLOTS = 128
SMALL = pl.CostEstimate(flops=1, bytes_accessed=1, transcendentals=0)


def flip(value, bit):
    count = lax.axis_size("expert")
    return lax.ppermute(value, "expert", [(i, i ^ bit) for i in range(count)])


def turn(value, step):
    count = lax.axis_size("dp")
    return lax.ppermute(value, "dp", [(i, (i + step) % count) for i in range(count)])


def order_kernel(to_own, order_ref, v_ref, o_ref):
    half = 64
    lanes = v_ref.shape[1] // 2
    groups = v_ref.shape[1] // 128
    odd = order_ref[groups] == 1
    for pair in range(groups // 2):
        first = pl.ds(pl.multiple_of(order_ref[2 * pair] * 128, 128), 128)
        second = pl.ds(pl.multiple_of(order_ref[2 * pair + 1] * 128, 128), 128)
        if to_own:
            a = v_ref[:, first].astype(jnp.float32)
            b = v_ref[:, second].astype(jnp.float32)
            low = jnp.concatenate([a[:, :half], b[:, :half]], axis=1)
            high = jnp.concatenate([a[:, half:], b[:, half:]], axis=1)
            o_ref[:, pair * 128 : pair * 128 + 128] = jnp.where(odd, high, low).astype(o_ref.dtype)
            o_ref[:, lanes + pair * 128 : lanes + pair * 128 + 128] = jnp.where(
                odd, low, high
            ).astype(o_ref.dtype)
        else:
            low = v_ref[:, pair * 128 : pair * 128 + 128].astype(jnp.float32)
            high = v_ref[:, lanes + pair * 128 : lanes + pair * 128 + 128].astype(jnp.float32)
            low, high = jnp.where(odd, high, low), jnp.where(odd, low, high)
            o_ref[:, first] = jnp.concatenate([low[:, :half], high[:, :half]], axis=1).astype(
                o_ref.dtype
            )
            o_ref[:, second] = jnp.concatenate([low[:, half:], high[:, half:]], axis=1).astype(
                o_ref.dtype
            )


def reorder(value, order, to_own):
    return pl.pallas_call(
        functools.partial(order_kernel, to_own),
        out_shape=jax.ShapeDtypeStruct(value.shape, value.dtype),
        in_specs=[
            pl.BlockSpec(memory_space=pltpu.SMEM),
            pl.BlockSpec(memory_space=pltpu.VMEM),
        ],
        out_specs=pl.BlockSpec(memory_space=pltpu.VMEM),
        compiler_params=pltpu.CompilerParams(vmem_limit_bytes=16 * 1024 * 1024),
        cost_estimate=pl.CostEstimate(flops=0, bytes_accessed=4 * value.size, transcendentals=0),
    )(order, value)


def ring_gather(value):
    pieces = [value]
    for _ in range(lax.axis_size("dp") - 1):
        pieces.append(turn(pieces[-1], 1))
    return pieces


def ring_scatter(pieces):
    total = pieces[-1]
    for piece in pieces[-2::-1]:
        total = turn(total, -1).astype(jnp.float32) + piece.astype(jnp.float32)
        if piece is not pieces[0]:
            total = total.astype(piece.dtype)
    return total


def side_by_side(pieces, width):
    return (
        jnp.concatenate([p[:, :width] for p in pieces], axis=0),
        jnp.concatenate([p[:, width:] for p in pieces], axis=0),
    )


def by_x(own, far):
    n = own.shape[0] // 2
    return jnp.concatenate([own[:n], far[:n], own[n:], far[n:]], axis=0)


def ring_scatter_up(pieces):
    low, wide = pieces[0].dtype, jnp.float32
    total = pieces[1]
    for piece in pieces[2:]:
        total = (turn(total, 1).astype(wide) + piece.astype(wide)).astype(low)
    return turn(total, 1).astype(wide) + pieces[0].astype(wide)


def expert_rounds(count_dp, count_expert):
    rounds = []
    for r in range(2):
        pairs = []
        for d in range(count_dp):
            for e in range(count_expert):
                goal = 2 * (e & 1) + (d // 2 + r) % 2
                pairs.append((d * count_expert + e, goal * count_expert + (e & ~1) + d % 2))
        rounds.append(pairs)
    return rounds


def owner_pieces(weight, place):
    d, c, x, y = place
    return [lax.dynamic_index_in_dim(weight, (d // 2 + r) % 2, 0, keepdims=False) for r in range(2)]


def to_owner(pieces):
    rounds = expert_rounds(lax.axis_size("dp"), lax.axis_size("expert"))
    return [lax.ppermute(p, ("dp", "expert"), pairs) for p, pairs in zip(pieces, rounds)]


def to_both(held, far, place):
    d, c, x, y = place
    return jnp.where(y == c, held, far), jnp.where(y == c, far, held)


def from_owner(keep, got, place):
    d, c, x, y = place
    return jnp.where(y == c, keep, got), jnp.where(y == c, got, keep)


def to_shards(parts):
    rounds = expert_rounds(lax.axis_size("dp"), lax.axis_size("expert"))
    return [
        lax.ppermute(part, ("dp", "expert"), [(b, a) for a, b in pairs])
        for part, pairs in zip(parts, rounds)
    ]


def two_experts(pieces, place):
    d, c, x, y = place
    first, second = (p.astype(jnp.float32) for p in pieces)
    own = d // 2 == 0
    return jnp.stack([jnp.where(own, first, second), jnp.where(own, second, first)])


def contract_kernel(count, *refs):
    out_ref = refs[-1]
    out_ref[...] = sum(
        lax.dot_general(
            left_ref[...],
            right_ref[...],
            (((0,), (0,)), ((), ())),
            preferred_element_type=jnp.float32,
        )
        for left_ref, right_ref in zip(refs[:count], refs[count : 2 * count])
    ).astype(out_ref.dtype)


def contract(lefts, rights, low=jnp.bfloat16):
    depth, width = lefts[0].shape
    across = rights[0].shape[1]
    block = 512
    return pl.pallas_call(
        functools.partial(contract_kernel, len(lefts)),
        grid=(width // block,),
        in_specs=[pl.BlockSpec((depth, block), lambda i: (0, i))] * len(lefts)
        + [pl.BlockSpec((depth, across), lambda i: (0, 0))] * len(rights),
        out_specs=pl.BlockSpec((block, across), lambda i: (i, 0)),
        out_shape=jax.ShapeDtypeStruct((width, across), low),
        compiler_params=pltpu.CompilerParams(vmem_limit_bytes=48 * 1024 * 1024),
        cost_estimate=SMALL,
    )(*lefts, *rights)


def add_contract_kernel(firsts, left_ref, right_ref, got_ref, *out_refs):
    step = pl.program_id(0)
    width = out_refs[0].shape[1]
    total = lax.dot_general(
        left_ref[...], right_ref[...], (((0,), (0,)), ((), ())), preferred_element_type=jnp.float32
    )
    total = (total + got_ref[...].astype(jnp.float32)).astype(got_ref.dtype)
    for n, first in enumerate(firsts):
        far = step >= 2 if first == "y" else step % 2 == 1
        part = total[:, n * width : (n + 1) * width]

        @pl.when(jnp.logical_not(far))
        def _(n=n, part=part):
            out_refs[2 * n][...] = part

        @pl.when(far)
        def _(n=n, part=part):
            out_refs[2 * n + 1][...] = part


def add_contract(left, right, got, firsts):
    depth, rows = left.shape
    block = rows // 4
    width = right.shape[1] // len(firsts)
    outs, specs = [], []
    for first in firsts:
        if first == "y":
            maps = (lambda i: (jnp.minimum(i, 1), 0)), (lambda i: (jnp.maximum(i - 2, 0), 0))
        else:
            maps = (lambda i: (i // 2, 0)), (lambda i: (i // 2, 0))
        outs += [jax.ShapeDtypeStruct((2 * block, width), got.dtype)] * 2
        specs += [pl.BlockSpec((block, width), index_map) for index_map in maps]
    return pl.pallas_call(
        functools.partial(add_contract_kernel, firsts),
        grid=(4,),
        in_specs=[
            pl.BlockSpec((depth, block), lambda i: (0, i)),
            pl.BlockSpec((depth, right.shape[1]), lambda i: (0, 0)),
            pl.BlockSpec((block, right.shape[1]), lambda i: (i, 0)),
        ],
        out_specs=specs,
        out_shape=outs,
        compiler_params=pltpu.CompilerParams(vmem_limit_bytes=48 * 1024 * 1024),
        cost_estimate=SMALL,
    )(left, right, got)


def head_norm(v):
    return lax.rsqrt(jnp.mean(v * v, axis=-1, keepdims=True) + EPS)


def dot32(left, right, dims):
    return lax.dot_general(
        left, right, ((dims[:1], dims[1:]), ((), ())), preferred_element_type=jnp.float32
    )


def masked_softmax(q, k, same):
    scores = jnp.where(same, dot32(q, k, (1, 1)) * HD ** (-0.5), -1e30)
    weights = jnp.exp(scores - jnp.max(scores, axis=-1, keepdims=True))
    return weights / jnp.sum(weights, axis=-1, keepdims=True)


def attend_kernel(
    order_ref, raw_q, raw_k, v_ref, gain_q, gain_k, cos_ref, sin_ref, seg_c, seg_r, q_ref, k_ref, o_ref
):
    low = jnp.bfloat16
    same = seg_c[...] == seg_r[...]
    lanes = o_ref.shape[1] // 2
    groups = lanes // 64
    odd = order_ref[groups] == 1

    def head(h):
        cols = pl.ds(pl.multiple_of(h * HD, HD), HD)

        def prepared(raw, gain):
            v = raw[:, cols]
            v = v * head_norm(v) * gain[:, cols]
            return (v * cos_ref[...] + pltpu.roll(v, HD // 2, 1) * sin_ref[...]).astype(low)

        q, k = prepared(raw_q, gain_q), prepared(raw_k, gain_k)
        q_ref[:, cols], k_ref[:, cols] = q, k
        probs = masked_softmax(q, k, same).astype(low)
        return dot32(probs, v_ref[:, cols], (1, 0))

    @pl.loop(0, groups // 2)
    def _(pair):
        a, b = head(order_ref[2 * pair]), head(order_ref[2 * pair + 1])
        first = jnp.concatenate([a[:, :64], b[:, :64]], axis=1)
        second = jnp.concatenate([a[:, 64:], b[:, 64:]], axis=1)
        cols = pl.ds(pl.multiple_of(pair * 128, 128), 128)
        o_ref[:, cols] = jnp.where(odd, second, first).astype(low)
        cols = pl.ds(pl.multiple_of(lanes + pair * 128, 128), 128)
        o_ref[:, cols] = jnp.where(odd, first, second).astype(low)


def attend_back_kernel(
    order_ref,
    grad_ref,
    q_ref,
    k_ref,
    v_ref,
    raw_q,
    raw_k,
    gain_q,
    gain_k,
    cos_ref,
    sin_ref,
    seg_c,
    seg_r,
    d_ref,
    gq_ref,
    gk_ref,
):
    low, wide = jnp.bfloat16, jnp.float32
    same = seg_c[...] == seg_r[...]
    lanes = grad_ref.shape[1] // 2
    groups = lanes // 64
    odd = order_ref[groups] == 1
    scale = HD ** (-0.5)

    def back(grad, raw, gain, at, g_ref, cols):
        grad = grad * cos_ref[...] + pltpu.roll(grad * sin_ref[...], HD // 2, 1)
        v = raw[:, cols]
        r = head_norm(v)
        g_ref[:, cols] = jnp.sum(grad * v * r, axis=0, keepdims=True)
        grad = grad * gain[:, cols]
        d_ref[:, at] = (
            r * grad - v * (r * r * r) * jnp.mean(grad * v, axis=-1, keepdims=True)
        ).astype(low)

    def head(h, grad):
        cols, at_k, at_v = (
            pl.ds(pl.multiple_of(h * HD + n * 2 * lanes, HD), HD) for n in range(3)
        )
        q, k = q_ref[:, cols], k_ref[:, cols]
        probs = jnp.where(same, masked_softmax(q, k, same), 0.0)
        grad_probs = dot32(grad, v_ref[:, cols], (1, 1))
        grad_scores = probs * (grad_probs - jnp.sum(grad_probs * probs, axis=-1, keepdims=True))
        grad_scores = grad_scores.astype(low)
        d_ref[:, at_v] = dot32(probs.astype(low), grad, (0, 0)).astype(low)
        back(dot32(grad_scores, k, (1, 0)) * scale, raw_q, gain_q, cols, gq_ref, cols)
        back(dot32(grad_scores, q, (0, 0)) * scale, raw_k, gain_k, at_k, gk_ref, cols)

    @pl.loop(0, groups // 2)
    def _(pair):
        cols = pl.ds(pl.multiple_of(pair * 128, 128), 128)
        first = grad_ref[:, cols].astype(wide)
        cols = pl.ds(pl.multiple_of(lanes + pair * 128, 128), 128)
        second = grad_ref[:, cols].astype(wide)
        first, second = jnp.where(odd, second, first), jnp.where(odd, first, second)
        for n in range(2):
            part = slice(64 * n, 64 * n + 64)
            grad = jnp.concatenate([first[:, part], second[:, part]], axis=1).astype(low)
            head(order_ref[2 * pair + n], grad)


def on_chip(kernel, outs, *args):
    vmem = pl.BlockSpec(memory_space=pltpu.VMEM)
    return pl.pallas_call(
        kernel,
        out_shape=outs,
        in_specs=[pl.BlockSpec(memory_space=pltpu.SMEM)] + [vmem] * (len(args) - 1),
        out_specs=[vmem] * len(outs),
        compiler_params=pltpu.CompilerParams(vmem_limit_bytes=32 * 1024 * 1024),
        cost_estimate=SMALL,
    )(*args)


def expert_kernel(experts, count, tokens, *refs):
    low, wide = jnp.bfloat16, jnp.float32
    place_ref, refs = refs[0], refs[1:]
    in_refs, refs = refs[:count], refs[count:]
    gate_refs, up_refs, down_refs, router_ref, refs = refs[:2], refs[2:4], refs[4:6], refs[6], refs[7:]
    x_ref, hid_ref, dy_ref, da_ref, du_ref, refs = *refs[:5], refs[5:]
    dh_refs, out_refs, refs = refs[:2], refs[2:4], refs[4:]
    pair = count // 2
    pick_ref, turned_ref, c_ref, a_ref, u_ref, y_ref, dx_ref = refs
    expert = place_ref[0]
    width = in_refs[0].shape[1]
    inner = hid_ref.shape[1]
    name_rows = in_refs[0].shape[0] - 2 * tokens
    tile = 512
    deep, flat = width // 4, inner // 4

    def dot(left, right, dims):
        return lax.dot_general(left, right, ((dims[:1], dims[1:]), ((), ())), preferred_element_type=wide)

    def slice_at(pos, size):
        return pl.ds(pl.multiple_of(place_ref[1 + pos] * size, size), size)

    before = lax.broadcasted_iota(jnp.int32, (tokens, tokens), 0)
    upto = lax.broadcasted_iota(jnp.int32, (tokens, tokens), 1)
    upto = jnp.where(before <= upto, 1.0, 0.0).astype(low)
    name_row = lax.broadcasted_iota(jnp.int32, (name_rows, tokens), 0)
    slot = lax.broadcasted_iota(jnp.int32, (SLOTS, tokens), 0)
    lane = lax.broadcasted_iota(jnp.int32, (SLOTS, 128), 1)
    gates = []
    for b in range(count):
        named = in_refs[b][2 * tokens :, :tokens]
        own = jnp.sum(jnp.where(name_row == expert, named.astype(wide), 0.0), axis=0, keepdims=True)
        rank = dot(jnp.broadcast_to(own, (16, tokens)).astype(low), upto, (1, 0))[:1]
        chosen = (rank.astype(jnp.int32) - 1 == slot) & (own > 0.5)
        picks = jnp.where(chosen, 1.0, 0.0)
        turned_ref[b] = picks.T.astype(low)
        picks = picks.astype(low)
        rows = pl.ds(b * SLOTS, SLOTS)
        pick_ref[b] = picks
        logits = jnp.zeros((SLOTS, 128), wide)
        for pos in range(4):
            x = dot(picks, in_refs[b][:tokens, slice_at(pos, deep)], (1, 0)).astype(low)
            x_ref[rows, pos * deep : (pos + 1) * deep] = x
            logits += dot(x, router_ref[slice_at(pos, deep), :], (1, 0))
        c_ref[rows] = dot(picks, in_refs[b][tokens : 2 * tokens], (1, 0)).astype(low)
        named = jnp.concatenate([named, jnp.zeros((128 - name_rows, tokens), low)], axis=0)
        named = dot(picks, named, (1, 1)) > 0.5
        logits = jnp.where(named, logits, -1e30)
        weights = jnp.exp(logits - jnp.max(logits, axis=1, keepdims=True))
        total = jnp.sum(weights, axis=1, keepdims=True)
        gates.append(jnp.sum(jnp.where(lane == expert, weights, 0.0), axis=1, keepdims=True) / total)
    gate = jnp.concatenate(gates, axis=0)

    @pl.loop(0, 4)
    def _(pos):
        cols = slice_at(pos, flat)
        a, u = (
            sum(
                dot(x_ref[:, h * (width // 2) : (h + 1) * (width // 2)], w_refs[h][:, cols], (1, 0))
                for h in range(2)
            )
            for w_refs in (gate_refs, up_refs)
        )
        cols = pl.ds(pl.multiple_of(pos * flat, flat), flat)
        a_ref[:, cols] = a
        u_ref[:, cols] = u
        hid_ref[:, cols] = (a / (1.0 + jnp.exp(-a)) * u).astype(low)

    def forward(j, dgate):
        cols = pl.ds(pl.multiple_of(j * tile, tile), tile)
        y = sum(
            dot(hid_ref[:, h * (inner // 2) : (h + 1) * (inner // 2)], down_refs[h][:, cols], (1, 0))
            for h in range(2)
        )
        y = y.astype(low).astype(wide)
        c = c_ref[:, cols].astype(wide)
        y_ref[...] = (gate * y).astype(low)
        dy_ref[:, cols] = (gate * c).astype(low)
        for b in range(count):
            out_refs[b // pair][b % pair, :, cols] = dot(
                turned_ref[b], y_ref[pl.ds(b * SLOTS, SLOTS)], (1, 0)
            ).astype(low)
        return dgate + jnp.sum(c * y, axis=1, keepdims=True)

    dgate = lax.fori_loop(0, width // tile, forward, jnp.zeros((count * SLOTS, 1), wide))
    for b in range(count):
        rows = dgate[b * SLOTS : (b + 1) * SLOTS]
        rows = jnp.sum(jnp.where(pick_ref[b].astype(wide) > 0.5, rows, 0.0), axis=0, keepdims=True)
        rows = jnp.where(name_row == expert, rows, 0.0)
        high = rows.astype(low)
        names = pl.ds(tokens, name_rows)
        dh_ref = dh_refs[b // pair]
        dh_ref[b % pair, names, :] = jnp.zeros((name_rows, width), low)
        dh_ref[b % pair, names, :tokens] = high
        dh_ref[b % pair, names, 2 * tokens : 3 * tokens] = (rows - high.astype(wide)).astype(low)

    for h in range(2):

        @pl.loop(0, 2)
        def _(r, h=h):
            dhid = dot(
                dy_ref[...], down_refs[h][pl.ds(pl.multiple_of(r * flat, flat), flat), :], (1, 1)
            )
            pos = 2 * h + r
            cols = pl.ds(pl.multiple_of(pos * flat, flat), flat)
            a, u = a_ref[:, cols], u_ref[:, cols]
            s = 1.0 / (1.0 + jnp.exp(-a))
            cols = slice_at(pos, flat)
            da_ref[:, cols] = (dhid * u * (s * (1.0 + a * (1.0 - s)))).astype(low)
            du_ref[:, cols] = (dhid * (a * s)).astype(low)

    for h in range(2):

        @pl.loop(0, width // (2 * tile))
        def _(i, h=h):
            rows = pl.ds(pl.multiple_of(i * tile, tile), tile)
            dx = dot(da_ref[...], gate_refs[h][rows, :], (1, 1)) + dot(
                du_ref[...], up_refs[h][rows, :], (1, 1)
            )
            dx_ref[...] = dx.astype(low)
            per = deep // tile
            start = place_ref[1 + 2 * h + i // per] * deep + (i % per) * tile
            cols = pl.ds(pl.multiple_of(start, tile), tile)
            for b in range(count):
                dh_refs[b // pair][b % pair, :tokens, cols] = dot(
                    turned_ref[b], dx_ref[pl.ds(b * SLOTS, SLOTS)], (1, 0)
                ).astype(low)


def expert_chunk(place, blocks, tokens, gate_w, up_w, down_w, router_w, experts):
    low, wide = jnp.bfloat16, jnp.float32
    count = len(blocks)
    width = blocks[0].shape[1]
    inner = gate_w[0].shape[1]
    rows = count * SLOTS
    vmem = pl.BlockSpec(memory_space=pltpu.VMEM)
    outs = [
        jax.ShapeDtypeStruct((rows, width), low),
        jax.ShapeDtypeStruct((rows, inner), low),
        jax.ShapeDtypeStruct((rows, width), low),
        jax.ShapeDtypeStruct((rows, inner), low),
        jax.ShapeDtypeStruct((rows, inner), low),
        *[jax.ShapeDtypeStruct((count // 2, blocks[0].shape[0] - tokens, width), low)] * 2,
        *[jax.ShapeDtypeStruct((count // 2, tokens, width), low)] * 2,
    ]
    return pl.pallas_call(
        functools.partial(expert_kernel, experts, count, tokens),
        out_shape=outs,
        in_specs=[pl.BlockSpec(memory_space=pltpu.SMEM)] + [vmem] * (count + 7),
        out_specs=[vmem] * len(outs),
        scratch_shapes=[
            pltpu.VMEM((count, SLOTS, tokens), low),
            pltpu.VMEM((count, tokens, SLOTS), low),
            pltpu.VMEM((rows, width), low),
            pltpu.VMEM((rows, inner), wide),
            pltpu.VMEM((rows, inner), wide),
            pltpu.VMEM((rows, 512), low),
            pltpu.VMEM((rows, 512), low),
        ],
        compiler_params=pltpu.CompilerParams(vmem_limit_bytes=58 * 1024 * 1024),
        cost_estimate=SMALL,
    )(place, *blocks, *gate_w, *up_w, *down_w, router_w)


def by_links(
    tokens,
    cotangent,
    lengths,
    routes,
    w_query,
    w_key,
    w_value,
    w_out,
    w_router,
    w_gate,
    w_up,
    w_down,
    g_attn,
    g_query,
    g_key,
    g_ffn,
):
    low, wide = jnp.bfloat16, jnp.float32
    row_count = tokens.shape[0]
    rows = w_query.shape[0]
    experts = w_router.shape[1]
    count_dp = lax.axis_size("dp")
    score_scale = HD ** (-0.5)
    d = lax.axis_index("dp")
    e = lax.axis_index("expert")
    c, x, y = e & 1, (e >> 1) & 1, e >> 2
    place = (d, c, x, y)
    own_expert = 8 * c + 4 * x + d
    at_owner = jnp.stack(
        [own_expert] + [2 * ((d + r) % 2) + (c ^ h) for h in range(2) for r in range(2)]
    ).astype(jnp.int32)
    group = jnp.arange(16, dtype=jnp.int32)
    group_order = (
        ((d - (group & 3)) % count_dp) * 4 + ((((group >> 3) & 1) ^ y) * 2 + (((group >> 2) & 1) ^ x))
    )
    order = jnp.concatenate([group_order, c[None]]).astype(jnp.int32)
    shard = jnp.arange(32, dtype=jnp.int32)
    to_whole = (
        (((shard & 1) ^ c) * 16)
        + (((shard >> 2) & 1) ^ y) * 8
        + (((shard >> 1) & 1) ^ x) * 4
        + (d - (shard >> 3)) % count_dp
    )

    slab = jnp.concatenate(
        [w_router]
        + [g[:, None] for g in (g_attn, g_query, g_key, g_ffn)]
        + [jnp.zeros((rows, 128 - experts - 4), low)],
        axis=1,
    )
    expert_ids = jnp.arange(experts, dtype=jnp.int32)
    named = jnp.any(routes[:, :, None] == expert_ids, axis=1)
    names = jnp.zeros((-(-experts // 16) * 16, D), low)
    names = lax.dynamic_update_slice(names, named.astype(low).T, (0, 0))
    sync = lax.optimization_barrier
    width = D + 128
    vo = jnp.concatenate([w_value, w_out], axis=1)
    vo_y = flip(vo, 4)
    qk = ring_gather(jnp.concatenate([w_query, slab, w_key], axis=1))
    q_a, k_b = side_by_side(qk, width)
    q_a, k_b, vo, vo_y, w_down = sync((q_a, k_b, vo, vo_y, w_down))
    vo0 = jnp.concatenate([vo, vo_y], axis=0)
    q_x, k_y, vo1 = flip(q_a, 2), flip(k_b, 4), turn(vo0, 1)
    q_a, k_b = jnp.concatenate([q_a, q_x], axis=0), jnp.concatenate([k_b, k_y], axis=0)
    q_a, k_b, vo1, w_down = sync((q_a, k_b, vo1, w_down))
    q_y, k_x, vo2 = flip(q_a, 4), flip(k_b, 2), turn(vo1, 1)
    vo3 = turn(vo2, 1)
    vo = (vo0, vo1, vo2, vo3)
    v_b, o_b = side_by_side([p[:rows] for p in vo] + [p[rows:] for p in vo], D)
    q_a, k_b = jnp.concatenate([q_a, q_y], axis=0), by_x(k_b, k_x)
    q_a, k_b, v_b, o_b, *down = sync((q_a, k_b, v_b, o_b, *owner_pieces(w_down, place)))
    v_x, q_other, k_other = flip(v_b, 2), flip(q_a, 1), flip(k_b, 1)
    v_b, held_down = by_x(v_b, v_x), jnp.concatenate(to_owner(down))
    v_b, o_b, q_other, k_other, held_down, *gate = sync(
        (v_b, o_b, q_other, k_other, held_down, *owner_pieces(w_gate, place))
    )
    o_x, v_other, down_far = flip(o_b, 2), flip(v_b, 1), flip(held_down, 4)
    gate = to_owner(gate)
    v_other, q_a, q_other, k_b, k_other, v_b = sync((v_other, q_a, q_other, k_b, k_other, v_b))
    value_w = (v_b, v_other)
    slab = jnp.concatenate([q_a[:, D:], q_other[:, D:]], axis=0)
    slab = jnp.take(slab.reshape(32, rows, 128), to_whole, axis=0).reshape(D, 128)
    query_w, key_w = (q_a[:, :D], q_other[:, :D]), (k_b, k_other)
    router_w = slab[:, :experts]
    attn_gain, query_gain, key_gain, ffn_gain = (
        slab[:, experts + i].astype(wide) for i in range(4)
    )
    segment, offset = layout(lengths[0], row_count)
    inputs = tokens.astype(wide)
    normed_f, norm_attn_pull = jax.vjp(normalize, inputs, attn_gain)
    normed_attn = reorder(normed_f.astype(low), order, True)
    half = D // 2

    def times(left, pair):
        return jnp.dot(left[:, :half], pair[0], preferred_element_type=wide) + jnp.dot(
            left[:, half:], pair[1], preferred_element_type=wide
        )

    raw_q = times(normed_attn, query_w)
    raw_k = times(normed_attn, key_w)

    frequency = THETA ** (-jnp.arange(HD // 2, dtype=wide) / (HD // 2))
    angles = offset.astype(wide)[:, None] * frequency[None, :]
    cosine, sine = jnp.cos(angles), jnp.sin(angles)
    turns = (
        jnp.concatenate([cosine, cosine], axis=1),
        jnp.concatenate([-sine, sine], axis=1),
        segment[:, None],
        segment[None, :],
    )
    head_gains = (query_gain[None], key_gain[None])
    values = times(normed_attn, value_w).astype(low)
    raw_q, raw_k, values, o_x, down_far, *gate = sync((raw_q, raw_k, values, o_x, down_far, *gate))
    o_b, held_gate = by_x(o_b, o_x), jnp.concatenate(gate)
    down_own, down_give = to_both(held_down, down_far, place)
    o_b, held_gate, down_give, raw_q, raw_k, values, *up = sync(
        (o_b, held_gate, down_give, raw_q, raw_k, values, *owner_pieces(w_up, place))
    )
    gate_far, up = flip(held_gate, 4), to_owner(up)
    o_other, down_got = flip(o_b, 1), flip(down_give, 1)
    o_other, raw_q, raw_k, values = sync((o_other, raw_q, raw_k, values))
    out_w = (o_b, o_other)
    like = jax.ShapeDtypeStruct((row_count, D), low)
    queries, keys_rot, context = on_chip(
        attend_kernel, [like] * 3, order, raw_q, raw_k, values, *head_gains, *turns
    )
    midway = inputs + times(context, out_w)
    normed2_f, norm_ffn_pull = jax.vjp(normalize, midway, ffn_gain)
    normed_ffn = normed2_f.astype(low)
    normed_ffn, gate_far, down_got, *up = sync((normed_ffn, gate_far, down_got, *up))
    held_up = jnp.concatenate(up)
    down_w = (down_own, down_got)

    def dense_gates(values, named_here):
        logits = jnp.dot(values, router_w, preferred_element_type=wide)
        logits = jnp.where(named_here, logits, -jnp.inf)
        exp_logits = jnp.exp(logits - jnp.max(logits, axis=-1, keepdims=True))
        return exp_logits / jnp.sum(exp_logits, axis=-1, keepdims=True)

    router_wide = jnp.pad(router_w, ((0, 0), (0, 128 - experts)))

    def chunk(piece, piece_x, piece_c, piece_xc):
        return expert_chunk(
            at_owner,
            (piece, piece_x, piece_c, piece_xc),
            row_count,
            gate_w,
            up_w,
            down_w,
            router_wide,
            experts,
        )

    def add(left, right):
        return (left.astype(wide) + right.astype(wide)).astype(low)

    def both_x(own, far):
        return add(own[0], far[0]), add(own[1], far[1])

    sent0 = jnp.concatenate([normed_ffn, cotangent, names], axis=0)
    up_far = flip(held_up, 4)
    gate_own, gate_give = to_both(held_gate, gate_far, place)
    gate_got = flip(gate_give, 1)
    sent1, sent0_x, sent0_c = turn(sent0, 1), flip(sent0, 2), flip(sent0, 1)
    sent1, sent0_x, sent0_c, up_far, gate_got = sync((sent1, sent0_x, sent0_c, up_far, gate_got))
    up_own, up_give = to_both(held_up, up_far, place)
    gate_w, up_w = (gate_own, gate_got), (up_own, flip(up_give, 1))
    sent2, sent1_x, sent1_c = turn(sent1, 1), flip(sent1, 2), flip(sent1, 1)
    outs0 = chunk(sent0, sent0_x, sent0_c, flip(sent0_x, 1))
    sent2, sent1_x, sent1_c, *outs0 = sync((sent2, sent1_x, sent1_c, *outs0))
    sent3, sent2_x, sent2_c = turn(sent2, 1), flip(sent2, 2), flip(sent2, 1)
    outs1 = chunk(sent1, sent1_x, sent1_c, flip(sent1_x, 1))
    sent3, sent2_x, sent2_c, *outs1 = sync((sent3, sent2_x, sent2_c, *outs1))
    sent3_x, sent3_c = flip(sent3, 2), flip(sent3, 1)
    outs2 = chunk(sent2, sent2_x, sent2_c, flip(sent2_x, 1))
    h1_c, m1_c = flip(outs1[6], 1), flip(outs1[8], 1)
    sent3_x, sent3_c, h1_c, m1_c, *outs2 = sync((sent3_x, sent3_c, h1_c, m1_c, *outs2))
    outs3 = chunk(sent3, sent3_x, sent3_c, flip(sent3_x, 1))
    h1, m1 = both_x(outs1[5], h1_c), both_x(outs1[7], m1_c)
    h1_x, m1_x, h2_c, m2_c = flip(h1[1], 2), flip(m1[1], 2), flip(outs2[6], 1), flip(outs2[8], 1)
    h1_x, m1_x, h2_c, m2_c, *outs3 = sync((h1_x, m1_x, h2_c, m2_c, *outs3))
    outs = (outs0, outs1, outs2, outs3)
    arrived, hidden, grad_produced, grad_gate_low, grad_up_low = ([o[i] for o in outs] for i in range(5))
    ring, h2 = add(h1[0], h1_x), both_x(outs2[5], h2_c)
    ring, *h2 = sync((ring, *h2))
    ring, h2_x = turn(ring, 1), flip(h2[1], 2)
    h3_c, h0_c, m3_c = flip(outs3[6], 1), flip(outs0[6], 1), flip(outs3[8], 1)
    h3_c, arrived, grad_gate_low = sync((h3_c, arrived, grad_gate_low))
    gate_sum = contract(arrived, grad_gate_low)
    gate_got = flip(gate_sum[D // 2 :], 1)
    ring, h2_x, h3_c, h0_c, m3_c = sync((ring, h2_x, h3_c, h0_c, m3_c))
    ring, h3 = add(add(h2[0], h2_x), ring), both_x(outs3[5], h3_c)
    ring, *h3 = sync((ring, *h3))
    ring, h3_x, m0_c = turn(ring, 1), flip(h3[1], 2), flip(outs0[8], 1)
    gate_keep, gate_give = from_owner(gate_sum[: D // 2], gate_got, place)
    gate_give, arrived, grad_up_low = sync((gate_give, arrived, grad_up_low))
    gate_far = flip(gate_give, 4)
    up_sum = contract(arrived, grad_up_low)
    up_got = flip(up_sum[D // 2 :], 1)
    m1 = add(m1[0], m1_x)
    ring, h3_x, m0_c, m1 = sync((ring, h3_x, m0_c, m1))
    ring, h0 = add(add(h3[0], h3_x), ring), both_x(outs0[5], h0_c)
    ring, *h0 = sync((ring, *h0))
    ring, h0_x, m_ring = turn(ring, 1), flip(h0[1], 2), turn(m1, 1)
    up_got, hidden, grad_produced = sync((up_got, hidden, grad_produced))
    down_sum = contract(hidden, grad_produced)
    up_keep, up_give = from_owner(up_sum[: D // 2], up_got, place)
    ms = [both_x(o[7], t) for o, t in ((outs2, m2_c), (outs3, m3_c), (outs0, m0_c))]
    m_far = jnp.concatenate([t[1] for t in ms], axis=0)
    ring, h0_x, m_ring, down_sum, up_keep, up_give, gate_far, m_far = sync(
        (ring, h0_x, m_ring, down_sum, up_keep, up_give, gate_far, m_far)
    )
    def two(value):
        n = value.shape[0] // 2
        return value[:n], value[n:]

    def halves_sum(left, right):
        return [add(a, b) for a, b in zip(two(left), two(right))]

    down_mine, down_other = two(down_sum)
    ring, h0_x, m_far, up_give, down_mine, down_other, *gate_parts = sync(
        (ring, h0_x, m_far, up_give, down_mine, down_other, *halves_sum(gate_keep, gate_far))
    )
    down_got = flip(down_other, 1)
    gate_back, up_far, m_x = to_shards(gate_parts), flip(up_give, 4), flip(m_far, 2)
    down_got, ring, h0_x = sync((down_got, ring, h0_x))
    back = h0[0].astype(wide) + h0_x.astype(wide) + ring.astype(wide)
    grad_normed_ffn = back[:row_count]
    grad_gates = back[row_count : row_count + experts]
    grad_gates = (grad_gates[:, :row_count] + grad_gates[:, 2 * row_count : 3 * row_count]).T

    grad_out = cotangent.astype(wide)
    gates = dense_gates(normed_ffn, named)
    grad_chosen = gates * (grad_gates - jnp.sum(gates * grad_gates, axis=1, keepdims=True))
    grad_logits = grad_chosen.astype(low)
    grad_router_local = contract_rows(grad_logits, normed_ffn)
    grad_normed_ffn = grad_normed_ffn + times_transposed(grad_logits, router_w)
    grad_midway_norm, grad_ffn_gain = norm_ffn_pull(grad_normed_ffn)
    grad_midway = grad_out + grad_midway_norm
    grad_attn = grad_midway.astype(low)

    def times_back(left, pair):
        return jnp.concatenate(
            [times_transposed(left, pair[0]), times_transposed(left, pair[1])], axis=1
        )

    out_core = flip(contract([context[:, half:]], [grad_attn]), 1)
    grad_context = times_back(grad_attn, out_w).astype(low)
    grad_heads, grad_query_gain, grad_key_gain = on_chip(
        attend_back_kernel,
        [jax.ShapeDtypeStruct((row_count, 3 * D), low)] + [jax.ShapeDtypeStruct((1, D), wide)] * 2,
        order,
        grad_context,
        queries,
        keys_rot,
        values,
        raw_q,
        raw_k,
        *head_gains,
        *turns,
    )
    heads_other = contract([normed_attn[:, half:]], [grad_heads])
    down_keep, down_give = from_owner(down_mine, down_got, place)
    out_own, out_far = add_contract(context[:, :half], grad_attn, out_core, ("x",))
    m_x, up_far, down_keep, down_give, out_own, out_far, heads_other, *gate_back = sync(
        (m_x, up_far, down_keep, down_give, out_own, out_far, heads_other, *gate_back)
    )
    grad_gate = two_experts(gate_back, place)
    m2, m3, m0 = (
        add(t[0], m_x[k * row_count : (k + 1) * row_count]) for k, t in enumerate(ms)
    )

    def fold(value, bit):
        n = value.shape[1] // 2
        return value[:, :n] + flip(value[:, n:], bit)

    out_far, down_give, heads_other, *up_parts = sync(
        (out_far, down_give, heads_other, *halves_sum(up_keep, up_far))
    )
    up_back, down_far = to_shards(up_parts), flip(down_give, 4)
    out_far, heads_core = flip(out_far, 2), flip(heads_other, 1)
    heads_core, grad_heads = sync((heads_core, grad_heads))
    query_own, query_far, key_own, key_far, value_own, value_far = add_contract(
        normed_attn[:, :half], grad_heads, heads_core, ("y", "x", "x")
    )
    grad_normed_attn = sum(
        times_back(grad_heads[:, k * D : (k + 1) * D], w)
        for k, w in enumerate((query_w, key_w, value_w))
    )
    grad_normed_attn = reorder(grad_normed_attn, order, False)
    grad_inputs_norm, grad_attn_gain = norm_attn_pull(grad_normed_attn)
    grad_tokens = (grad_midway + grad_inputs_norm).astype(low)
    small = jnp.concatenate(
        [grad_router_local, grad_attn_gain[None], grad_query_gain, grad_key_gain, grad_ffn_gain[None]]
        + [jnp.zeros((-(experts + 4) % 8, D), wide)],
        axis=0,
    )
    small = reorder(small, order, True)
    down_far, out_far, small, *parts = sync(
        (down_far, out_far, small, query_own, query_far, key_own, key_far, value_own, value_far, *up_back)
    )
    query_own, query_far, key_own, key_far, value_own, value_far, *up_back = parts
    grad_up = two_experts(up_back, place)
    out_own, out_far = halves_sum(out_own, out_far)
    query_far, key_far, value_far, out_own, out_far, *down_parts = sync(
        (query_far, key_far, value_far, out_own, out_far, *halves_sum(down_keep, down_far))
    )
    query_far, key_far, down_back = flip(query_far, 4), flip(key_far, 2), to_shards(down_parts)
    small = fold(small, 1)
    query_far, key_far, small, m_ring, *down_back = sync(
        (query_far, key_far, small, m_ring, *down_back)
    )
    grad_down = two_experts(down_back, place)

    key_own, key_far = halves_sum(key_own, key_far)
    query_own, query_far = halves_sum(query_own, query_far)
    ring, key_far, out_far, value_far, query_far = sync(
        (add(m2, m_ring), key_far, out_far, value_far, query_far)
    )
    ring, key_far, out_far, value_far = (
        turn(ring, 1), flip(key_far, 4), flip(out_far, 4), flip(value_far, 2)
    )
    ring = turn(add(m3, ring), 1)
    small = fold(small, 4)
    ring, key_far, out_far, value_far, small = sync((ring, key_far, out_far, value_far, small))
    block_out = (midway + m0.astype(wide) + ring.astype(wide)).astype(low)
    value_own, value_far = halves_sum(value_own, value_far)

    def by_steps(both):
        return [both[i * rows : (i + 1) * rows] for i in range(count_dp)]

    ko = by_steps(jnp.concatenate([add(key_own, key_far), add(out_own, out_far)], axis=1))
    value_far, *ko = sync((value_far, *ko))
    ko_ring, query_far, value_far = turn(ko[3], -1), flip(query_far, 2), flip(value_far, 4)
    ko_ring = turn(add(ko[2], ko_ring), -1)
    small = fold(small, 2)
    query_far, value_far, small, ko_ring = sync((query_far, value_far, small, ko_ring))
    n = small.shape[0]
    small = small.reshape(n, count_dp, rows).transpose(1, 2, 0).reshape(count_dp * rows, n)
    small = jnp.pad(small.astype(low), ((0, 0), (0, 128 - n)))
    qv = by_steps(
        jnp.concatenate([add(query_own, query_far), add(value_own, value_far), small], axis=1)
    )
    ko_ring, qv_ring = turn(add(ko[1], ko_ring), -1), turn(qv[3], -1)
    ko_ring, qv_ring = sync((ko_ring, qv_ring))
    ko_ring = ko_ring.astype(wide) + ko[0].astype(wide)
    qv_ring = turn(add(qv[2], qv_ring), -1)
    qv_ring = turn(add(qv[1], qv_ring), -1).astype(wide) + qv[0].astype(wide)
    grad_key, grad_outproj = ko_ring[:, :D], ko_ring[:, D:]
    grad_query, grad_value = qv_ring[:, :D], qv_ring[:, D : 2 * D]
    small = qv_ring[:, 2 * D :]
    return (
        block_out,
        grad_tokens,
        grad_query,
        grad_key,
        grad_value,
        grad_outproj,
        small[:, :experts],
        grad_gate,
        grad_up,
        grad_down,
        small[:, experts],
        small[:, experts + 1],
        small[:, experts + 2],
        small[:, experts + 3],
    )


def solution(mesh):
    in_specs = (
        P(("dp", "expert"), None),
        P(("dp", "expert"), None),
        P(("dp", "expert"), None),
        P(("dp", "expert"), None),
        P(("dp", "expert"), None),
        P(("dp", "expert"), None),
        P(("dp", "expert"), None),
        P(("dp", "expert"), None),
        P(("dp", "expert"), None),
        P("expert", "dp", None),
        P("expert", "dp", None),
        P("expert", "dp", None),
        P(("dp", "expert")),
        P(("dp", "expert")),
        P(("dp", "expert")),
        P(("dp", "expert")),
    )
    out_specs = (
        P(("dp", "expert"), None),
        P(("dp", "expert"), None),
        P(("dp", "expert"), None),
        P(("dp", "expert"), None),
        P(("dp", "expert"), None),
        P(("dp", "expert"), None),
        P(("dp", "expert"), None),
        P("expert", "dp", None),
        P("expert", "dp", None),
        P("expert", "dp", None),
        P(("dp", "expert")),
        P(("dp", "expert")),
        P(("dp", "expert")),
        P(("dp", "expert")),
    )
    local = by_links if (mesh.shape["dp"], mesh.shape["expert"]) == (4, 8) else by_axes
    return jax.shard_map(local, mesh=mesh, in_specs=in_specs, out_specs=out_specs, check_vma=False)
```
